32 devices in a mesh: seg: 2 (over x), rad: 4 (over y, core), ax: 4 (over z).
Axes of the slice: x: 2, y: 2, z: 4, core: 2. Of those that a mesh axis runs over, the one named last changes fastest.
Arguments:
- start_states: float32 [4, 3, 16, 192, 384], P('seg', None, 'ax', 'rad'), may hold values from -4.2 to 4.2
- radial_inverse: float32 [192, 192, 192], P('ax'), may hold values from 0 to 1.2, as said below
- offsets: int32 [4], P('seg'), may hold values from 0 to 15
- mode_count: int32 [1], replicated, may hold values from 128 to 192
Outputs:
- residual: float32 [4, 3, 16, 192, 384], P('seg', None, 'ax', 'rad')
The draws below stay inside these ranges and needn't reach their ends.
Inputs may be any that keep to these rules, and one draw needn't show every extreme that they name: `radial_inverse`: for each mode, a dense matrix with positive entries.
All inputs are finite; a program needn't handle non-finite values.
Results may differ from the reference program's by a relative error of at most 0.0001.
Values sent between devices are 32-bit elements; how exact they have to be, the bound alone decides.
No kernel may reach another device: no remote copies, remote signals or barrier semaphores. Data moves between devices by JAX's collectives and lax.ppermute only.
A program may use at most 128 MiB of HBM per device.

```python
import math
import jax
import jax.numpy as jnp
from jax import lax

R = 192
NM = 192
NTH = 384
NZ = 16
SEGS = 4
STEPS = 2


def draw_radial_inverse(key, part):
    length_key, factor_key = jax.random.split(key)
    lengths = jnp.exp(jax.random.uniform(length_key, (NM, 1, 1), jnp.float32, math.log(70.0), math.log(400.0)))
    factors = jax.random.uniform(factor_key, (NM, R, R), jnp.float32, 0.5, 1.5)
    positions = jnp.arange(R).astype(jnp.float32)
    distance = jnp.abs(positions[:, None] - positions[None, :])
    return jnp.eye(R, dtype=jnp.float32)[None] + 0.1 * jnp.exp(-distance[None] / lengths) * factors


def with_ends(values, stream_key, low, top_value):
    spot = [jax.random.randint(jax.random.fold_in(stream_key, axis), (), 0, length) for axis, length in enumerate(values.shape)]
    longest = values.shape.index(max(values.shape))
    next_to = spot[:longest] + [(spot[longest] + 1) % values.shape[longest]] + spot[longest + 1:]
    return values.at[tuple(spot)].set(low).at[tuple(next_to)].set(top_value)


def block_levels(rng, extent, cuts, smallest, high):
    gain, own = 1.0, jax.random.fold_in(rng, 6)
    for dim, parts in cuts:
        draws = jnp.exp(jax.random.uniform(jax.random.fold_in(own, dim), (parts,), jnp.float32, smallest / len(cuts), high / len(cuts)))
        gain = gain * jnp.repeat(draws, extent[dim] // parts).reshape([-1 if axis == dim else 1 for axis in range(len(extent))])
    return gain


def normal_values(key, dims, spread, bound, shards=(), kind=jnp.bfloat16):
    gain = block_levels(key, dims, shards, -0.22, 0.18) if shards else 1.0
    array = jax.random.normal(key, dims, jnp.float32) * spread * gain
    return jnp.minimum(jnp.maximum(array, -bound), bound).astype(kind)


def setup_inputs(seed: int = 0) -> dict:
    arg_keys = jax.random.split(jax.random.key(seed), 5)
    return {
        "start_states": normal_values(arg_keys[0], (SEGS, 3, NZ, R, NTH), 0.7, 4.2, ((0, 2), (2, 4), (3, 4)), jnp.float32),
        "radial_inverse": draw_radial_inverse(jax.random.fold_in(arg_keys[4], 71), 0),
        "offsets": with_ends(jax.random.randint(arg_keys[2], (SEGS,), 0, NZ), jax.random.fold_in(arg_keys[2], 1), 0, NZ - 1).astype(jnp.int32),
        "mode_count": jax.random.randint(arg_keys[3], (1,), NM * 2 // 3, NM + 1).astype(jnp.int32),
    }


def synthesize(coefficients):
    cosine_part = coefficients[..., 0::2]
    sine_part = coefficients[..., 1::2]
    spectrum = (cosine_part - 1j * sine_part) * (NTH / 2.0)
    spectrum = spectrum.at[..., 0].set(cosine_part[..., 0] * NTH)
    spectrum = jnp.concatenate([spectrum, jnp.zeros_like(spectrum[..., :1])], axis=-1)
    return jnp.fft.irfft(spectrum, n=NTH, axis=-1) / math.sqrt(NM)

def analyze(field, kept_modes):
    spectrum = jnp.fft.rfft(field, axis=-1)[..., :NM]
    mode_index = jnp.arange(NM)
    scale = math.sqrt(NM) / NTH
    cosine_part = jnp.real(spectrum) * jnp.where(mode_index == 0, 1.0, 2.0) * scale
    sine_part = -jnp.imag(spectrum) * (2.0 * scale)
    stacked = jnp.stack([cosine_part, sine_part], axis=-1)
    stacked = jnp.where((mode_index < kept_modes)[:, None], stacked, 0.0)
    return stacked.reshape(field.shape)

def advance(current, radial_inverse, kept_modes, profile):
    physical = synthesize(current)
    gradient = (jnp.roll(physical, -1, axis=1) - jnp.roll(physical, 1, axis=1)) * 20.0
    forcing = physical - 0.02 * (profile + physical[2:3]) * gradient
    spectral = analyze(forcing, kept_modes).reshape(3, NZ, R, NM, 2)
    solved = jnp.einsum('mrs,czsmk->czrmk', radial_inverse, spectral, precision=lax.Precision.HIGHEST)
    return solved.reshape(3, NZ, R, NTH)

def reference(start_states, radial_inverse, offsets, mode_count):
    radius = (jnp.arange(R).astype(jnp.float32) + 0.5) / R
    profile = (1.0 - radius * radius).reshape(1, 1, R, 1)
    results = []
    for segment in range(SEGS):
        current = start_states[segment]
        for step_index in range(STEPS):
            current = advance(current, radial_inverse, mode_count[0], profile)
        rolled = jnp.roll(current, offsets[segment], axis=1)
        results.append(rolled - start_states[(segment + 1) % SEGS])
    return jnp.stack(results, axis=0)
```

```python
import functools
import math

import jax
import jax.numpy as jnp
import ml_dtypes
import numpy as np
from jax import lax
from jax.experimental import pallas as pl
from jax.experimental.pallas import tpu as pltpu
from jax.sharding import PartitionSpec as P

STEPS = 2
MESH_AXES = ("seg", "rad", "ax")
VMEM_LIMIT = 48 * 1024 * 1024

highest = lax.Precision.HIGHEST


def passed_along(value, axis, steps):
    count = lax.axis_size(axis)
    pairs = [(source, (source + steps) % count) for source in range(count)]
    return lax.ppermute(value, axis, pairs)


def padded_2(array, sides, width):
    for axis, dim in sides:
        peers, length = (lax.axis_size(axis), array.shape[dim])
        up = [(i, (i + 1) % peers) for i in range(peers)]
        down = [(j, i) for i, j in up]
        last = lax.slice_in_dim(array, length - width, length, axis=dim)
        leading = lax.slice_in_dim(array, 0, width, axis=dim)
        before = lax.ppermute(last, axis, up)
        after = lax.ppermute(leading, axis, down)
        array = jnp.concatenate([before, array, after], axis=dim)
    return array


def fourier_tables(columns, kept_modes):
    modes_total = columns // 2
    row_index = lax.broadcasted_iota(jnp.int32, (columns, columns), 0)
    point_index = lax.broadcasted_iota(jnp.int32, (columns, columns), 1)
    mode_index = row_index // 2
    phase = (mode_index * point_index % columns).astype(jnp.float32) * (2.0 * math.pi / columns)
    even_rows = row_index % 2 == 0
    cosine = jnp.cos(phase)
    sine = jnp.sin(phase)
    root = math.sqrt(modes_total)
    synthesis = jnp.where(even_rows, cosine, sine) / root
    weights = jnp.where(mode_index == 0, 1.0, 2.0)
    analysis = jnp.where(even_rows, weights * cosine, 2.0 * sine) * (root / columns)
    analysis = jnp.where(mode_index < kept_modes, analysis, 0.0)
    return (synthesis, analysis)


def radial_solve(pencils, radial_inverse, radial_rows):
    local_modes = radial_inverse.shape[0]
    local_columns, members, axial_cells, ignored = pencils.shape
    own_rows = lax.dynamic_slice_in_dim(
        radial_inverse, lax.axis_index("rad") * radial_rows, radial_rows, 1
    )
    piece = lax.all_gather(pencils, "rad", axis=3, tiled=True)
    piece_rows = piece.shape[3]
    grouped = piece.reshape(local_modes, 2, members, axial_cells, piece_rows)
    product = jnp.einsum("mrs,mkqzs->mkqzr", own_rows, grouped, precision=highest)
    return product.reshape(local_columns, members, axial_cells, radial_rows)


def general_body(start_states, radial_inverse, offsets, mode_count):
    groups, components, axial_rows, radial_rows, columns = start_states.shape
    synthesis, analysis = fourier_tables(columns, mode_count[0])
    radius = (
        (lax.axis_index("rad") * radial_rows + jnp.arange(radial_rows)).astype(jnp.float32) + 0.5
    ) / (radial_rows * lax.axis_size("rad"))
    profile = (1.0 - radius * radius).reshape(1, 1, 1, radial_rows, 1)
    following = passed_along(start_states[0], "seg", -1)
    current = start_states
    for step_index in range(STEPS):
        if step_index == 0:
            physical = jnp.einsum("gczrj,jp->gczrp", current, synthesis, precision=highest)
        else:
            physical = jnp.einsum("jgczr,jp->gczrp", current, synthesis, precision=highest)
        padded = padded_2(physical, (("ax", 2),), 1)
        gradient = (padded[:, :, 2:] - padded[:, :, :-2]) * 20.0
        advecting = profile + padded[:, 2:3, 1:-1]
        forcing = physical - 0.02 * advecting * gradient
        spectral = jnp.einsum("gczrp,jp->jgczr", forcing, analysis, precision=highest)
        pencils = lax.all_to_all(spectral, "ax", split_axis=0, concat_axis=3, tiled=True)
        local_columns = pencils.shape[0]
        axial_cells = pencils.shape[3]
        pencils = pencils.reshape(local_columns, groups * components, axial_cells, radial_rows)
        solved = radial_solve(pencils, radial_inverse, radial_rows)
        if step_index == STEPS - 1:
            blocks = solved.reshape(local_columns, groups, components, axial_cells, radial_rows)
            shifted = [
                jnp.roll(blocks[:, member], offsets[member], axis=2) for member in range(groups)
            ]
            solved = jnp.stack(shifted, axis=1).reshape(
                local_columns, groups * components, axial_cells, radial_rows
            )
        returned = lax.all_to_all(solved, "ax", split_axis=2, concat_axis=0, tiled=True)
        current = returned.reshape(columns, groups, components, axial_rows, radial_rows)
    ending = jnp.transpose(current, (1, 2, 3, 4, 0))
    upcoming = jnp.concatenate([start_states[1:], following[None]], axis=0)
    return ending - upcoming


def halves(high):
    top = high.astype(jnp.bfloat16)
    return top, (high - top.astype(jnp.float32)).astype(jnp.bfloat16)


def product(left, right, contract):
    return lax.dot_general(
        left, right, ((contract[:1], contract[1:]), ((), ())), preferred_element_type=jnp.float32
    )


def stacked_table(table):
    top = table.astype(ml_dtypes.bfloat16)
    rest = (table - top.astype(np.float64)).astype(ml_dtypes.bfloat16)
    return np.concatenate([top, top, rest], axis=1)


def column_order(columns, quarter_modes, shares):
    each = quarter_modes // shares
    order = []
    for share in range(shares):
        for low in range(2):
            for high in range(2):
                first = (2 * high + low) * quarter_modes + share * each
                order.extend(range(2 * first, 2 * (first + each)))
    assert sorted(order) == list(range(columns))
    return np.array(order)


def tables(columns, order):
    modes_total = columns // 2
    rows = np.arange(columns)
    mode = rows // 2
    phase = (mode[:, None] * np.arange(columns)[None, :]) % columns * (2.0 * np.pi / columns)
    even = (rows % 2 == 0)[:, None]
    root = math.sqrt(modes_total)
    synthesis = np.where(even, np.cos(phase), np.sin(phase)) / root
    weights = np.where(mode == 0, 1.0, 2.0)[:, None]
    analysis = np.where(even, weights * np.cos(phase), 2.0 * np.sin(phase)) * (root / columns)
    return (
        stacked_table(np.ascontiguousarray(synthesis.T)),
        stacked_table(np.ascontiguousarray(synthesis.T[:, order])),
        stacked_table(analysis[order]),
        mode[order].astype(np.int32),
    )


def lane_index():
    return lax.broadcasted_iota(jnp.int32, (1, 128), 1)


def physical_to_spectral(physical, profile, analysis):
    lane = lane_index()
    z = lane % 16
    forcing = []
    for tile in range(3):
        field = physical[tile]
        above = jnp.where(z == 15, pltpu.roll(field, 15, 1), pltpu.roll(field, 127, 1))
        below = jnp.where(z == 0, pltpu.roll(field, 113, 1), pltpu.roll(field, 1, 1))
        speed = jnp.where(lane < 32, pltpu.roll(field, 64, 1), pltpu.roll(field, 96, 1))
        speed = jnp.where(lane < 64, speed, field)
        speed = jnp.where(lane < 96, speed, physical[2])
        forcing.append(field - 0.4 * (profile[tile : tile + 1] + speed) * (above - below))
    forcing = jnp.concatenate(forcing, axis=1)
    top, rest = halves(forcing)
    return product(analysis, jnp.concatenate([top, rest, top], axis=0), (1, 0))


def write_spectral(spectral, out_ref):
    members, tiles, width, ignored = out_ref.shape
    for tile in range(tiles):
        block = spectral[:, tile * 128 : (tile + 1) * 128]
        out_ref[:, tile] = block.reshape(members, width, 128)


def first_phase_a(rows_ref, synthesis_ref, analysis_ref, profile_ref, out_ref):
    parts = []
    for tile in range(3):
        parts.append(rows_ref[tile])
        parts.append(rows_ref[3, tile * 32 : (tile + 1) * 32])
    top, rest = halves(jnp.concatenate(parts, axis=0))
    physical = product(synthesis_ref[...], jnp.concatenate([top, rest, top], axis=1), (1, 1))
    physical = [physical[:, tile * 128 : (tile + 1) * 128] for tile in range(3)]
    write_spectral(physical_to_spectral(physical, profile_ref[0], analysis_ref[...]), out_ref)


def later_phase_a(wire_ref, synthesis_ref, analysis_ref, profile_ref, out_ref):
    members, tiles, width, ignored = wire_ref.shape
    state = jnp.concatenate(
        [wire_ref[:, tile].reshape(members * width, 128) for tile in range(tiles)], axis=1
    )
    top, rest = halves(state)
    physical = product(synthesis_ref[...], jnp.concatenate([top, rest, top], axis=0), (1, 0))
    physical = [physical[:, tile * 128 : (tile + 1) * 128] for tile in range(3)]
    write_spectral(physical_to_spectral(physical, profile_ref[0], analysis_ref[...]), out_ref)


def unpack_radii(wire_ref, held_ref, places):
    members, tiles, width, ignored = wire_ref.shape
    lane = lane_index()
    for member in range(members):
        for group in range(tiles // 3):
            waves = [wire_ref[member, 3 * group + tile] for tile in range(3)]
            fourth = jnp.where(lane < 32, pltpu.roll(waves[0], 32, 1), pltpu.roll(waves[1], 64, 1))
            fourth = jnp.where(lane < 64, fourth, pltpu.roll(waves[2], 96, 1))
            base = (places[member] + 4 * group) * width
            for index, block in enumerate(waves + [fourth]):
                held_ref[base + index * width : base + (index + 1) * width, :] = block


def solved_modes(half_ref, own_ref, other_ref, held_ref, transposed, store):
    each, radii, ignored = own_ref.shape
    width = 4 * each
    first_half = half_ref[0] == 0
    for mode in range(2 * each):
        index = mode % each
        here, there = own_ref[index], other_ref[index]
        if mode < each:
            matrix = jnp.where(first_half, here, there)
        else:
            matrix = jnp.where(first_half, there, here)
        state = jnp.concatenate(
            [held_ref[pl.ds(2 * mode + part, radii, stride=width), :] for part in range(2)], axis=1
        )
        matrix_top, matrix_rest = halves(matrix)
        if transposed:
            top, rest = halves(state.T)
            solved = product(top, matrix_top, (1, 1))
            solved += product(rest, matrix_top, (1, 1)) + product(top, matrix_rest, (1, 1))
        else:
            top, rest = halves(state)
            solved = product(matrix_top, top, (1, 0))
            solved += product(matrix_top, rest, (1, 0)) + product(matrix_rest, top, (1, 0))
        store(mode, solved)


def phase_b(places, half_ref, own_ref, other_ref, wire_ref, out_ref, held_ref, solved_ref):
    members, tiles, width, ignored = wire_ref.shape
    radii = own_ref.shape[1]
    unpack_radii(wire_ref, held_ref, places)

    def store(mode, solved):
        for part in range(2):
            solved_ref[pl.ds(2 * mode + part, radii, stride=width), :] = solved[
                :, part * 128 : (part + 1) * 128
            ]

    solved_modes(half_ref, own_ref, other_ref, held_ref, False, store)
    lane = lane_index()
    for member in range(members):
        for group in range(tiles // 3):
            base = (places[member] + 4 * group) * width
            blocks = [solved_ref[base + i * width : base + (i + 1) * width, :] for i in range(4)]
            for tile in range(3):
                fourth = pltpu.roll(blocks[3], 96 - 32 * tile, 1)
                out_ref[member, 3 * group + tile] = jnp.where(lane < 96, blocks[tile], fourth)


def last_phase_b(
    places, peers, half_ref, offset_ref, own_ref, other_ref, wire_ref, out_ref, held_ref, solved_ref
):
    members, tiles, width, ignored = wire_ref.shape
    radii = own_ref.shape[1]
    seg_places, rad_places, ax_places = peers
    planes = 16 // ax_places
    each = radii // rad_places
    unpack_radii(wire_ref, held_ref, places)

    def store(mode, solved):
        for part in range(2):
            rows = pl.ds(2 * mode + part, 96, stride=width)
            block = solved[part * 128 : part * 128 + 96]
            solved_ref[0, rows, :] = block[:, :128]
            solved_ref[1, rows, 0 : radii - 128] = block[:, 128:]

    solved_modes(half_ref, own_ref, other_ref, held_ref, True, store)
    lane = lane_index()

    def radial_piece(low, high, rad, at):
        first = rad * each
        if first + each <= 128:
            return pltpu.roll(low, (at - first) % 128, 1)
        if first >= 128:
            return pltpu.roll(high, (at - first) % 128, 1)
        return pltpu.roll(jnp.where(lane >= first, low, high), (at - first) % 128, 1)

    for seg in range(seg_places):
        for ax in range(ax_places):
            blocks = {}
            for component in range(3):
                for plane in range(planes):
                    source = lax.rem(ax * planes + plane - offset_ref[seg] + 16, 16)
                    row = ((component * seg_places + seg) * 16 + source) * width
                    row = pl.multiple_of(row, 8)
                    blocks[component, plane] = (
                        solved_ref[0, pl.ds(row, width), :],
                        solved_ref[1, pl.ds(row, width), :],
                    )
            for rad in range(rad_places):
                pairs = []
                for component in range(3):
                    for pair in range(planes // 2):
                        left = radial_piece(*blocks[component, 2 * pair], rad, 0)
                        right = radial_piece(*blocks[component, 2 * pair + 1], rad, each)
                        pairs.append(jnp.where(lane < each, left, right))
                split = [
                    block[8 * part : 8 * part + 8] for part in range(width // 8) for block in pairs
                ]
                target = (seg * rad_places + rad) * ax_places + ax
                for group in range(len(split) // 4):
                    for tile in range(3):
                        fourth = pltpu.roll(split[4 * group + 3], 96 - 32 * tile, 1)
                        out_ref[target, 3 * group + tile] = jnp.where(
                            lane < 96, split[4 * group + tile], fourth
                        )
                whole = len(split) // 4
                for index in range(4 * whole, len(split)):
                    out_ref[target, 3 * whole + index - 4 * whole] = split[index]


def residual_end(peers, wire_ref, start_ref, following_ref, out_ref, held_ref):
    seg_places, rad_places, ax_places = peers
    groups, components, planes, each, columns = out_ref.shape
    lane = lane_index()
    shares = seg_places * rad_places
    width = columns // (2 * shares)
    chunk = width // 2
    count = (width // 8) * components * (planes // 2)
    for half in range(2):
        for share in range(shares):
            for low in range(2):
                source = share * ax_places + 2 * half + low
                split = []
                for group in range(count // 4):
                    waves = [wire_ref[source, 3 * group + tile] for tile in range(3)]
                    fourth = jnp.where(
                        lane < 32, pltpu.roll(waves[0], 32, 1), pltpu.roll(waves[1], 64, 1)
                    )
                    split += waves + [jnp.where(lane < 64, fourth, pltpu.roll(waves[2], 96, 1))]
                for index in range(count % 4):
                    split.append(wire_ref[source, 3 * (count // 4) + index])
                per_part = components * (planes // 2)
                for slot in range(per_part):
                    rows = jnp.concatenate(
                        [split[part * per_part + slot] for part in range(width // 8)], axis=0
                    )
                    for high in range(2):
                        at = (2 * high + low) * (columns // 4) + share * chunk
                        held_ref[slot, at : at + chunk, :] = rows[high * chunk : (high + 1) * chunk]
        for component in range(components):
            for pair in range(planes // 2):
                ending = held_ref[component * (planes // 2) + pair].T
                for side in range(2):
                    plane = 2 * pair + side
                    if half + 1 < groups:
                        upcoming = start_ref[half + 1, component, plane]
                    else:
                        upcoming = following_ref[component, plane]
                    out_ref[half, component, plane] = (
                        ending[side * each : (side + 1) * each] - upcoming
                    )


def whole_blocks(count):
    return [pl.BlockSpec(memory_space=pltpu.VMEM)] * count


def fits(shape, peers):
    groups, components, axial_rows, radial_rows, columns = shape
    seg_places, rad_places, ax_places = peers
    members = seg_places * rad_places * 2
    return (
        (groups, components, seg_places, ax_places) == (2, 3, 2, 4)
        and axial_rows * ax_places == 16
        and radial_rows == 48
        and rad_places * radial_rows == 192
        and columns == 384
        and members == 16
    )


def half_body(peers, start_states, radial_inverse, offsets, mode_count):
    groups, components, axial_rows, radial_rows, columns = start_states.shape
    seg_places, rad_places, ax_places = peers
    axial = axial_rows * ax_places
    radii = radial_rows * rad_places
    shares = seg_places * rad_places
    members = 2 * shares
    own_radii = radii // members
    own_modes = radial_inverse.shape[0] // shares
    width = columns // members
    tiles = own_radii * 3 // 4
    order = column_order(columns, radial_inverse.shape[0], shares)
    synthesis_natural, synthesis, analysis, mode_of_row = tables(columns, order)

    seg, rad, ax = (lax.axis_index(name) for name in MESH_AXES)
    half, low = ax // 2, ax % 2

    def device(s, r, a):
        return (s * rad_places + r) * ax_places + a

    half_groups = [
        [
            device(s, r, 2 * h + l)
            for s in range(seg_places)
            for r in range(rad_places)
            for l in range(2)
        ]
        for h in range(2)
    ]
    mirror = [(a, (a + 2) % 4) for a in range(4)]
    places = [
        r * radial_rows + (s * 2 + l) * own_radii
        for s in range(seg_places)
        for r in range(rad_places)
        for l in range(2)
    ]

    split = start_states.reshape(
        groups, components, axial_rows, seg_places, 2, own_radii, columns
    )
    split = jnp.transpose(split, (3, 0, 4, 5, 1, 2, 6))
    split = split.reshape(seg_places * ax_places, own_radii * components * axial_rows, columns)
    arrived = lax.all_to_all(split, ("seg", "ax"), 0, 0, tiled=True)
    arrived = arrived.reshape(
        seg_places, ax_places, own_radii, components, axial_rows, columns
    )
    rows = jnp.transpose(arrived, (2, 3, 0, 1, 4, 5))
    rows = rows.reshape(own_radii, components * seg_places * axial, columns)

    share = seg * rad_places + rad
    own_inverse = lax.dynamic_slice_in_dim(radial_inverse, share * own_modes, own_modes, 0)
    other_inverse = lax.ppermute(own_inverse, "ax", mirror)
    following = passed_along(start_states[0], "seg", -1)
    swapped = passed_along(offsets, "seg", 1)
    low_offsets = jnp.where(seg == 0, offsets, swapped)
    high_offsets = jnp.where(seg == 0, swapped, offsets)
    half_offsets = jnp.stack([low_offsets[half], high_offsets[half]])
    half_index = half.reshape(1).astype(jnp.int32)

    kept = (jnp.asarray(mode_of_row) < mode_count[0])[:, None]
    analysis = jnp.where(kept, jnp.asarray(analysis), jnp.zeros((), jnp.bfloat16))
    synthesis_natural = jnp.asarray(synthesis_natural)
    synthesis = jnp.asarray(synthesis)
    first = rad * radial_rows + (seg * 2 + low) * own_radii
    tile_index = np.arange(tiles)[:, None]
    lane = np.arange(128)[None, :]
    local = 4 * (tile_index // 3) + np.where(lane < 96, tile_index % 3, 3)
    radius = ((first + jnp.asarray(local)).astype(jnp.float32) + 0.5) / radii
    profile = (1.0 - radius * radius).reshape(tiles // 3, 3, 128)

    params = pltpu.CompilerParams(vmem_limit_bytes=VMEM_LIMIT)
    wire = jax.ShapeDtypeStruct((members, tiles, width, 128), jnp.float32)
    wire_spec = pl.BlockSpec((members, 3, width, 128), lambda g: (0, g, 0, 0))
    table_spec = pl.BlockSpec((columns, 3 * columns), lambda g: (0, 0))
    profile_spec = pl.BlockSpec((1, 3, 128), lambda g: (g, 0, 0))
    held = pltpu.VMEM((radii * width, 128), jnp.float32)

    def exchanged(value):
        return lax.all_to_all(
            value, MESH_AXES, 0, 0, axis_index_groups=half_groups, tiled=True
        )

    with jax.named_scope("phase_a_first"):
        spectral = pl.pallas_call(
            first_phase_a,
            grid=(tiles // 3,),
            in_specs=[
                pl.BlockSpec((4,) + rows.shape[1:], lambda g: (g, 0, 0)),
                table_spec,
                table_spec,
                profile_spec,
            ],
            out_specs=wire_spec,
            out_shape=wire,
            compiler_params=params,
        )(rows, synthesis_natural, analysis, profile)
    lines = exchanged(spectral)
    with jax.named_scope("phase_b_first"):
        solved = pl.pallas_call(
            functools.partial(phase_b, places),
            in_specs=[pl.BlockSpec(memory_space=pltpu.SMEM)] + whole_blocks(3),
            out_specs=pl.BlockSpec(memory_space=pltpu.VMEM),
            out_shape=wire,
            scratch_shapes=[held, held],
            compiler_params=params,
        )(half_index, own_inverse, other_inverse, lines)
    state = exchanged(solved)
    with jax.named_scope("phase_a_later"):
        spectral = pl.pallas_call(
            later_phase_a,
            grid=(tiles // 3,),
            in_specs=[wire_spec, table_spec, table_spec, profile_spec],
            out_specs=wire_spec,
            out_shape=wire,
            compiler_params=params,
        )(state, synthesis, analysis, profile)
    lines = exchanged(spectral)
    count = (width // 8) * components * (axial_rows // 2)
    end_tiles = (count // 4) * 3 + count % 4
    everyone = seg_places * rad_places * ax_places
    with jax.named_scope("phase_b_last"):
        ending = pl.pallas_call(
            functools.partial(last_phase_b, places, peers),
            in_specs=[pl.BlockSpec(memory_space=pltpu.SMEM)] * 2 + whole_blocks(3),
            out_specs=pl.BlockSpec(memory_space=pltpu.VMEM),
            out_shape=jax.ShapeDtypeStruct((everyone, end_tiles, 8, 128), jnp.float32),
            scratch_shapes=[held, pltpu.VMEM((2, 96 * width, 128), jnp.float32)],
            compiler_params=params,
        )(half_index, half_offsets, own_inverse, other_inverse, lines)
    ending = lax.all_to_all(ending, MESH_AXES, 0, 0, tiled=True)
    with jax.named_scope("residual_end"):
        return pl.pallas_call(
            functools.partial(residual_end, peers),
            in_specs=whole_blocks(3),
            out_specs=pl.BlockSpec(memory_space=pltpu.VMEM),
            out_shape=jax.ShapeDtypeStruct(start_states.shape, jnp.float32),
            scratch_shapes=[pltpu.VMEM((components * (axial_rows // 2), columns, 128), jnp.float32)],
            compiler_params=params,
        )(ending, start_states, following)


def solution(mesh):
    peers = tuple(mesh.shape[name] for name in MESH_AXES)

    def body(start_states, radial_inverse, offsets, mode_count):
        if fits(start_states.shape, peers):
            return half_body(peers, start_states, radial_inverse, offsets, mode_count)
        return general_body(start_states, radial_inverse, offsets, mode_count)

    placed = (P("seg", None, "ax", "rad", None), P("ax", None, None), P("seg"), P())
    return jax.shard_map(
        body,
        mesh=mesh,
        in_specs=placed,
        out_specs=P("seg", None, "ax", "rad", None),
        check_vma=False,
    )
```

```python
import functools
import math

import jax
import jax.numpy as jnp
import ml_dtypes
import numpy as np
from jax import lax
from jax.experimental import pallas as pl
from jax.experimental.pallas import tpu as pltpu
from jax.sharding import PartitionSpec as P

STEPS = 2
MESH_AXES = ("seg", "rad", "ax")
VMEM_LIMIT = 48 * 1024 * 1024
FLOPS = 40_000_000_000

highest = lax.Precision.HIGHEST


def passed_along(value, axis, steps):
    count = lax.axis_size(axis)
    pairs = [(source, (source + steps) % count) for source in range(count)]
    return lax.ppermute(value, axis, pairs)


def padded_2(array, sides, width):
    for axis, dim in sides:
        peers, length = (lax.axis_size(axis), array.shape[dim])
        up = [(i, (i + 1) % peers) for i in range(peers)]
        down = [(j, i) for i, j in up]
        last = lax.slice_in_dim(array, length - width, length, axis=dim)
        leading = lax.slice_in_dim(array, 0, width, axis=dim)
        before = lax.ppermute(last, axis, up)
        after = lax.ppermute(leading, axis, down)
        array = jnp.concatenate([before, array, after], axis=dim)
    return array


def fourier_tables(columns, kept_modes):
    modes_total = columns // 2
    row_index = lax.broadcasted_iota(jnp.int32, (columns, columns), 0)
    point_index = lax.broadcasted_iota(jnp.int32, (columns, columns), 1)
    mode_index = row_index // 2
    phase = (mode_index * point_index % columns).astype(jnp.float32) * (2.0 * math.pi / columns)
    even_rows = row_index % 2 == 0
    cosine = jnp.cos(phase)
    sine = jnp.sin(phase)
    root = math.sqrt(modes_total)
    synthesis = jnp.where(even_rows, cosine, sine) / root
    weights = jnp.where(mode_index == 0, 1.0, 2.0)
    analysis = jnp.where(even_rows, weights * cosine, 2.0 * sine) * (root / columns)
    analysis = jnp.where(mode_index < kept_modes, analysis, 0.0)
    return (synthesis, analysis)


def radial_solve(pencils, radial_inverse, radial_rows):
    local_modes = radial_inverse.shape[0]
    local_columns, members, axial_cells, ignored = pencils.shape
    own_rows = lax.dynamic_slice_in_dim(
        radial_inverse, lax.axis_index("rad") * radial_rows, radial_rows, 1
    )
    piece = lax.all_gather(pencils, "rad", axis=3, tiled=True)
    piece_rows = piece.shape[3]
    grouped = piece.reshape(local_modes, 2, members, axial_cells, piece_rows)
    product = jnp.einsum("mrs,mkqzs->mkqzr", own_rows, grouped, precision=highest)
    return product.reshape(local_columns, members, axial_cells, radial_rows)


def general_body(start_states, radial_inverse, offsets, mode_count):
    groups, components, axial_rows, radial_rows, columns = start_states.shape
    synthesis, analysis = fourier_tables(columns, mode_count[0])
    radius = (
        (lax.axis_index("rad") * radial_rows + jnp.arange(radial_rows)).astype(jnp.float32) + 0.5
    ) / (radial_rows * lax.axis_size("rad"))
    profile = (1.0 - radius * radius).reshape(1, 1, 1, radial_rows, 1)
    following = passed_along(start_states[0], "seg", -1)
    current = start_states
    for step_index in range(STEPS):
        if step_index == 0:
            physical = jnp.einsum("gczrj,jp->gczrp", current, synthesis, precision=highest)
        else:
            physical = jnp.einsum("jgczr,jp->gczrp", current, synthesis, precision=highest)
        padded = padded_2(physical, (("ax", 2),), 1)
        gradient = (padded[:, :, 2:] - padded[:, :, :-2]) * 20.0
        advecting = profile + padded[:, 2:3, 1:-1]
        forcing = physical - 0.02 * advecting * gradient
        spectral = jnp.einsum("gczrp,jp->jgczr", forcing, analysis, precision=highest)
        pencils = lax.all_to_all(spectral, "ax", split_axis=0, concat_axis=3, tiled=True)
        local_columns = pencils.shape[0]
        axial_cells = pencils.shape[3]
        pencils = pencils.reshape(local_columns, groups * components, axial_cells, radial_rows)
        solved = radial_solve(pencils, radial_inverse, radial_rows)
        if step_index == STEPS - 1:
            blocks = solved.reshape(local_columns, groups, components, axial_cells, radial_rows)
            shifted = [
                jnp.roll(blocks[:, member], offsets[member], axis=2) for member in range(groups)
            ]
            solved = jnp.stack(shifted, axis=1).reshape(
                local_columns, groups * components, axial_cells, radial_rows
            )
        returned = lax.all_to_all(solved, "ax", split_axis=2, concat_axis=0, tiled=True)
        current = returned.reshape(columns, groups, components, axial_rows, radial_rows)
    ending = jnp.transpose(current, (1, 2, 3, 4, 0))
    upcoming = jnp.concatenate([start_states[1:], following[None]], axis=0)
    return ending - upcoming


def halves(high):
    top = high.astype(jnp.bfloat16)
    return top, (high - top.astype(jnp.float32)).astype(jnp.bfloat16)


def product(left, right, contract):
    return lax.dot_general(
        left, right, ((contract[:1], contract[1:]), ((), ())), preferred_element_type=jnp.float32
    )


def stacked_table(table):
    top = table.astype(ml_dtypes.bfloat16)
    rest = (table - top.astype(np.float64)).astype(ml_dtypes.bfloat16)
    return np.concatenate([top, top, rest], axis=1)


def column_order(columns, quarter_modes, shares):
    each = quarter_modes // shares
    order = []
    for share in range(shares):
        for low in range(2):
            for high in range(2):
                first = (2 * high + low) * quarter_modes + share * each
                order.extend(range(2 * first, 2 * (first + each)))
    assert sorted(order) == list(range(columns))
    return np.array(order)


def tables(columns, order):
    modes_total = columns // 2
    rows = np.arange(columns)
    mode = rows // 2
    phase = (mode[:, None] * np.arange(columns)[None, :]) % columns * (2.0 * np.pi / columns)
    even = (rows % 2 == 0)[:, None]
    root = math.sqrt(modes_total)
    synthesis = np.where(even, np.cos(phase), np.sin(phase)) / root
    weights = np.where(mode == 0, 1.0, 2.0)[:, None]
    analysis = np.where(even, weights * np.cos(phase), 2.0 * np.sin(phase)) * (root / columns)
    return (
        stacked_table(np.ascontiguousarray(synthesis.T)),
        stacked_table(np.ascontiguousarray(synthesis.T[:, order])),
        stacked_table(analysis[order]),
        mode[order].astype(np.int32),
    )


def lane_index():
    return lax.broadcasted_iota(jnp.int32, (1, 128), 1)


def physical_to_spectral(physical, profile, analysis):
    lane = lane_index()
    z = lane % 16
    forcing = []
    for tile in range(3):
        field = physical[tile]
        above = jnp.where(z == 15, pltpu.roll(field, 15, 1), pltpu.roll(field, 127, 1))
        below = jnp.where(z == 0, pltpu.roll(field, 113, 1), pltpu.roll(field, 1, 1))
        speed = jnp.where(lane < 32, pltpu.roll(field, 64, 1), pltpu.roll(field, 96, 1))
        speed = jnp.where(lane < 64, speed, field)
        speed = jnp.where(lane < 96, speed, physical[2])
        forcing.append(field - 0.4 * (profile[tile : tile + 1] + speed) * (above - below))
    forcing = jnp.concatenate(forcing, axis=1)
    top, rest = halves(forcing)
    return product(analysis, jnp.concatenate([top, rest, top], axis=0), (1, 0))


def write_spectral(spectral, out_ref):
    members, tiles, width, ignored = out_ref.shape
    for tile in range(tiles):
        block = spectral[:, tile * 128 : (tile + 1) * 128]
        out_ref[:, tile] = block.reshape(members, width, 128)


def pack_start(start_ref, out_ref):
    ignored, components, planes, each, columns = start_ref.shape
    seg_places, ignored, lows, strips, rows, ignored = out_ref.shape
    period = components * planes
    own = rows // period
    for component in range(components):
        for plane in range(planes):
            for seg in range(seg_places):
                for low in range(lows):
                    first = (seg * lows + low) * own
                    block = start_ref[0, component, plane, first : first + own]
                    at = pl.ds(component * planes + plane, own, stride=period)
                    for strip in range(strips):
                        out_ref[seg, 0, low, strip, at, :] = block[
                            :, strip * 128 : (strip + 1) * 128
                        ]


def first_phase_a(rows_ref, synthesis_ref, analysis_ref, profile_ref, out_ref):
    sources, strips = rows_ref.shape[:2]
    strip_rows = []
    for strip in range(strips):
        parts = []
        for tile in range(3):
            for radius, components in ((tile, range(3)), (3, (tile,))):
                for component in components:
                    first = 12 * radius + 4 * component
                    parts += [rows_ref[i, strip, first : first + 4] for i in range(sources)]
        strip_rows.append(jnp.concatenate(parts, axis=0))
    top, rest = halves(jnp.concatenate(strip_rows, axis=1))
    physical = product(synthesis_ref[...], jnp.concatenate([top, rest, top], axis=1), (1, 1))
    physical = [physical[:, tile * 128 : (tile + 1) * 128] for tile in range(3)]
    write_spectral(physical_to_spectral(physical, profile_ref[0], analysis_ref[...]), out_ref)


def later_phase_a(wire_ref, synthesis_ref, analysis_ref, profile_ref, out_ref):
    members, tiles, width, ignored = wire_ref.shape
    state = jnp.concatenate(
        [wire_ref[:, tile].reshape(members * width, 128) for tile in range(tiles)], axis=1
    )
    top, rest = halves(state)
    physical = product(synthesis_ref[...], jnp.concatenate([top, rest, top], axis=0), (1, 0))
    physical = [physical[:, tile * 128 : (tile + 1) * 128] for tile in range(3)]
    write_spectral(physical_to_spectral(physical, profile_ref[0], analysis_ref[...]), out_ref)


def unpack_radii(wire_ref, held_ref, places):
    members, tiles, width, ignored = wire_ref.shape
    lane = lane_index()
    for member in range(members):
        for group in range(tiles // 3):
            waves = [wire_ref[member, 3 * group + tile] for tile in range(3)]
            fourth = jnp.where(lane < 32, pltpu.roll(waves[0], 32, 1), pltpu.roll(waves[1], 64, 1))
            fourth = jnp.where(lane < 64, fourth, pltpu.roll(waves[2], 96, 1))
            base = (places[member] + 4 * group) * width
            for index, block in enumerate(waves + [fourth]):
                held_ref[base + index * width : base + (index + 1) * width, :] = block


def ordered_inverse(half_ref, own_ref, other_ref, top_ref, rest_ref):
    each = own_ref.shape[0]
    first_half = half_ref[0] == 0
    for index in range(each):
        here, there = own_ref[index], other_ref[index]
        for at, matrix in (
            (index, jnp.where(first_half, here, there)),
            (each + index, jnp.where(first_half, there, here)),
        ):
            top_ref[at], rest_ref[at] = halves(matrix)


def solved_modes(top_ref, rest_ref, held_ref, transposed, store):
    modes, radii, ignored = top_ref.shape
    width = 2 * modes
    for mode in range(modes):
        matrix_top, matrix_rest = top_ref[mode], rest_ref[mode]
        state = jnp.concatenate(
            [held_ref[pl.ds(2 * mode + part, radii, stride=width), :] for part in range(2)], axis=1
        )
        if transposed:
            top, rest = halves(state.T)
            solved = product(top, matrix_top, (1, 1))
            solved += product(rest, matrix_top, (1, 1)) + product(top, matrix_rest, (1, 1))
        else:
            top, rest = halves(state)
            solved = product(matrix_top, top, (1, 0))
            solved += product(matrix_top, rest, (1, 0)) + product(matrix_rest, top, (1, 0))
        store(mode, solved)


def phase_b(places, top_ref, rest_ref, wire_ref, out_ref, held_ref, solved_ref):
    members, tiles, width, ignored = wire_ref.shape
    radii = top_ref.shape[1]
    unpack_radii(wire_ref, held_ref, places)

    def store(mode, solved):
        for part in range(2):
            solved_ref[pl.ds(2 * mode + part, radii, stride=width), :] = solved[
                :, part * 128 : (part + 1) * 128
            ]

    solved_modes(top_ref, rest_ref, held_ref, False, store)
    lane = lane_index()
    for member in range(members):
        for group in range(tiles // 3):
            base = (places[member] + 4 * group) * width
            blocks = [solved_ref[base + i * width : base + (i + 1) * width, :] for i in range(4)]
            for tile in range(3):
                fourth = pltpu.roll(blocks[3], 96 - 32 * tile, 1)
                out_ref[member, 3 * group + tile] = jnp.where(lane < 96, blocks[tile], fourth)


def last_phase_b(
    places, peers, offset_ref, top_ref, rest_ref, wire_ref, out_ref, held_ref, solved_ref
):
    members, tiles, width, ignored = wire_ref.shape
    radii = top_ref.shape[1]
    seg_places, rad_places, ax_places = peers
    planes = 16 // ax_places
    each = radii // rad_places
    unpack_radii(wire_ref, held_ref, places)

    def store(mode, solved):
        for part in range(2):
            rows = pl.ds(2 * mode + part, 96, stride=width)
            block = solved[part * 128 : part * 128 + 96]
            solved_ref[0, rows, :] = block[:, :128]
            solved_ref[1, rows, 0 : radii - 128] = block[:, 128:]

    solved_modes(top_ref, rest_ref, held_ref, True, store)
    lane = lane_index()

    def radial_piece(low, high, rad, at):
        first = rad * each
        if first + each <= 128:
            return pltpu.roll(low, (at - first) % 128, 1)
        if first >= 128:
            return pltpu.roll(high, (at - first) % 128, 1)
        return pltpu.roll(jnp.where(lane >= first, low, high), (at - first) % 128, 1)

    for seg in range(seg_places):
        for ax in range(ax_places):
            blocks = {}
            for component in range(3):
                for plane in range(planes):
                    source = lax.rem(ax * planes + plane - offset_ref[seg] + 16, 16)
                    row = ((component * seg_places + seg) * 16 + source) * width
                    row = pl.multiple_of(row, 8)
                    blocks[component, plane] = (
                        solved_ref[0, pl.ds(row, width), :],
                        solved_ref[1, pl.ds(row, width), :],
                    )
            for rad in range(rad_places):
                pairs = []
                for component in range(3):
                    for pair in range(planes // 2):
                        left = radial_piece(*blocks[component, 2 * pair], rad, 0)
                        right = radial_piece(*blocks[component, 2 * pair + 1], rad, each)
                        pairs.append(jnp.where(lane < each, left, right))
                split = [
                    block[8 * part : 8 * part + 8] for part in range(width // 8) for block in pairs
                ]
                target = (seg * rad_places + rad) * ax_places + ax
                for group in range(len(split) // 4):
                    for tile in range(3):
                        fourth = pltpu.roll(split[4 * group + 3], 96 - 32 * tile, 1)
                        out_ref[target, 3 * group + tile] = jnp.where(
                            lane < 96, split[4 * group + tile], fourth
                        )
                whole = len(split) // 4
                for index in range(4 * whole, len(split)):
                    out_ref[target, 3 * whole + index - 4 * whole] = split[index]


def residual_end(peers, wire_ref, start_ref, following_ref, out_ref, held_ref):
    seg_places, rad_places, ax_places = peers
    groups, components, planes, each, columns = out_ref.shape
    lane = lane_index()
    shares = seg_places * rad_places
    width = columns // (2 * shares)
    chunk = width // 2
    count = (width // 8) * components * (planes // 2)
    for half in range(2):
        for share in range(shares):
            for low in range(2):
                source = share * ax_places + 2 * half + low
                split = []
                for group in range(count // 4):
                    waves = [wire_ref[source, 3 * group + tile] for tile in range(3)]
                    fourth = jnp.where(
                        lane < 32, pltpu.roll(waves[0], 32, 1), pltpu.roll(waves[1], 64, 1)
                    )
                    split += waves + [jnp.where(lane < 64, fourth, pltpu.roll(waves[2], 96, 1))]
                for index in range(count % 4):
                    split.append(wire_ref[source, 3 * (count // 4) + index])
                per_part = components * (planes // 2)
                for slot in range(per_part):
                    rows = jnp.concatenate(
                        [split[part * per_part + slot] for part in range(width // 8)], axis=0
                    )
                    for high in range(2):
                        at = (2 * high + low) * (columns // 4) + share * chunk
                        held_ref[slot, at : at + chunk, :] = rows[high * chunk : (high + 1) * chunk]
        for component in range(components):
            for pair in range(planes // 2):
                ending = held_ref[component * (planes // 2) + pair].T
                for side in range(2):
                    plane = 2 * pair + side
                    if half + 1 < groups:
                        upcoming = start_ref[half + 1, component, plane]
                    else:
                        upcoming = following_ref[component, plane]
                    out_ref[half, component, plane] = (
                        ending[side * each : (side + 1) * each] - upcoming
                    )


def whole_blocks(count):
    return [pl.BlockSpec(memory_space=pltpu.VMEM)] * count


def fits(shape, peers):
    groups, components, axial_rows, radial_rows, columns = shape
    seg_places, rad_places, ax_places = peers
    members = seg_places * rad_places * 2
    return (
        (groups, components, seg_places, ax_places) == (2, 3, 2, 4)
        and axial_rows * ax_places == 16
        and radial_rows == 48
        and rad_places * radial_rows == 192
        and columns == 384
        and members == 16
    )


def half_body(peers, start_states, radial_inverse, offsets, mode_count):
    groups, components, axial_rows, radial_rows, columns = start_states.shape
    seg_places, rad_places, ax_places = peers
    axial = axial_rows * ax_places
    radii = radial_rows * rad_places
    shares = seg_places * rad_places
    members = 2 * shares
    own_radii = radii // members
    own_modes = radial_inverse.shape[0] // shares
    width = columns // members
    tiles = own_radii * 3 // 4
    order = column_order(columns, radial_inverse.shape[0], shares)
    synthesis_natural, synthesis, analysis, mode_of_row = tables(columns, order)

    seg, rad, ax = (lax.axis_index(name) for name in MESH_AXES)
    half, low = ax // 2, ax % 2

    def device(s, r, a):
        return (s * rad_places + r) * ax_places + a

    half_groups = [
        [
            device(s, r, 2 * h + l)
            for s in range(seg_places)
            for r in range(rad_places)
            for l in range(2)
        ]
        for h in range(2)
    ]
    mirror = [(a, (a + 2) % 4) for a in range(4)]
    places = [
        r * radial_rows + (s * 2 + l) * own_radii
        for s in range(seg_places)
        for r in range(rad_places)
        for l in range(2)
    ]

    params = pltpu.CompilerParams(vmem_limit_bytes=VMEM_LIMIT)

    row_count = own_radii * components * axial_rows
    strips = columns // 128
    with jax.named_scope("pack_start"):
        split = pl.pallas_call(
            pack_start,
            grid=(groups,),
            in_specs=[pl.BlockSpec((1,) + start_states.shape[1:], lambda b: (b, 0, 0, 0, 0))],
            out_specs=pl.BlockSpec(
                (seg_places, 1, 2, strips, row_count, 128), lambda b: (0, b, 0, 0, 0, 0)
            ),
            out_shape=jax.ShapeDtypeStruct(
                (seg_places, groups, 2, strips, row_count, 128), jnp.float32
            ),
            compiler_params=params,
        )(start_states)
    split = split.reshape(seg_places * ax_places, strips, row_count, 128)
    rows = lax.all_to_all(split, ("seg", "ax"), 0, 0, tiled=True)

    share = seg * rad_places + rad
    own_inverse = lax.dynamic_slice_in_dim(radial_inverse, share * own_modes, own_modes, 0)
    following = passed_along(start_states[0], "seg", -1)
    swapped = passed_along(offsets, "seg", 1)
    low_offsets = jnp.where(seg == 0, offsets, swapped)
    high_offsets = jnp.where(seg == 0, swapped, offsets)
    half_offsets = jnp.stack([low_offsets[half], high_offsets[half]])
    half_index = half.reshape(1).astype(jnp.int32)
    rows, own_inverse, half_offsets, following = lax.optimization_barrier(
        (rows, own_inverse, half_offsets, following)
    )
    other_inverse = lax.ppermute(own_inverse, "ax", mirror)
    matrices = jax.ShapeDtypeStruct((2 * own_modes, radii, radii), jnp.bfloat16)
    with jax.named_scope("ordered_inverse"):
        inverse = pl.pallas_call(
            ordered_inverse,
            in_specs=[pl.BlockSpec(memory_space=pltpu.SMEM)] + whole_blocks(2),
            out_specs=whole_blocks(2),
            out_shape=[matrices, matrices],
            compiler_params=params,
            cost_estimate=pl.CostEstimate(
                flops=FLOPS, bytes_accessed=16 * own_modes * radii * radii, transcendentals=0
            ),
        )(half_index, own_inverse, other_inverse)

    kept = (jnp.asarray(mode_of_row) < mode_count[0])[:, None]
    analysis = jnp.where(kept, jnp.asarray(analysis), jnp.zeros((), jnp.bfloat16))
    synthesis_natural = jnp.asarray(synthesis_natural)
    synthesis = jnp.asarray(synthesis)
    first = rad * radial_rows + (seg * 2 + low) * own_radii
    tile_index = np.arange(tiles)[:, None]
    lane = np.arange(128)[None, :]
    local = 4 * (tile_index // 3) + np.where(lane < 96, tile_index % 3, 3)
    radius = ((first + jnp.asarray(local)).astype(jnp.float32) + 0.5) / radii
    profile = (1.0 - radius * radius).reshape(tiles // 3, 3, 128)

    wire = jax.ShapeDtypeStruct((members, tiles, width, 128), jnp.float32)
    wire_spec = pl.BlockSpec((members, 3, width, 128), lambda g: (0, g, 0, 0))
    table_spec = pl.BlockSpec((columns, 3 * columns), lambda g: (0, 0))
    profile_spec = pl.BlockSpec((1, 3, 128), lambda g: (g, 0, 0))
    held = pltpu.VMEM((radii * width, 128), jnp.float32)

    def exchanged(value):
        return lax.all_to_all(
            value, MESH_AXES, 0, 0, axis_index_groups=half_groups, tiled=True
        )

    with jax.named_scope("phase_a_first"):
        spectral = pl.pallas_call(
            first_phase_a,
            grid=(tiles // 3,),
            in_specs=[
                pl.BlockSpec((rows.shape[0], strips, 48, 128), lambda g: (0, 0, g, 0)),
                table_spec,
                table_spec,
                profile_spec,
            ],
            out_specs=wire_spec,
            out_shape=wire,
            compiler_params=params,
        )(rows, synthesis_natural, analysis, profile)
    lines = exchanged(spectral)
    with jax.named_scope("phase_b_first"):
        solved = pl.pallas_call(
            functools.partial(phase_b, places),
            in_specs=whole_blocks(3),
            out_specs=pl.BlockSpec(memory_space=pltpu.VMEM),
            out_shape=wire,
            scratch_shapes=[held, held],
            compiler_params=params,
        )(*inverse, lines)
    state = exchanged(solved)
    with jax.named_scope("phase_a_later"):
        spectral = pl.pallas_call(
            later_phase_a,
            grid=(tiles // 3,),
            in_specs=[wire_spec, table_spec, table_spec, profile_spec],
            out_specs=wire_spec,
            out_shape=wire,
            compiler_params=params,
        )(state, synthesis, analysis, profile)
    lines = exchanged(spectral)
    count = (width // 8) * components * (axial_rows // 2)
    end_tiles = (count // 4) * 3 + count % 4
    everyone = seg_places * rad_places * ax_places
    with jax.named_scope("phase_b_last"):
        ending = pl.pallas_call(
            functools.partial(last_phase_b, places, peers),
            in_specs=[pl.BlockSpec(memory_space=pltpu.SMEM)] + whole_blocks(3),
            out_specs=pl.BlockSpec(memory_space=pltpu.VMEM),
            out_shape=jax.ShapeDtypeStruct((everyone, end_tiles, 8, 128), jnp.float32),
            scratch_shapes=[held, pltpu.VMEM((2, 96 * width, 128), jnp.float32)],
            compiler_params=params,
        )(half_offsets, *inverse, lines)
    ending = lax.all_to_all(ending, MESH_AXES, 0, 0, tiled=True)
    with jax.named_scope("residual_end"):
        return pl.pallas_call(
            functools.partial(residual_end, peers),
            in_specs=whole_blocks(3),
            out_specs=pl.BlockSpec(memory_space=pltpu.VMEM),
            out_shape=jax.ShapeDtypeStruct(start_states.shape, jnp.float32),
            scratch_shapes=[pltpu.VMEM((components * (axial_rows // 2), columns, 128), jnp.float32)],
            compiler_params=params,
        )(ending, start_states, following)


def solution(mesh):
    peers = tuple(mesh.shape[name] for name in MESH_AXES)

    def body(start_states, radial_inverse, offsets, mode_count):
        if fits(start_states.shape, peers):
            return half_body(peers, start_states, radial_inverse, offsets, mode_count)
        return general_body(start_states, radial_inverse, offsets, mode_count)

    placed = (P("seg", None, "ax", "rad", None), P("ax", None, None), P("seg"), P())
    return jax.shard_map(
        body,
        mesh=mesh,
        in_specs=placed,
        out_specs=P("seg", None, "ax", "rad", None),
        check_vma=False,
    )
```

```python
import functools
import math

import jax
import jax.numpy as jnp
import ml_dtypes
import numpy as np
from jax import lax
from jax.experimental import pallas as pl
from jax.experimental.pallas import tpu as pltpu
from jax.sharding import PartitionSpec as P

STEPS = 2
MESH_AXES = ("seg", "rad", "ax")
UNROLL = [12, 2, 2, 2, 2, 2, 16, 6]
VMEM_LIMIT = 24 * 1024 * 1024
FLOPS = 40_000_000_000

highest = lax.Precision.HIGHEST


def passed_along(value, axis, steps):
    count = lax.axis_size(axis)
    pairs = [(source, (source + steps) % count) for source in range(count)]
    return lax.ppermute(value, axis, pairs)


def padded_2(array, sides, width):
    for axis, dim in sides:
        peers, length = (lax.axis_size(axis), array.shape[dim])
        up = [(i, (i + 1) % peers) for i in range(peers)]
        down = [(j, i) for i, j in up]
        last = lax.slice_in_dim(array, length - width, length, axis=dim)
        leading = lax.slice_in_dim(array, 0, width, axis=dim)
        before = lax.ppermute(last, axis, up)
        after = lax.ppermute(leading, axis, down)
        array = jnp.concatenate([before, array, after], axis=dim)
    return array


def fourier_tables(columns, kept_modes):
    modes_total = columns // 2
    row_index = lax.broadcasted_iota(jnp.int32, (columns, columns), 0)
    point_index = lax.broadcasted_iota(jnp.int32, (columns, columns), 1)
    mode_index = row_index // 2
    phase = (mode_index * point_index % columns).astype(jnp.float32) * (2.0 * math.pi / columns)
    even_rows = row_index % 2 == 0
    cosine = jnp.cos(phase)
    sine = jnp.sin(phase)
    root = math.sqrt(modes_total)
    synthesis = jnp.where(even_rows, cosine, sine) / root
    weights = jnp.where(mode_index == 0, 1.0, 2.0)
    analysis = jnp.where(even_rows, weights * cosine, 2.0 * sine) * (root / columns)
    analysis = jnp.where(mode_index < kept_modes, analysis, 0.0)
    return (synthesis, analysis)


def radial_solve(pencils, radial_inverse, radial_rows):
    local_modes = radial_inverse.shape[0]
    local_columns, members, axial_cells, ignored = pencils.shape
    own_rows = lax.dynamic_slice_in_dim(
        radial_inverse, lax.axis_index("rad") * radial_rows, radial_rows, 1
    )
    piece = lax.all_gather(pencils, "rad", axis=3, tiled=True)
    piece_rows = piece.shape[3]
    grouped = piece.reshape(local_modes, 2, members, axial_cells, piece_rows)
    product = jnp.einsum("mrs,mkqzs->mkqzr", own_rows, grouped, precision=highest)
    return product.reshape(local_columns, members, axial_cells, radial_rows)


def general_body(start_states, radial_inverse, offsets, mode_count):
    groups, components, axial_rows, radial_rows, columns = start_states.shape
    synthesis, analysis = fourier_tables(columns, mode_count[0])
    radius = (
        (lax.axis_index("rad") * radial_rows + jnp.arange(radial_rows)).astype(jnp.float32) + 0.5
    ) / (radial_rows * lax.axis_size("rad"))
    profile = (1.0 - radius * radius).reshape(1, 1, 1, radial_rows, 1)
    following = passed_along(start_states[0], "seg", -1)
    current = start_states
    for step_index in range(STEPS):
        if step_index == 0:
            physical = jnp.einsum("gczrj,jp->gczrp", current, synthesis, precision=highest)
        else:
            physical = jnp.einsum("jgczr,jp->gczrp", current, synthesis, precision=highest)
        padded = padded_2(physical, (("ax", 2),), 1)
        gradient = (padded[:, :, 2:] - padded[:, :, :-2]) * 20.0
        advecting = profile + padded[:, 2:3, 1:-1]
        forcing = physical - 0.02 * advecting * gradient
        spectral = jnp.einsum("gczrp,jp->jgczr", forcing, analysis, precision=highest)
        pencils = lax.all_to_all(spectral, "ax", split_axis=0, concat_axis=3, tiled=True)
        local_columns = pencils.shape[0]
        axial_cells = pencils.shape[3]
        pencils = pencils.reshape(local_columns, groups * components, axial_cells, radial_rows)
        solved = radial_solve(pencils, radial_inverse, radial_rows)
        if step_index == STEPS - 1:
            blocks = solved.reshape(local_columns, groups, components, axial_cells, radial_rows)
            shifted = [
                jnp.roll(blocks[:, member], offsets[member], axis=2) for member in range(groups)
            ]
            solved = jnp.stack(shifted, axis=1).reshape(
                local_columns, groups * components, axial_cells, radial_rows
            )
        returned = lax.all_to_all(solved, "ax", split_axis=2, concat_axis=0, tiled=True)
        current = returned.reshape(columns, groups, components, axial_rows, radial_rows)
    ending = jnp.transpose(current, (1, 2, 3, 4, 0))
    upcoming = jnp.concatenate([start_states[1:], following[None]], axis=0)
    return ending - upcoming


def halves(high):
    top = high.astype(jnp.bfloat16)
    return top, (high - top.astype(jnp.float32)).astype(jnp.bfloat16)


def product(left, right, contract):
    return lax.dot_general(
        left, right, ((contract[:1], contract[1:]), ((), ())), preferred_element_type=jnp.float32
    )


def stacked_table(table):
    top = table.astype(ml_dtypes.bfloat16)
    rest = (table - top.astype(np.float64)).astype(ml_dtypes.bfloat16)
    return np.concatenate([top, top, rest], axis=1)


def column_order(columns, quarter_modes, shares):
    each = quarter_modes // shares
    order = []
    for share in range(shares):
        for low in range(2):
            for high in range(2):
                first = (2 * high + low) * quarter_modes + share * each
                order.extend(range(2 * first, 2 * (first + each)))
    assert sorted(order) == list(range(columns))
    return np.array(order)


def tables(columns, order):
    modes_total = columns // 2
    rows = np.arange(columns)
    mode = rows // 2
    phase = (mode[:, None] * np.arange(columns)[None, :]) % columns * (2.0 * np.pi / columns)
    even = (rows % 2 == 0)[:, None]
    root = math.sqrt(modes_total)
    synthesis = np.where(even, np.cos(phase), np.sin(phase)) / root
    weights = np.where(mode == 0, 1.0, 2.0)[:, None]
    analysis = np.where(even, weights * np.cos(phase), 2.0 * np.sin(phase)) * (root / columns)
    return (
        np.ascontiguousarray(stacked_table(synthesis.T).T),
        stacked_table(np.ascontiguousarray(synthesis.T[:, order])),
        stacked_table(analysis[order]),
        mode[order].astype(np.int32),
    )


def lane_index(block):
    return lax.broadcasted_iota(jnp.int32, block.shape, 1)


def spread(tiles, fourth):
    lane = lane_index(fourth)
    return [
        jnp.where(lane < 96, block, pltpu.roll(fourth, 96 - 32 * index, 1))
        for index, block in enumerate(tiles)
    ]


def gathered(waves):
    lane = lane_index(waves[0])
    fourth = jnp.where(lane < 32, pltpu.roll(waves[0], 32, 1), pltpu.roll(waves[1], 64, 1))
    return waves + [jnp.where(lane < 64, fourth, pltpu.roll(waves[2], 96, 1))]


def every(blocks, first, step):
    return jnp.concatenate(blocks[first::step], axis=0)


def pieces(block):
    return [block[at : at + 8] for at in range(0, block.shape[0], 8)]


def spread_list(blocks):
    whole = len(blocks) // 4 * 4
    quarters = [every(blocks[:whole], first, 4) for first in range(4)]
    full = [pieces(block) for block in spread(quarters[:3], quarters[3])]
    return [block for group in zip(*full) for block in group] + blocks[whole:]


def gathered_list(full, count):
    whole = count // 4 * 3
    blocks = [pieces(block) for block in gathered([every(full[:whole], i, 3) for i in range(3)])]
    return [block for group in zip(*blocks) for block in group] + full[whole:]


def physical_to_spectral(physical, profile, analysis):
    lane = lane_index(physical[0])
    z = lane & 7
    low = lane & 16 == 0
    forcing = []
    for tile in range(3):
        field = physical[tile]
        above = jnp.where(low, pltpu.roll(field, 119, 1), pltpu.roll(field, 23, 1))
        above = jnp.where(z < 7, pltpu.roll(field, 127, 1), above)
        below = jnp.where(low, pltpu.roll(field, 105, 1), pltpu.roll(field, 9, 1))
        below = jnp.where(z > 0, pltpu.roll(field, 1, 1), below)
        speed = jnp.where(lane < 32, pltpu.roll(field, 64, 1), pltpu.roll(field, 96, 1))
        speed = jnp.where(lane < 64, speed, field)
        speed = jnp.where(lane < 96, speed, physical[2])
        forcing.append(field - 0.4 * (profile[tile : tile + 1] + speed) * (above - below))
    forcing = jnp.concatenate(forcing, axis=1)
    top, rest = halves(forcing)
    return product(analysis, jnp.concatenate([top, rest, top], axis=0), (1, 0))


def write_spectral(spectral, count_ref, mode_ref, out_ref):
    members, ignored, width, ignored = out_ref.shape
    kept = mode_ref[...] < count_ref[0]
    for tile in range(3):
        block = jnp.where(kept, spectral[:, tile * 128 : (tile + 1) * 128], 0.0)
        out_ref[:, tile] = block.reshape(members, width, 128)


def first_phase_a(
    count_ref,
    before_ref,
    own_ref,
    after_ref,
    synthesis_ref,
    analysis_ref,
    mode_ref,
    profile_ref,
    out_ref,
    held_ref,
):
    groups, components, planes, radii, columns = own_ref.shape
    strips = columns // 128
    rows = []
    for segment in range(groups):
        for component in range(components):
            rows.append(before_ref[segment, component])
            rows += [own_ref[segment, component, plane] for plane in range(planes)]
            rows.append(after_ref[segment, component])
    top, rest = halves(jnp.concatenate(rows, axis=0))
    physical = product(jnp.concatenate([top, rest, top], axis=1), synthesis_ref[...], (1, 0))
    physical = physical.reshape(groups, components, planes + 2, radii, columns)
    profile = jnp.concatenate([profile_ref[...]] * strips, axis=1)
    for segment in range(groups):
        for plane in range(planes):
            speed = 0.4 * (profile + physical[segment, 2, plane + 1])
            for component in range(components):
                line = physical[segment, component]
                forcing = line[plane + 1] - speed * (line[plane + 2] - line[plane])
                first = (component * groups + segment) * radii * planes
                at = pl.ds(first + plane, radii, stride=planes)
                for strip in range(strips):
                    held_ref[strip, at, :] = forcing[:, strip * 128 : (strip + 1) * 128]
    quad = 4 * planes
    lines = []
    for strip in range(strips):
        parts = []
        for tile in range(3):
            for four, blocks in ((tile, range(6)), (3, (2 * tile, 2 * tile + 1))):
                for block in blocks:
                    at = block * radii * planes + four * quad
                    parts.append(held_ref[strip, at : at + quad, :])
        lines.append(jnp.concatenate(parts, axis=0))
    top, rest = halves(jnp.concatenate(lines, axis=1))
    spectral = product(analysis_ref[...], jnp.concatenate([top, rest, top], axis=1), (1, 1))
    write_spectral(spectral, count_ref, mode_ref, out_ref)


def later_phase_a(
    members,
    count_ref,
    wire_ref,
    synthesis_ref,
    analysis_ref,
    mode_ref,
    profile_ref,
    out_ref,
    state_ref,
):
    sources, tiles, ignored, ignored = wire_ref.shape
    groups, ignored, ignored = state_ref.shape
    parts = out_ref.shape[2] // 8
    pairs = 2 * groups
    group = pl.program_id(0)

    @pl.when(group == 0)
    def _():
        low = lax.broadcasted_iota(jnp.int32, (8 * pairs, 128), 1) & 16 == 0

        @pl.loop(0, members, unroll=UNROLL[5])
        def _(member):
            first = member // 2 * 4 + lax.rem(member, 2)
            both = [
                gathered_list(pieces(wire_ref[source].reshape(tiles * 8, 128)), pairs * parts)
                for source in (first, first + 2)
            ]
            for part in range(parts):
                at = pl.ds(pl.multiple_of((member * parts + part) * 8, 8), 8)
                one, two = (
                    jnp.concatenate(blocks[part * pairs : (part + 1) * pairs], axis=0)
                    for blocks in both
                )
                even = pieces(jnp.where(low, one, pltpu.roll(two, 16, 1)))
                odd = pieces(jnp.where(low, pltpu.roll(one, 112, 1), two))
                radii = [every(even, 0, 2), every(odd, 0, 2), every(even, 1, 2), every(odd, 1, 2)]
                for tile, block in enumerate(spread(radii[:3], radii[3])):
                    for place in range(groups):
                        state_ref[place, at, tile * 128 : (tile + 1) * 128] = block[
                            8 * place : 8 * place + 8
                        ]

    top, rest = halves(state_ref[group])
    physical = product(synthesis_ref[...], jnp.concatenate([top, rest, top], axis=0), (1, 0))
    physical = [physical[:, tile * 128 : (tile + 1) * 128] for tile in range(3)]
    spectral = physical_to_spectral(physical, profile_ref[0], analysis_ref[...])
    write_spectral(spectral, count_ref, mode_ref, out_ref)


def unpack_quads(wire_ref, held_ref, peers):
    members, tiles, width, ignored = wire_ref.shape
    seg_places, rad_places, ignored = peers
    lane = lax.broadcasted_iota(jnp.int32, (4 * width, 128), 1)
    eight, four = lane & 8 == 0, lane & 4 == 0

    def swapped(mask, step, left, right):
        return (
            jnp.where(mask, left, pltpu.roll(right, step, 1)),
            jnp.where(mask, pltpu.roll(left, 128 - step, 1), right),
        )

    groups = tiles // 3

    @pl.loop(0, rad_places * groups, unroll=UNROLL[1])
    def _(index):
        rad, group = index // groups, lax.rem(index, groups)
        sources = [(s * rad_places + rad) * 2 + l for s in range(seg_places) for l in range(2)]
        waves = [
            jnp.concatenate([wire_ref[source, 3 * group + tile] for source in sources], axis=0)
            for tile in range(3)
        ]
        quads = gathered(waves)
        one, two, three, last = (
            jnp.concatenate([quad[at : at + width] for quad in quads], axis=0)
            for at in range(0, 4 * width, width)
        )
        one, three = swapped(eight, 8, one, three)
        two, last = swapped(eight, 8, two, last)
        radii = swapped(four, 4, one, two) + swapped(four, 4, three, last)
        for place, block in enumerate(radii):
            for quad in range(4):
                at = pl.multiple_of((index * 16 + 4 * quad + place) * width, 8)
                held_ref[pl.ds(at, width), :] = block[quad * width : (quad + 1) * width]


def first_radius(member, own):
    rad = lax.rem(member // 2, 4)
    return ((rad * 2 + member // 8) * 2 + lax.rem(member, 2)) * own


def unpack_radii(wire_ref, held_ref):
    members, tiles, width, ignored = wire_ref.shape
    own = tiles * 4 // 3

    @pl.loop(0, members, unroll=UNROLL[2])
    def _(member):
        first = first_radius(member, own)
        waves = [
            jnp.concatenate([wire_ref[member, at] for at in range(tile, tiles, 3)], axis=0)
            for tile in range(3)
        ]
        for index, block in enumerate(gathered(waves)):
            for group in range(tiles // 3):
                at = pl.multiple_of((first + 4 * group + index) * width, 8)
                held_ref[pl.ds(at, width), :] = block[group * width : (group + 1) * width]


def pack_inverse(place_ref, inverse_ref, out_ref, held_ref, sem):
    each, radii, ignored = held_ref.shape
    copy = pltpu.make_async_copy(inverse_ref.at[pl.ds(place_ref[0] * each, each)], held_ref, sem)
    copy.start()
    copy.wait()
    for index in range(each):
        out_ref[index] = held_ref[index, :, :128]
    for index in range(each // 2):
        out_ref[each + index, :, :64] = held_ref[index, :, 128:]
        out_ref[each + index, :, 64:] = held_ref[each // 2 + index, :, 128:]


def ordered_inverse(place_ref, own_ref, other_ref, top_ref, rest_ref):
    each = top_ref.shape[0] // 2
    first_half = place_ref[1] == 0

    def matrix(ref, index):
        side = index // (each // 2) * 64
        tail = ref[each + index % (each // 2), :, side : side + 64]
        return jnp.concatenate([ref[index], tail], axis=1)

    for index in range(each):
        here, there = matrix(own_ref, index), matrix(other_ref, index)
        top_ref[index], rest_ref[index] = halves(jnp.where(first_half, here, there))
        top_ref[each + index], rest_ref[each + index] = halves(jnp.where(first_half, there, here))


def inverse_copies(top_hbm, rest_hbm, top_ref, rest_ref, sems):
    copies = [
        pltpu.make_async_copy(source, target, sems.at[index])
        for index, (source, target) in enumerate(((top_hbm, top_ref), (rest_hbm, rest_ref)))
    ]
    for copy in copies:
        copy.start()
    return copies


def solved_modes(top_ref, rest_ref, held_ref, transposed, store):
    modes, radii, ignored = top_ref.shape
    width = 2 * modes

    @pl.loop(0, modes, unroll=UNROLL[0])
    def _(mode):
        matrix_top, matrix_rest = top_ref[mode], rest_ref[mode]
        state = jnp.concatenate(
            [held_ref[pl.ds(2 * mode + part, radii, stride=width), :] for part in range(2)], axis=1
        )
        if transposed:
            top, rest = halves(state.T)
            solved = product(top, matrix_top, (1, 1))
            solved += product(rest, matrix_top, (1, 1)) + product(top, matrix_rest, (1, 1))
        else:
            top, rest = halves(state)
            solved = product(matrix_top, top, (1, 0))
            solved += product(matrix_top, rest, (1, 0)) + product(matrix_rest, top, (1, 0))
        store(mode, solved)


def phase_b(
    peers, top_hbm, rest_hbm, wire_ref, out_ref, held_ref, solved_ref, top_ref, rest_ref, sems
):
    members, tiles, width, ignored = wire_ref.shape
    radii = top_ref.shape[1]
    ax_places = peers[2]
    copies = inverse_copies(top_hbm, rest_hbm, top_ref, rest_ref, sems)
    unpack_quads(wire_ref, held_ref, peers)
    for copy in copies:
        copy.wait()

    def store(mode, solved):
        for part in range(2):
            solved_ref[pl.ds(2 * mode + part, radii, stride=width), :] = solved[
                :, part * 128 : (part + 1) * 128
            ]

    solved_modes(top_ref, rest_ref, held_ref, False, store)
    own = radii // members
    low = lax.broadcasted_iota(jnp.int32, (own * width // 2, 128), 1) & 16 == 0

    @pl.loop(0, members, unroll=UNROLL[3])
    def _(member):
        place = first_radius(member, own) * width
        for half in range(2):
            one, two = (
                jnp.concatenate(
                    [
                        solved_ref[pl.ds(pl.multiple_of(place + index * width, 8), width), :]
                        for index in range(first, own, 2)
                    ],
                    axis=0,
                )
                for first in range(2)
            )
            if half == 0:
                blocks = pieces(jnp.where(low, one, pltpu.roll(two, 16, 1)))
            else:
                blocks = pieces(jnp.where(low, pltpu.roll(one, 112, 1), two))
            parts = width // 8
            split = [block for part in range(parts) for block in blocks[part::parts]]
            target = member // 2 * ax_places + 2 * half + lax.rem(member, 2)
            for index, block in enumerate(spread_list(split)):
                out_ref[target, index] = block


def last_phase_b(
    peers,
    place_ref,
    own_offset_ref,
    other_offset_ref,
    top_hbm,
    rest_hbm,
    wire_ref,
    out_ref,
    held_ref,
    solved_ref,
    top_ref,
    rest_ref,
    sems,
):
    members, tiles, width, ignored = wire_ref.shape
    radii = top_ref.shape[1]
    seg_places, rad_places, ax_places = peers
    planes = 16 // ax_places
    each = radii // rad_places
    copies = inverse_copies(top_hbm, rest_hbm, top_ref, rest_ref, sems)
    unpack_radii(wire_ref, held_ref)
    for copy in copies:
        copy.wait()

    def store(mode, solved):
        for part in range(2):
            rows = pl.ds(2 * mode + part, 96, stride=width)
            block = solved[part * 128 : part * 128 + 96]
            solved_ref[0, rows, :] = block[:, :128]
            solved_ref[1, rows, 0 : radii - 128] = block[:, 128:]

    solved_modes(top_ref, rest_ref, held_ref, True, store)
    lane = lax.broadcasted_iota(jnp.int32, (planes // 2 * width, 128), 1)

    def radial_piece(low, high, rad, at):
        first = rad * each
        if first + each <= 128:
            return pltpu.roll(low, (at - first) % 128, 1)
        if first >= 128:
            return pltpu.roll(high, (at - first) % 128, 1)
        return pltpu.roll(jnp.where(lane >= first, low, high), (at - first) % 128, 1)

    half = place_ref[1]

    @pl.loop(0, seg_places * ax_places, unroll=UNROLL[4])
    def _(index):
        seg, ax = index // ax_places, lax.rem(index, ax_places)
        offset = jnp.where(place_ref[2] == seg, own_offset_ref[half], other_offset_ref[half])
        blocks = {}
        for component in range(3):
            for plane in range(planes):
                source = lax.rem(ax * planes + plane - offset + 16, 16)
                row = (component * 32 + source // 8 * 16 + seg * 8 + lax.rem(source, 8)) * width
                row = pl.multiple_of(row, 8)
                blocks[component, plane] = row
        for rad in range(rad_places):
            parts = width // 8
            slots = []
            for component in range(3):
                sides = []
                for side in range(2):
                    rows = [
                        pl.ds(blocks[component, plane], width) for plane in range(side, planes, 2)
                    ]
                    low, high = (
                        jnp.concatenate([solved_ref[strip, at, :] for at in rows], axis=0)
                        for strip in range(2)
                    )
                    sides.append(radial_piece(low, high, rad, side * each))
                slots += pieces(jnp.where(lane < each, *sides))
            split = [block for part in range(parts) for block in slots[part::parts]]
            target = (seg * rad_places + rad) * ax_places + ax
            for at, block in enumerate(spread_list(split)):
                out_ref[target, at] = block


def residual_end(peers, wire_ref, start_ref, following_ref, out_ref, held_ref):
    seg_places, rad_places, ax_places = peers
    groups, components, planes, each, columns = out_ref.shape
    shares = seg_places * rad_places
    width = columns // (2 * shares)
    chunk = width // 2
    count = (width // 8) * components * (planes // 2)
    slots = components * (planes // 2)
    for half in range(2):

        @pl.loop(0, 2 * shares, unroll=UNROLL[6])
        def _(member):
            share, low = member // 2, lax.rem(member, 2)
            source = share * ax_places + 2 * half + low
            split = gathered_list(pieces(wire_ref[source].reshape(-1, 128)), count)
            for slot in range(slots):
                parts = [split[part * slots + slot] for part in range(width // 8)]
                rows = jnp.concatenate(parts, axis=0)
                for high in range(2):
                    at = (2 * high + low) * (columns // 4) + share * chunk
                    held_ref[slot, pl.ds(at, chunk), :] = rows[high * chunk : (high + 1) * chunk]

        @pl.loop(0, slots, unroll=UNROLL[7])
        def _(slot):
            component, pair = slot // (planes // 2), lax.rem(slot, planes // 2)
            ending = held_ref[slot].T
            for side in range(2):
                plane = 2 * pair + side
                if half + 1 < groups:
                    upcoming = start_ref[half + 1, component, plane]
                else:
                    upcoming = following_ref[component, plane]
                out_ref[half, component, plane] = ending[side * each : (side + 1) * each] - upcoming


def in_place(value):
    return pltpu.with_memory_space_constraint(value, pltpu.HBM)


def whole_blocks(count):
    return [pl.BlockSpec(memory_space=pltpu.VMEM)] * count


def fits(shape, peers):
    groups, components, axial_rows, radial_rows, columns = shape
    seg_places, rad_places, ax_places = peers
    members = seg_places * rad_places * 2
    return (
        (groups, components, seg_places, ax_places) == (2, 3, 2, 4)
        and axial_rows * ax_places == 16
        and radial_rows == 48
        and rad_places * radial_rows == 192
        and columns == 384
        and members == 16
    )


def half_body(peers, start_states, radial_inverse, offsets, mode_count):
    groups, components, axial_rows, radial_rows, columns = start_states.shape
    seg_places, rad_places, ax_places = peers
    axial = axial_rows * ax_places
    radii = radial_rows * rad_places
    shares = seg_places * rad_places
    members = 2 * shares
    own_radii = radii // members
    own_modes = radial_inverse.shape[0] // shares
    width = columns // members
    tiles = own_radii * 3 // 4
    order = column_order(columns, radial_inverse.shape[0], shares)
    synthesis_natural, synthesis, analysis, mode_of_row = tables(columns, order)

    seg, rad, ax = (lax.axis_index(name) for name in MESH_AXES)
    half, low = ax // 2, ax % 2

    def device(s, r, a):
        return (s * rad_places + r) * ax_places + a

    half_groups = [
        [
            device(s, r, 2 * h + l)
            for s in range(seg_places)
            for r in range(rad_places)
            for l in range(2)
        ]
        for h in range(2)
    ]
    mirror = [(a, (a + 2) % 4) for a in range(4)]
    params = pltpu.CompilerParams(vmem_limit_bytes=VMEM_LIMIT)
    up = [(i, (i + 1) % ax_places) for i in range(ax_places)]
    down = [(j, i) for i, j in up]
    before = lax.ppermute(start_states[:, :, axial_rows - 1], "ax", up)
    after = lax.ppermute(start_states[:, :, 0], "ax", down)

    share = seg * rad_places + rad
    place = jnp.stack([share, half, seg]).astype(jnp.int32)
    with jax.named_scope("pack_inverse"):
        dense_inverse = pl.pallas_call(
            pack_inverse,
            in_specs=[
                pl.BlockSpec(memory_space=pltpu.SMEM),
                pl.BlockSpec(memory_space=pltpu.HBM),
            ],
            out_specs=pl.BlockSpec(memory_space=pltpu.VMEM),
            out_shape=jax.ShapeDtypeStruct((own_modes * 3 // 2, radii, 128), jnp.float32),
            scratch_shapes=[
                pltpu.VMEM((own_modes, radii, radii), jnp.float32),
                pltpu.SemaphoreType.DMA,
            ],
            compiler_params=params,
        )(place, in_place(radial_inverse))
    other_offsets = passed_along(offsets, "seg", 1)
    first = rad * radial_rows + (seg * 2 + low) * own_radii
    tile_index = np.arange(tiles)[:, None]
    lane = np.arange(128)[None, :]
    local = 4 * (tile_index // 3) + np.where(lane < 96, tile_index % 3, 3)
    radius = ((first + jnp.asarray(local)).astype(jnp.float32) + 0.5) / radii
    profile = (1.0 - radius * radius).reshape(tiles // 3, 3, 128)

    own_radius = ((rad * radial_rows + jnp.arange(radial_rows)).astype(jnp.float32) + 0.5) / radii
    own_profile = jnp.broadcast_to((1.0 - own_radius * own_radius)[:, None], (radial_rows, 128))

    following = passed_along(start_states[0], "seg", -1)
    before, after, dense_inverse, following, other_offsets, profile, own_profile = (
        lax.optimization_barrier(
            (before, after, dense_inverse, following, other_offsets, profile, own_profile)
        )
    )
    other_inverse = lax.ppermute(dense_inverse, "ax", mirror)
    matrices = jax.ShapeDtypeStruct((2 * own_modes, radii, radii), jnp.bfloat16)
    in_hbm = [pl.BlockSpec(memory_space=pltpu.HBM)] * 2
    inverse_scratch = [pltpu.VMEM(matrices.shape, matrices.dtype)] * 2
    inverse_scratch += [pltpu.SemaphoreType.DMA((2,))]
    with jax.named_scope("ordered_inverse"):
        inverse = pl.pallas_call(
            ordered_inverse,
            in_specs=[pl.BlockSpec(memory_space=pltpu.SMEM)] + whole_blocks(2),
            out_specs=[pl.BlockSpec(matrices.shape, lambda: (0, 0, 0))] * 2,
            out_shape=[pltpu.HBM(matrices.shape, matrices.dtype)] * 2,
            compiler_params=params,
            cost_estimate=pl.CostEstimate(
                flops=FLOPS, bytes_accessed=16 * own_modes * radii * radii, transcendentals=0
            ),
        )(place, dense_inverse, other_inverse)
    synthesis_natural, synthesis, analysis = (
        jnp.asarray(table) for table in (synthesis_natural, synthesis, analysis)
    )
    mode_rows = jnp.asarray(np.repeat(mode_of_row[:, None], 128, axis=1))
    wire = jax.ShapeDtypeStruct((members, tiles, width, 128), jnp.float32)
    wire_spec = pl.BlockSpec((members, 3, width, 128), lambda g: (0, g, 0, 0))
    held = pltpu.VMEM((radii * width, 128), jnp.float32)
    count = (width // 8) * components * (axial_rows // 2)
    end_tiles = (count // 4) * 3 + count % 4
    everyone = seg_places * rad_places * ax_places
    spread_wire = jax.ShapeDtypeStruct((everyone, end_tiles, 8, 128), jnp.float32)

    def exchanged(value):
        return lax.all_to_all(
            value, MESH_AXES, 0, 0, axis_index_groups=half_groups, tiled=True
        )

    step = radial_rows // 3
    halo_spec = pl.BlockSpec((groups, components, step, columns), lambda g: (0, 0, g, 0))
    with jax.named_scope("phase_a_first"):
        spectral = pl.pallas_call(
            first_phase_a,
            grid=(3,),
            in_specs=[
                pl.BlockSpec(memory_space=pltpu.SMEM),
                halo_spec,
                pl.BlockSpec(
                    (groups, components, axial_rows, step, columns), lambda g: (0, 0, 0, g, 0)
                ),
                halo_spec,
                pl.BlockSpec((3 * columns, columns), lambda g: (0, 0)),
                pl.BlockSpec((columns, 3 * columns), lambda g: (0, 0)),
                pl.BlockSpec((columns, 128), lambda g: (0, 0)),
                pl.BlockSpec((step, 128), lambda g: (g, 0)),
            ],
            out_specs=wire_spec,
            out_shape=wire,
            scratch_shapes=[
                pltpu.VMEM(
                    (columns // 128, groups * components * axial_rows * step, 128), jnp.float32
                )
            ],
            compiler_params=params,
        )(
            mode_count,
            before,
            start_states,
            after,
            synthesis_natural,
            analysis,
            mode_rows,
            own_profile,
        )
    lines = exchanged(spectral)
    with jax.named_scope("phase_b_first"):
        solved = pl.pallas_call(
            functools.partial(phase_b, peers),
            in_specs=in_hbm + whole_blocks(1),
            out_specs=pl.BlockSpec(memory_space=pltpu.VMEM),
            out_shape=spread_wire,
            scratch_shapes=[held, held] + inverse_scratch,
            compiler_params=params,
        )(*map(in_place, inverse), lines)
    state = lax.all_to_all(solved, MESH_AXES, 0, 0, tiled=True)
    with jax.named_scope("phase_a_later"):
        spectral = pl.pallas_call(
            functools.partial(later_phase_a, members),
            grid=(tiles // 3,),
            in_specs=[
                pl.BlockSpec(memory_space=pltpu.SMEM),
                pl.BlockSpec(spread_wire.shape, lambda g: (0, 0, 0, 0)),
                pl.BlockSpec((columns, 3 * columns), lambda g: (0, 0)),
                pl.BlockSpec((columns, 3 * columns), lambda g: (0, 0)),
                pl.BlockSpec((columns, 128), lambda g: (0, 0)),
                pl.BlockSpec((1, 3, 128), lambda g: (g, 0, 0)),
            ],
            out_specs=wire_spec,
            out_shape=wire,
            scratch_shapes=[pltpu.VMEM((tiles // 3, columns, 3 * 128), jnp.float32)],
            compiler_params=params,
        )(mode_count, state, synthesis, analysis, mode_rows, profile)
    lines = exchanged(spectral)
    with jax.named_scope("phase_b_last"):
        ending = pl.pallas_call(
            functools.partial(last_phase_b, peers),
            in_specs=[pl.BlockSpec(memory_space=pltpu.SMEM)] * 3 + in_hbm + whole_blocks(1),
            out_specs=pl.BlockSpec(memory_space=pltpu.VMEM),
            out_shape=spread_wire,
            scratch_shapes=[held, pltpu.VMEM((2, 96 * width, 128), jnp.float32)]
            + inverse_scratch,
            compiler_params=params,
        )(place, offsets, other_offsets, *map(in_place, inverse), lines)
    ending = lax.all_to_all(ending, MESH_AXES, 0, 0, tiled=True)
    with jax.named_scope("residual_end"):
        return pl.pallas_call(
            functools.partial(residual_end, peers),
            in_specs=whole_blocks(3),
            out_specs=pl.BlockSpec(memory_space=pltpu.VMEM),
            out_shape=jax.ShapeDtypeStruct(start_states.shape, jnp.float32),
            scratch_shapes=[pltpu.VMEM((components * (axial_rows // 2), columns, 128), jnp.float32)],
            compiler_params=params,
        )(ending, start_states, following)


def solution(mesh):
    peers = tuple(mesh.shape[name] for name in MESH_AXES)

    def body(start_states, radial_inverse, offsets, mode_count):
        if fits(start_states.shape, peers):
            return half_body(peers, start_states, radial_inverse, offsets, mode_count)
        return general_body(start_states, radial_inverse, offsets, mode_count)

    placed = (P("seg", None, "ax", "rad", None), P("ax", None, None), P("seg"), P())
    return jax.shard_map(
        body,
        mesh=mesh,
        in_specs=placed,
        out_specs=P("seg", None, "ax", "rad", None),
        check_vma=False,
    )
```

```python
import functools
import math

import jax
import jax.numpy as jnp
import ml_dtypes
import numpy as np
from jax import lax
from jax.experimental import pallas as pl
from jax.experimental.pallas import tpu as pltpu
from jax.sharding import PartitionSpec as P

STEPS = 2
MESH_AXES = ("seg", "rad", "ax")
UNROLL = [12, 2, 16, 2, 8, 4, 16, 6]
VMEM_LIMIT = 24 * 1024 * 1024
FLOPS = 40_000_000_000

highest = lax.Precision.HIGHEST


def passed_along(value, axis, steps):
    count = lax.axis_size(axis)
    pairs = [(source, (source + steps) % count) for source in range(count)]
    return lax.ppermute(value, axis, pairs)


def padded_2(array, sides, width):
    for axis, dim in sides:
        peers, length = (lax.axis_size(axis), array.shape[dim])
        up = [(i, (i + 1) % peers) for i in range(peers)]
        down = [(j, i) for i, j in up]
        last = lax.slice_in_dim(array, length - width, length, axis=dim)
        leading = lax.slice_in_dim(array, 0, width, axis=dim)
        before = lax.ppermute(last, axis, up)
        after = lax.ppermute(leading, axis, down)
        array = jnp.concatenate([before, array, after], axis=dim)
    return array


def fourier_tables(columns, kept_modes):
    modes_total = columns // 2
    row_index = lax.broadcasted_iota(jnp.int32, (columns, columns), 0)
    point_index = lax.broadcasted_iota(jnp.int32, (columns, columns), 1)
    mode_index = row_index // 2
    phase = (mode_index * point_index % columns).astype(jnp.float32) * (2.0 * math.pi / columns)
    even_rows = row_index % 2 == 0
    cosine = jnp.cos(phase)
    sine = jnp.sin(phase)
    root = math.sqrt(modes_total)
    synthesis = jnp.where(even_rows, cosine, sine) / root
    weights = jnp.where(mode_index == 0, 1.0, 2.0)
    analysis = jnp.where(even_rows, weights * cosine, 2.0 * sine) * (root / columns)
    analysis = jnp.where(mode_index < kept_modes, analysis, 0.0)
    return (synthesis, analysis)


def radial_solve(pencils, radial_inverse, radial_rows):
    local_modes = radial_inverse.shape[0]
    local_columns, members, axial_cells, ignored = pencils.shape
    own_rows = lax.dynamic_slice_in_dim(
        radial_inverse, lax.axis_index("rad") * radial_rows, radial_rows, 1
    )
    piece = lax.all_gather(pencils, "rad", axis=3, tiled=True)
    piece_rows = piece.shape[3]
    grouped = piece.reshape(local_modes, 2, members, axial_cells, piece_rows)
    product = jnp.einsum("mrs,mkqzs->mkqzr", own_rows, grouped, precision=highest)
    return product.reshape(local_columns, members, axial_cells, radial_rows)


def general_body(start_states, radial_inverse, offsets, mode_count):
    groups, components, axial_rows, radial_rows, columns = start_states.shape
    synthesis, analysis = fourier_tables(columns, mode_count[0])
    radius = (
        (lax.axis_index("rad") * radial_rows + jnp.arange(radial_rows)).astype(jnp.float32) + 0.5
    ) / (radial_rows * lax.axis_size("rad"))
    profile = (1.0 - radius * radius).reshape(1, 1, 1, radial_rows, 1)
    following = passed_along(start_states[0], "seg", -1)
    current = start_states
    for step_index in range(STEPS):
        if step_index == 0:
            physical = jnp.einsum("gczrj,jp->gczrp", current, synthesis, precision=highest)
        else:
            physical = jnp.einsum("jgczr,jp->gczrp", current, synthesis, precision=highest)
        padded = padded_2(physical, (("ax", 2),), 1)
        gradient = (padded[:, :, 2:] - padded[:, :, :-2]) * 20.0
        advecting = profile + padded[:, 2:3, 1:-1]
        forcing = physical - 0.02 * advecting * gradient
        spectral = jnp.einsum("gczrp,jp->jgczr", forcing, analysis, precision=highest)
        pencils = lax.all_to_all(spectral, "ax", split_axis=0, concat_axis=3, tiled=True)
        local_columns = pencils.shape[0]
        axial_cells = pencils.shape[3]
        pencils = pencils.reshape(local_columns, groups * components, axial_cells, radial_rows)
        solved = radial_solve(pencils, radial_inverse, radial_rows)
        if step_index == STEPS - 1:
            blocks = solved.reshape(local_columns, groups, components, axial_cells, radial_rows)
            shifted = [
                jnp.roll(blocks[:, member], offsets[member], axis=2) for member in range(groups)
            ]
            solved = jnp.stack(shifted, axis=1).reshape(
                local_columns, groups * components, axial_cells, radial_rows
            )
        returned = lax.all_to_all(solved, "ax", split_axis=2, concat_axis=0, tiled=True)
        current = returned.reshape(columns, groups, components, axial_rows, radial_rows)
    ending = jnp.transpose(current, (1, 2, 3, 4, 0))
    upcoming = jnp.concatenate([start_states[1:], following[None]], axis=0)
    return ending - upcoming


def halves(high):
    top = high.astype(jnp.bfloat16)
    return top, (high - top.astype(jnp.float32)).astype(jnp.bfloat16)


def product(left, right, contract):
    return lax.dot_general(
        left, right, ((contract[:1], contract[1:]), ((), ())), preferred_element_type=jnp.float32
    )


def stacked_table(table):
    top = table.astype(ml_dtypes.bfloat16)
    rest = (table - top.astype(np.float64)).astype(ml_dtypes.bfloat16)
    return np.concatenate([top, top, rest], axis=1)


def column_order(columns, quarter_modes, shares):
    each = quarter_modes // shares
    order = []
    for share in range(shares):
        for low in range(2):
            for high in range(2):
                first = (2 * high + low) * quarter_modes + share * each
                order.extend(range(2 * first, 2 * (first + each)))
    assert sorted(order) == list(range(columns))
    return np.array(order)


def tables(columns, order):
    modes_total = columns // 2
    rows = np.arange(columns)
    mode = rows // 2
    phase = (mode[:, None] * np.arange(columns)[None, :]) % columns * (2.0 * np.pi / columns)
    even = (rows % 2 == 0)[:, None]
    root = math.sqrt(modes_total)
    synthesis = np.where(even, np.cos(phase), np.sin(phase)) / root
    weights = np.where(mode == 0, 1.0, 2.0)[:, None]
    analysis = np.where(even, weights * np.cos(phase), 2.0 * np.sin(phase)) * (root / columns)
    return (
        np.ascontiguousarray(stacked_table(synthesis.T).T),
        stacked_table(np.ascontiguousarray(synthesis.T[:, order])),
        stacked_table(analysis[order]),
        mode[order].astype(np.int32),
    )


def lane_index(block):
    return lax.broadcasted_iota(jnp.int32, block.shape, 1)


def spread(tiles, fourth):
    lane = lane_index(fourth)
    return [
        jnp.where(lane < 96, block, pltpu.roll(fourth, 96 - 32 * index, 1))
        for index, block in enumerate(tiles)
    ]


def gathered(waves):
    lane = lane_index(waves[0])
    fourth = jnp.where(lane < 32, pltpu.roll(waves[0], 32, 1), pltpu.roll(waves[1], 64, 1))
    return waves + [jnp.where(lane < 64, fourth, pltpu.roll(waves[2], 96, 1))]


def every(blocks, first, step):
    return jnp.concatenate(blocks[first::step], axis=0)


def pieces(block):
    return [block[at : at + 8] for at in range(0, block.shape[0], 8)]


def spread_list(blocks):
    whole = len(blocks) // 4 * 4
    quarters = [every(blocks[:whole], first, 4) for first in range(4)]
    full = [pieces(block) for block in spread(quarters[:3], quarters[3])]
    return [block for group in zip(*full) for block in group] + blocks[whole:]


def gathered_list(full, count):
    whole = count // 4 * 3
    blocks = [pieces(block) for block in gathered([every(full[:whole], i, 3) for i in range(3)])]
    return [block for group in zip(*blocks) for block in group] + full[whole:]


def physical_to_spectral(physical, profile, analysis):
    lane = lane_index(physical[0])
    z = lane & 15
    forcing = []
    for tile in range(3):
        field = physical[tile]
        above = jnp.where(z < 15, pltpu.roll(field, 127, 1), pltpu.roll(field, 15, 1))
        below = jnp.where(z > 0, pltpu.roll(field, 1, 1), pltpu.roll(field, 113, 1))
        speed = jnp.where(lane < 32, pltpu.roll(field, 64, 1), pltpu.roll(field, 96, 1))
        speed = jnp.where(lane < 64, speed, field)
        speed = jnp.where(lane < 96, speed, physical[2])
        forcing.append(field - 0.4 * (profile[tile : tile + 1] + speed) * (above - below))
    forcing = jnp.concatenate(forcing, axis=1)
    top, rest = halves(forcing)
    return product(analysis, jnp.concatenate([top, rest, top], axis=0), (1, 0))


def write_spectral(spectral, count_ref, mode_ref, out_ref):
    members, ignored, width, ignored = out_ref.shape
    kept = mode_ref[...] < count_ref[0]
    for tile in range(3):
        block = jnp.where(kept, spectral[:, tile * 128 : (tile + 1) * 128], 0.0)
        out_ref[:, tile] = block.reshape(members, width, 128)


def synthesized(rows, synthesis):
    top, rest = halves(jnp.concatenate(rows, axis=0))
    return product(jnp.concatenate([top, rest, top], axis=1), synthesis, (1, 0))


def own_physical(own_ref, synthesis_ref, out_ref):
    groups, components, planes, radii, columns = own_ref.shape
    rows = own_ref[...].reshape(groups * components * planes * radii, columns)
    out_ref[...] = synthesized([rows], synthesis_ref[...]).reshape(out_ref.shape)


def first_phase_a(
    count_ref,
    before_ref,
    own_ref,
    after_ref,
    synthesis_ref,
    analysis_ref,
    mode_ref,
    profile_ref,
    out_ref,
    held_ref,
):
    groups, components, planes, radii, columns = own_ref.shape
    strips = columns // 128
    count = groups * components
    sides = [ref[...].reshape(count * radii, columns) for ref in (before_ref, after_ref)]
    sides = synthesized(sides, synthesis_ref[...]).reshape(2, groups, components, radii, columns)
    profile = jnp.concatenate([profile_ref[...]] * strips, axis=1)
    for segment in range(groups):
        for plane in range(planes):
            speed = 0.4 * (profile + own_ref[segment, 2, plane])
            for component in range(components):
                line = [own_ref[segment, component, i] for i in range(planes)]
                line = [sides[0, segment, component], *line, sides[1, segment, component]]
                forcing = line[plane + 1] - speed * (line[plane + 2] - line[plane])
                first = (component * groups + segment) * radii * planes
                at = pl.ds(first + plane, radii, stride=planes)
                for strip in range(strips):
                    held_ref[strip, at, :] = forcing[:, strip * 128 : (strip + 1) * 128]
    quad = 4 * planes
    lines = []
    for strip in range(strips):
        parts = []
        for tile in range(3):
            for four, members in ((tile, range(components)), (3, (tile,))):
                for component in members:
                    for at in range(four * quad, (four + 1) * quad, quad // 2):
                        for segment in range(groups):
                            row = (component * groups + segment) * radii * planes + at
                            parts.append(held_ref[strip, row : row + quad // 2, :])
        lines.append(jnp.concatenate(parts, axis=0))
    top, rest = halves(jnp.concatenate(lines, axis=1))
    spectral = product(analysis_ref[...], jnp.concatenate([top, rest, top], axis=1), (1, 1))
    write_spectral(spectral, count_ref, mode_ref, out_ref)


def later_phase_a(
    count_ref,
    wire_ref,
    synthesis_ref,
    analysis_ref,
    mode_ref,
    profile_ref,
    out_ref,
    held_ref,
    physical_ref,
):
    sources, tiles, ignored, ignored = wire_ref.shape
    halves_of_ax, pairs, ignored, ignored = held_ref.shape
    parts = out_ref.shape[2] // 8

    def unpack():
        @pl.loop(0, sources, unroll=UNROLL[5])
        def _(source):
            half = lax.rem(source, 4) // 2
            member = source // 4 * 2 + lax.rem(source, 2)
            blocks = gathered_list(pieces(wire_ref[source].reshape(tiles * 8, 128)), pairs * parts)
            for part in range(parts):
                at = pl.ds(pl.multiple_of((member * parts + part) * 8, 8), 8)
                for pair in range(pairs):
                    held_ref[half, pair, at, :] = blocks[part * pairs + pair]

    def begin(group):
        radii = []
        for pair in range(2):
            one, two = (held_ref[half, 2 * group + pair] for half in range(halves_of_ax))
            low = lane_index(one) & 8 == 0
            radii.append(jnp.where(low, one, pltpu.roll(two, 8, 1)))
            radii.append(jnp.where(low, pltpu.roll(one, 120, 1), two))
        top, rest = halves(jnp.concatenate(spread(radii[:3], radii[3]), axis=1))
        physical_ref[group % 2] = product(
            synthesis_ref[...], jnp.concatenate([top, rest, top], axis=0), (1, 0)
        )

    def finish(group):
        physical = [physical_ref[group % 2, :, tile * 128 : (tile + 1) * 128] for tile in range(3)]
        spectral = physical_to_spectral(physical, profile_ref[group], analysis_ref[...])
        write_spectral(spectral, count_ref, mode_ref, out_ref)

    for step in range(pairs // 2 + 1):

        @pl.when(pl.program_id(0) == step)
        def _(step=step):
            if step == 0:
                unpack()
            if step < pairs // 2:
                begin(step)
            if step > 0:
                finish(step - 1)


def unpack_quads(wire_ref, held_ref, peers):
    members, tiles, width, ignored = wire_ref.shape
    seg_places, rad_places, ignored = peers
    lane = lax.broadcasted_iota(jnp.int32, (4 * width, 128), 1)
    sixteen, four = lane & 16 == 0, lane & 4 == 0

    def swapped(mask, step, left, right):
        return (
            jnp.where(mask, left, pltpu.roll(right, step, 1)),
            jnp.where(mask, pltpu.roll(left, 128 - step, 1), right),
        )

    groups = tiles // 3

    @pl.loop(0, rad_places * groups, unroll=UNROLL[1])
    def _(index):
        rad, group = index // groups, lax.rem(index, groups)
        sources = [(s * rad_places + rad) * 2 + l for s in range(seg_places) for l in range(2)]
        waves = [
            jnp.concatenate([wire_ref[source, 3 * group + tile] for source in sources], axis=0)
            for tile in range(3)
        ]
        quads = gathered(waves)
        one, two, three, last = (
            jnp.concatenate([quad[at : at + width] for quad in quads], axis=0)
            for at in range(0, 4 * width, width)
        )
        one, three = swapped(sixteen, 16, one, three)
        two, last = swapped(sixteen, 16, two, last)
        radii = swapped(four, 4, one, two) + swapped(four, 4, three, last)
        for place, block in enumerate(radii):
            for quad in range(4):
                at = pl.multiple_of((index * 16 + 4 * quad + place) * width, 8)
                held_ref[pl.ds(at, width), :] = block[quad * width : (quad + 1) * width]


def first_radius(member, own):
    rad = lax.rem(member // 2, 4)
    return ((rad * 2 + member // 8) * 2 + lax.rem(member, 2)) * own


def unpack_radii(wire_ref, held_ref):
    members, tiles, width, ignored = wire_ref.shape
    own = tiles * 4 // 3

    @pl.loop(0, members, unroll=UNROLL[2])
    def _(member):
        first = first_radius(member, own)
        waves = [
            jnp.concatenate([wire_ref[member, at] for at in range(tile, tiles, 3)], axis=0)
            for tile in range(3)
        ]
        for index, block in enumerate(gathered(waves)):
            for group in range(tiles // 3):
                at = pl.multiple_of((first + 4 * group + index) * width, 8)
                held_ref[pl.ds(at, width), :] = block[group * width : (group + 1) * width]


def pack_sent(
    place_ref, offset_ref, inverse_ref, start_ref, out_ref, first_ref, held_ref, start_held_ref, sems
):
    each, radii, ignored = held_ref.shape
    copy = pltpu.make_async_copy(
        inverse_ref.at[pl.ds(place_ref[0] * each, each)], held_ref, sems.at[0]
    )
    copy.start()
    first = pltpu.make_async_copy(start_ref.at[0], start_held_ref, sems.at[1])
    first.start()
    rows = first_ref.shape[0] - 8
    for index in range(8):
        offset = offset_ref[index % offset_ref.shape[0]].astype(jnp.float32)
        first_ref[rows + index : rows + index + 1, :] = jnp.full((1, first_ref.shape[1]), offset)
    copy.wait()
    for index in range(each):
        out_ref[index] = held_ref[index, :, :128]
    for index in range(each // 2):
        out_ref[each + index, :, :64] = held_ref[index, :, 128:]
        out_ref[each + index, :, 64:] = held_ref[each // 2 + index, :, 128:]
    first.wait()
    first_ref[0:rows, :] = start_held_ref[...].reshape(rows, first_ref.shape[1])


def ordered_inverse(place_ref, own_ref, other_ref, top_ref, rest_ref):
    each = top_ref.shape[0] // 2
    first_half = place_ref[1] == 0

    def matrix(ref, index):
        side = index // (each // 2) * 64
        tail = ref[each + index % (each // 2), :, side : side + 64]
        return jnp.concatenate([ref[index], tail], axis=1)

    for index in range(each):
        here, there = matrix(own_ref, index), matrix(other_ref, index)
        top_ref[index], rest_ref[index] = halves(jnp.where(first_half, here, there))
        top_ref[each + index], rest_ref[each + index] = halves(jnp.where(first_half, there, here))


def inverse_copies(top_hbm, rest_hbm, top_ref, rest_ref, sems):
    copies = [
        pltpu.make_async_copy(source, target, sems.at[index])
        for index, (source, target) in enumerate(((top_hbm, top_ref), (rest_hbm, rest_ref)))
    ]
    for copy in copies:
        copy.start()
    return copies


def solved_modes(top_ref, rest_ref, held_ref, transposed, store):
    modes, radii, ignored = top_ref.shape
    width = 2 * modes

    @pl.loop(0, modes, unroll=UNROLL[0])
    def _(mode):
        matrix_top, matrix_rest = top_ref[mode], rest_ref[mode]
        state = jnp.concatenate(
            [held_ref[pl.ds(2 * mode + part, radii, stride=width), :] for part in range(2)], axis=1
        )
        if transposed:
            matrix_top, matrix_rest = (
                jnp.concatenate([m[:96], m[:32], m[96:], m[:32]], axis=0)
                for m in (matrix_top, matrix_rest)
            )
            top, rest = halves(state.T)
            solved = product(top, matrix_top, (1, 1))
            solved += product(rest, matrix_top, (1, 1)) + product(top, matrix_rest, (1, 1))
        else:
            top, rest = halves(state)
            solved = product(matrix_top, top, (1, 0))
            solved += product(matrix_top, rest, (1, 0)) + product(matrix_rest, top, (1, 0))
        store(mode, solved)


def phase_b(
    peers, top_hbm, rest_hbm, wire_ref, out_ref, held_ref, solved_ref, top_ref, rest_ref, sems
):
    members, tiles, width, ignored = wire_ref.shape
    radii = top_ref.shape[1]
    ax_places = peers[2]
    copies = inverse_copies(top_hbm, rest_hbm, top_ref, rest_ref, sems)
    unpack_quads(wire_ref, held_ref, peers)
    for copy in copies:
        copy.wait()

    def store(mode, solved):
        for part in range(2):
            solved_ref[pl.ds(2 * mode + part, radii, stride=width), :] = solved[
                :, part * 128 : (part + 1) * 128
            ]

    solved_modes(top_ref, rest_ref, held_ref, False, store)
    own = radii // members
    low = lax.broadcasted_iota(jnp.int32, (own * width // 2, 128), 1) & 8 == 0

    @pl.loop(0, members, unroll=UNROLL[3])
    def _(member):
        place = first_radius(member, own) * width
        for half in range(2):
            one, two = (
                jnp.concatenate(
                    [
                        solved_ref[pl.ds(pl.multiple_of(place + index * width, 8), width), :]
                        for index in range(first, own, 2)
                    ],
                    axis=0,
                )
                for first in range(2)
            )
            if half == 0:
                blocks = pieces(jnp.where(low, one, pltpu.roll(two, 8, 1)))
            else:
                blocks = pieces(jnp.where(low, pltpu.roll(one, 120, 1), two))
            parts = width // 8
            split = [block for part in range(parts) for block in blocks[part::parts]]
            target = member // 2 * ax_places + 2 * half + lax.rem(member, 2)
            for index, block in enumerate(spread_list(split)):
                out_ref[target, index] = block


def last_phase_b(
    peers,
    place_ref,
    own_offset_ref,
    other_offset_ref,
    top_hbm,
    rest_hbm,
    wire_ref,
    out_ref,
    held_ref,
    solved_ref,
    top_ref,
    rest_ref,
    sems,
):
    members, tiles, width, ignored = wire_ref.shape
    radii = top_ref.shape[1]
    seg_places, rad_places, ax_places = peers
    planes = 16 // ax_places
    each = radii // rad_places
    half = place_ref[1]
    rows = other_offset_ref.shape[0] - 8
    others = [jnp.max(other_offset_ref[rows + i : rows + i + 1, :128]) for i in range(2)]
    other_offset = jnp.where(half == 0, *others).astype(jnp.int32)
    copies = inverse_copies(top_hbm, rest_hbm, top_ref, rest_ref, sems)
    unpack_radii(wire_ref, held_ref)
    for copy in copies:
        copy.wait()

    def store(mode, solved):
        for part in range(2):
            rows = pl.ds(2 * mode + part, 96, stride=width)
            block = solved[part * 128 : part * 128 + 96]
            for strip in range(2):
                solved_ref[strip, rows, :] = block[:, strip * 128 : (strip + 1) * 128]

    solved_modes(top_ref, rest_ref, held_ref, True, store)
    lane = lax.broadcasted_iota(jnp.int32, (planes // 2 * width, 128), 1)


    @pl.loop(0, seg_places * ax_places, unroll=UNROLL[4])
    def _(index):
        seg, ax = index // ax_places, lax.rem(index, ax_places)
        offset = jnp.where(place_ref[2] == seg, own_offset_ref[half], other_offset)
        blocks = {}
        for component in range(3):
            for plane in range(planes):
                source = lax.rem(ax * planes + plane - offset + 16, 16)
                row = (component * 32 + seg * 16 + source) * width
                row = pl.multiple_of(row, 8)
                blocks[component, plane] = row
        for rad in range(rad_places):
            parts = width // 8
            slots = []
            for component in range(3):
                sides = []
                for side in range(2):
                    rows = [
                        pl.ds(blocks[component, plane], width) for plane in range(side, planes, 2)
                    ]
                    lines = [solved_ref[rad // 2, at, :] for at in rows]
                    sides.append(jnp.concatenate(lines, axis=0))
                if rad % 2 == 0:
                    sides[1] = pltpu.roll(sides[1], each, 1)
                else:
                    sides[0] = pltpu.roll(sides[0], 128 - each, 1)
                slots += pieces(jnp.where(lane < each, *sides))
            split = [block for part in range(parts) for block in slots[part::parts]]
            target = (seg * rad_places + rad) * ax_places + ax
            for at, block in enumerate(spread_list(split)):
                out_ref[target, at] = block


def residual_end(peers, wire_ref, start_ref, following_ref, out_ref, held_ref):
    seg_places, rad_places, ax_places = peers
    ignored, components, planes, each, columns = out_ref.shape
    shares = seg_places * rad_places
    width = columns // (2 * shares)
    chunk = width // 2
    count = (width // 8) * components * (planes // 2)
    slots = components * (planes // 2)
    half = pl.program_id(0)

    @pl.loop(0, 2 * shares, unroll=UNROLL[6])
    def _(member):
        share, low = member // 2, lax.rem(member, 2)
        source = share * ax_places + 2 * half + low
        split = gathered_list(pieces(wire_ref[source].reshape(-1, 128)), count)
        for slot in range(slots):
            parts = [split[part * slots + slot] for part in range(width // 8)]
            rows = jnp.concatenate(parts, axis=0)
            for high in range(2):
                at = (2 * high + low) * (columns // 4) + share * chunk
                held_ref[slot, pl.ds(at, chunk), :] = rows[high * chunk : (high + 1) * chunk]

    @pl.loop(0, slots, unroll=UNROLL[7])
    def _(slot):
        component, pair = slot // (planes // 2), lax.rem(slot, planes // 2)
        ending = held_ref[slot].T
        for side in range(2):
            plane = 2 * pair + side
            row = pl.multiple_of((component * planes + plane) * each, 8)
            upcoming = jnp.where(
                half + 1 < pl.num_programs(0),
                start_ref[0, component, plane],
                following_ref[pl.ds(row, each), :],
            )
            out_ref[0, component, plane] = ending[side * each : (side + 1) * each] - upcoming


def in_place(value):
    return pltpu.with_memory_space_constraint(value, pltpu.HBM)


def whole_blocks(count):
    return [pl.BlockSpec(memory_space=pltpu.VMEM)] * count


def fits(shape, peers):
    groups, components, axial_rows, radial_rows, columns = shape
    seg_places, rad_places, ax_places = peers
    members = seg_places * rad_places * 2
    return (
        (groups, components, seg_places, ax_places) == (2, 3, 2, 4)
        and axial_rows * ax_places == 16
        and radial_rows == 48
        and rad_places * radial_rows == 192
        and columns == 384
        and members == 16
    )


def half_body(peers, start_states, radial_inverse, offsets, mode_count):
    groups, components, axial_rows, radial_rows, columns = start_states.shape
    seg_places, rad_places, ax_places = peers
    axial = axial_rows * ax_places
    radii = radial_rows * rad_places
    shares = seg_places * rad_places
    members = 2 * shares
    own_radii = radii // members
    own_modes = radial_inverse.shape[0] // shares
    width = columns // members
    tiles = own_radii * 3 // 4
    order = column_order(columns, radial_inverse.shape[0], shares)
    synthesis_natural, synthesis, analysis, mode_of_row = tables(columns, order)

    seg, rad, ax = (lax.axis_index(name) for name in MESH_AXES)
    half, low = ax // 2, ax % 2

    def device(s, r, a):
        return (s * rad_places + r) * ax_places + a

    half_groups = [
        [
            device(s, r, 2 * h + l)
            for s in range(seg_places)
            for r in range(rad_places)
            for l in range(2)
        ]
        for h in range(2)
    ]
    mirror = [(a, (a + 2) % 4) for a in range(4)]
    params = pltpu.CompilerParams(vmem_limit_bytes=VMEM_LIMIT)
    up = [(i, (i + 1) % ax_places) for i in range(ax_places)]
    down = [(j, i) for i, j in up]
    before = lax.ppermute(start_states[:, :, axial_rows - 1], "ax", up)
    after = lax.ppermute(start_states[:, :, 0], "ax", down)

    share = seg * rad_places + rad
    place = jnp.stack([share, half, seg]).astype(jnp.int32)
    first_rows = components * axial_rows * radial_rows
    with jax.named_scope("pack_sent"):
        dense_inverse, first_start = pl.pallas_call(
            pack_sent,
            in_specs=[
                pl.BlockSpec(memory_space=pltpu.SMEM),
                pl.BlockSpec(memory_space=pltpu.SMEM),
                pl.BlockSpec(memory_space=pltpu.HBM),
                pl.BlockSpec(memory_space=pltpu.HBM),
            ],
            out_specs=whole_blocks(2),
            out_shape=[
                jax.ShapeDtypeStruct((own_modes * 3 // 2, radii, 128), jnp.float32),
                jax.ShapeDtypeStruct((first_rows + 8, columns), jnp.float32),
            ],
            scratch_shapes=[
                pltpu.VMEM((own_modes, radii, radii), jnp.float32),
                pltpu.VMEM(start_states.shape[1:], jnp.float32),
                pltpu.SemaphoreType.DMA((2,)),
            ],
            compiler_params=params,
        )(place, offsets, in_place(radial_inverse), in_place(start_states))
    first = rad * radial_rows + (seg * 2 + low) * own_radii
    tile_index = np.arange(tiles)[:, None]
    lane = np.arange(128)[None, :]
    local = 4 * (tile_index // 3) + np.where(lane < 96, tile_index % 3, 3)
    radius = ((first + jnp.asarray(local)).astype(jnp.float32) + 0.5) / radii
    profile = (1.0 - radius * radius).reshape(tiles // 3, 3, 128)

    own_radius = ((rad * radial_rows + jnp.arange(radial_rows)).astype(jnp.float32) + 0.5) / radii
    own_profile = jnp.broadcast_to((1.0 - own_radius * own_radius)[:, None], (radial_rows, 128))

    following = passed_along(first_start, "seg", -1)
    synthesis_natural, synthesis, analysis = (
        jnp.asarray(table) for table in (synthesis_natural, synthesis, analysis)
    )
    mode_rows = jnp.asarray(np.repeat(mode_of_row[:, None], 128, axis=1))
    wire = jax.ShapeDtypeStruct((members, tiles, width, 128), jnp.float32)
    wire_spec = pl.BlockSpec((members, 3, width, 128), lambda g: (0, g, 0, 0))
    held = pltpu.VMEM((radii * width, 128), jnp.float32)
    count = (width // 8) * components * (axial_rows // 2)
    end_tiles = (count // 4) * 3 + count % 4
    everyone = seg_places * rad_places * ax_places
    spread_wire = jax.ShapeDtypeStruct((everyone, end_tiles, 8, 128), jnp.float32)

    def exchanged(value):
        return lax.all_to_all(
            value, MESH_AXES, 0, 0, axis_index_groups=half_groups, tiled=True
        )

    step = radial_rows // 3
    halo_spec = pl.BlockSpec((groups, components, step, columns), lambda g: (0, 0, g, 0))
    own_spec = pl.BlockSpec(
        (groups, components, axial_rows, step, columns), lambda g: (0, 0, 0, g, 0)
    )
    with jax.named_scope("own_physical"):
        physical = pl.pallas_call(
            own_physical,
            grid=(3,),
            in_specs=[own_spec] + whole_blocks(1),
            out_specs=own_spec,
            out_shape=jax.ShapeDtypeStruct(start_states.shape, jnp.float32),
            compiler_params=params,
        )(start_states, synthesis_natural)
    before, after, dense_inverse, physical, profile, own_profile = lax.optimization_barrier(
        (before, after, dense_inverse, physical, profile, own_profile)
    )
    other_inverse = lax.ppermute(dense_inverse, "ax", mirror)
    with jax.named_scope("phase_a_first"):
        spectral = pl.pallas_call(
            first_phase_a,
            grid=(3,),
            in_specs=[
                pl.BlockSpec(memory_space=pltpu.SMEM),
                halo_spec,
                own_spec,
                halo_spec,
                *whole_blocks(3),
                pl.BlockSpec((step, 128), lambda g: (g, 0)),
            ],
            out_specs=wire_spec,
            out_shape=pltpu.HBM(wire.shape, wire.dtype),
            scratch_shapes=[
                pltpu.VMEM(
                    (columns // 128, groups * components * axial_rows * step, 128), jnp.float32
                )
            ],
            compiler_params=params,
        )(
            mode_count,
            before,
            physical,
            after,
            synthesis_natural,
            analysis,
            mode_rows,
            own_profile,
        )
    matrices = jax.ShapeDtypeStruct((2 * own_modes, radii, radii), jnp.bfloat16)
    in_hbm = [pl.BlockSpec(memory_space=pltpu.HBM)] * 2
    inverse_scratch = [pltpu.VMEM(matrices.shape, matrices.dtype)] * 2
    inverse_scratch += [pltpu.SemaphoreType.DMA((2,))]
    with jax.named_scope("ordered_inverse"):
        inverse = pl.pallas_call(
            ordered_inverse,
            in_specs=[pl.BlockSpec(memory_space=pltpu.SMEM)] + whole_blocks(2),
            out_specs=[pl.BlockSpec(matrices.shape, lambda: (0, 0, 0))] * 2,
            out_shape=[pltpu.HBM(matrices.shape, matrices.dtype)] * 2,
            compiler_params=params,
            cost_estimate=pl.CostEstimate(
                flops=FLOPS, bytes_accessed=16 * own_modes * radii * radii, transcendentals=0
            ),
        )(place, dense_inverse, other_inverse)
    lines = exchanged(spectral)
    with jax.named_scope("phase_b_first"):
        solved = pl.pallas_call(
            functools.partial(phase_b, peers),
            in_specs=in_hbm + whole_blocks(1),
            out_specs=pl.BlockSpec(memory_space=pltpu.VMEM),
            out_shape=spread_wire,
            scratch_shapes=[held, held] + inverse_scratch,
            compiler_params=params,
        )(*map(in_place, inverse), lines)
    solved, following = lax.optimization_barrier((solved, following))
    state = lax.all_to_all(solved, MESH_AXES, 0, 0, tiled=True)
    with jax.named_scope("phase_a_later"):
        spectral = pl.pallas_call(
            later_phase_a,
            grid=(tiles // 3 + 1,),
            in_specs=[
                pl.BlockSpec(memory_space=pltpu.SMEM),
                *whole_blocks(4),
                *whole_blocks(1),
            ],
            out_specs=pl.BlockSpec(
                wire_spec.block_shape, lambda g: (0, jnp.maximum(g - 1, 0), 0, 0)
            ),
            out_shape=wire,
            scratch_shapes=[
                pltpu.VMEM((2, own_radii // 2, columns, 128), jnp.float32),
                pltpu.VMEM((2, columns, 3 * 128), jnp.float32),
            ],
            compiler_params=params,
        )(mode_count, state, synthesis, analysis, mode_rows, profile)
    lines = exchanged(spectral)
    with jax.named_scope("phase_b_last"):
        ending = pl.pallas_call(
            functools.partial(last_phase_b, peers),
            in_specs=[pl.BlockSpec(memory_space=pltpu.SMEM)] * 2
            + whole_blocks(1)
            + in_hbm
            + whole_blocks(1),
            out_specs=pl.BlockSpec(memory_space=pltpu.VMEM),
            out_shape=spread_wire,
            scratch_shapes=[held, pltpu.VMEM((2, 96 * width, 128), jnp.float32)]
            + inverse_scratch,
            compiler_params=params,
        )(place, offsets, following, *map(in_place, inverse), lines)
    ending = lax.all_to_all(ending, MESH_AXES, 0, 0, tiled=True)
    with jax.named_scope("residual_end"):
        return pl.pallas_call(
            functools.partial(residual_end, peers),
            grid=(groups,),
            in_specs=[
                *whole_blocks(1),
                pl.BlockSpec((1,) + start_states.shape[1:], lambda b: (groups - 1, 0, 0, 0, 0)),
                *whole_blocks(1),
            ],
            out_specs=pl.BlockSpec((1,) + start_states.shape[1:], lambda b: (b, 0, 0, 0, 0)),
            out_shape=jax.ShapeDtypeStruct(start_states.shape, jnp.float32),
            scratch_shapes=[pltpu.VMEM((components * (axial_rows // 2), columns, 128), jnp.float32)],
            compiler_params=params,
        )(ending, start_states, following)


def solution(mesh):
    peers = tuple(mesh.shape[name] for name in MESH_AXES)

    def body(start_states, radial_inverse, offsets, mode_count):
        if fits(start_states.shape, peers):
            return half_body(peers, start_states, radial_inverse, offsets, mode_count)
        return general_body(start_states, radial_inverse, offsets, mode_count)

    placed = (P("seg", None, "ax", "rad", None), P("ax", None, None), P("seg"), P())
    return jax.shard_map(
        body,
        mesh=mesh,
        in_specs=placed,
        out_specs=P("seg", None, "ax", "rad", None),
        check_vma=False,
    )
```

```python
import functools
import math

import jax
import jax.numpy as jnp
import ml_dtypes
import numpy as np
from jax import lax
from jax.experimental import pallas as pl
from jax.experimental.pallas import tpu as pltpu
from jax.sharding import PartitionSpec as P

STEPS = 2
MESH_AXES = ("seg", "rad", "ax")
UNROLL = [12, 2, 16, 2, 8, 4, 16, 6]
VMEM_LIMIT = 24 * 1024 * 1024
FLOPS = 40_000_000_000

highest = lax.Precision.HIGHEST


def passed_along(value, axis, steps):
    count = lax.axis_size(axis)
    pairs = [(source, (source + steps) % count) for source in range(count)]
    return lax.ppermute(value, axis, pairs)


def padded_2(array, sides, width):
    for axis, dim in sides:
        peers, length = (lax.axis_size(axis), array.shape[dim])
        up = [(i, (i + 1) % peers) for i in range(peers)]
        down = [(j, i) for i, j in up]
        last = lax.slice_in_dim(array, length - width, length, axis=dim)
        leading = lax.slice_in_dim(array, 0, width, axis=dim)
        before = lax.ppermute(last, axis, up)
        after = lax.ppermute(leading, axis, down)
        array = jnp.concatenate([before, array, after], axis=dim)
    return array


def fourier_tables(columns, kept_modes):
    modes_total = columns // 2
    row_index = lax.broadcasted_iota(jnp.int32, (columns, columns), 0)
    point_index = lax.broadcasted_iota(jnp.int32, (columns, columns), 1)
    mode_index = row_index // 2
    phase = (mode_index * point_index % columns).astype(jnp.float32) * (2.0 * math.pi / columns)
    even_rows = row_index % 2 == 0
    cosine = jnp.cos(phase)
    sine = jnp.sin(phase)
    root = math.sqrt(modes_total)
    synthesis = jnp.where(even_rows, cosine, sine) / root
    weights = jnp.where(mode_index == 0, 1.0, 2.0)
    analysis = jnp.where(even_rows, weights * cosine, 2.0 * sine) * (root / columns)
    analysis = jnp.where(mode_index < kept_modes, analysis, 0.0)
    return (synthesis, analysis)


def radial_solve(pencils, radial_inverse, radial_rows):
    local_modes = radial_inverse.shape[0]
    local_columns, members, axial_cells, ignored = pencils.shape
    own_rows = lax.dynamic_slice_in_dim(
        radial_inverse, lax.axis_index("rad") * radial_rows, radial_rows, 1
    )
    piece = lax.all_gather(pencils, "rad", axis=3, tiled=True)
    piece_rows = piece.shape[3]
    grouped = piece.reshape(local_modes, 2, members, axial_cells, piece_rows)
    product = jnp.einsum("mrs,mkqzs->mkqzr", own_rows, grouped, precision=highest)
    return product.reshape(local_columns, members, axial_cells, radial_rows)


def general_body(start_states, radial_inverse, offsets, mode_count):
    groups, components, axial_rows, radial_rows, columns = start_states.shape
    synthesis, analysis = fourier_tables(columns, mode_count[0])
    radius = (
        (lax.axis_index("rad") * radial_rows + jnp.arange(radial_rows)).astype(jnp.float32) + 0.5
    ) / (radial_rows * lax.axis_size("rad"))
    profile = (1.0 - radius * radius).reshape(1, 1, 1, radial_rows, 1)
    following = passed_along(start_states[0], "seg", -1)
    current = start_states
    for step_index in range(STEPS):
        if step_index == 0:
            physical = jnp.einsum("gczrj,jp->gczrp", current, synthesis, precision=highest)
        else:
            physical = jnp.einsum("jgczr,jp->gczrp", current, synthesis, precision=highest)
        padded = padded_2(physical, (("ax", 2),), 1)
        gradient = (padded[:, :, 2:] - padded[:, :, :-2]) * 20.0
        advecting = profile + padded[:, 2:3, 1:-1]
        forcing = physical - 0.02 * advecting * gradient
        spectral = jnp.einsum("gczrp,jp->jgczr", forcing, analysis, precision=highest)
        pencils = lax.all_to_all(spectral, "ax", split_axis=0, concat_axis=3, tiled=True)
        local_columns = pencils.shape[0]
        axial_cells = pencils.shape[3]
        pencils = pencils.reshape(local_columns, groups * components, axial_cells, radial_rows)
        solved = radial_solve(pencils, radial_inverse, radial_rows)
        if step_index == STEPS - 1:
            blocks = solved.reshape(local_columns, groups, components, axial_cells, radial_rows)
            shifted = [
                jnp.roll(blocks[:, member], offsets[member], axis=2) for member in range(groups)
            ]
            solved = jnp.stack(shifted, axis=1).reshape(
                local_columns, groups * components, axial_cells, radial_rows
            )
        returned = lax.all_to_all(solved, "ax", split_axis=2, concat_axis=0, tiled=True)
        current = returned.reshape(columns, groups, components, axial_rows, radial_rows)
    ending = jnp.transpose(current, (1, 2, 3, 4, 0))
    upcoming = jnp.concatenate([start_states[1:], following[None]], axis=0)
    return ending - upcoming


def halves(high):
    top = high.astype(jnp.bfloat16)
    return top, (high - top.astype(jnp.float32)).astype(jnp.bfloat16)


def product(left, right, contract):
    return lax.dot_general(
        left, right, ((contract[:1], contract[1:]), ((), ())), preferred_element_type=jnp.float32
    )


def stacked_table(table):
    top = table.astype(ml_dtypes.bfloat16)
    rest = (table - top.astype(np.float64)).astype(ml_dtypes.bfloat16)
    return np.concatenate([top, top, rest], axis=1)


def column_order(columns, quarter_modes, shares):
    each = quarter_modes // shares
    order = []
    for share in range(shares):
        for low in range(2):
            for high in range(2):
                first = (2 * high + low) * quarter_modes + share * each
                order.extend(range(2 * first, 2 * (first + each)))
    assert sorted(order) == list(range(columns))
    return np.array(order)


def tables(columns, order):
    modes_total = columns // 2
    rows = np.arange(columns)
    mode = rows // 2
    phase = (mode[:, None] * np.arange(columns)[None, :]) % columns * (2.0 * np.pi / columns)
    even = (rows % 2 == 0)[:, None]
    root = math.sqrt(modes_total)
    synthesis = np.where(even, np.cos(phase), np.sin(phase)) / root
    weights = np.where(mode == 0, 1.0, 2.0)[:, None]
    analysis = np.where(even, weights * np.cos(phase), 2.0 * np.sin(phase)) * (root / columns)
    return (
        np.ascontiguousarray(stacked_table(synthesis.T).T),
        stacked_table(np.ascontiguousarray(synthesis.T[:, order])),
        stacked_table(analysis[order]),
        mode[order].astype(np.int32),
    )


def lane_index(block):
    return lax.broadcasted_iota(jnp.int32, block.shape, 1)


def spread(tiles, fourth):
    lane = lane_index(fourth)
    return [
        jnp.where(lane < 96, block, pltpu.roll(fourth, 96 - 32 * index, 1))
        for index, block in enumerate(tiles)
    ]


def gathered(waves):
    lane = lane_index(waves[0])
    fourth = jnp.where(lane < 32, pltpu.roll(waves[0], 32, 1), pltpu.roll(waves[1], 64, 1))
    return waves + [jnp.where(lane < 64, fourth, pltpu.roll(waves[2], 96, 1))]


def every(blocks, first, step):
    return jnp.concatenate(blocks[first::step], axis=0)


def pieces(block):
    return [block[at : at + 8] for at in range(0, block.shape[0], 8)]


def spread_list(blocks):
    whole = len(blocks) // 4 * 4
    quarters = [every(blocks[:whole], first, 4) for first in range(4)]
    full = [pieces(block) for block in spread(quarters[:3], quarters[3])]
    return [block for group in zip(*full) for block in group] + blocks[whole:]


def gathered_list(full, count):
    whole = count // 4 * 3
    blocks = [pieces(block) for block in gathered([every(full[:whole], i, 3) for i in range(3)])]
    return [block for group in zip(*blocks) for block in group] + full[whole:]


def lane_moves():
    lane = np.arange(128)
    moves = np.zeros((128, 256), np.float32)
    above = lane // 16 * 16 + (lane + 1) % 16
    below = lane // 16 * 16 + (lane + 15) % 16
    np.add.at(moves, (above, lane), 1.0)
    np.add.at(moves, (below, lane), -1.0)
    whole = lane[:96]
    moves[64 + whole % 32, 128 + whole] = 1.0
    return np.concatenate([moves, moves], axis=0).astype(ml_dtypes.bfloat16)


def physical_to_spectral(physical, profile, analysis, moves):
    lane = lane_index(physical[0])
    forcing = []
    for tile in range(3):
        field = physical[tile]
        moved = product(jnp.concatenate(halves(field), axis=1), moves, (1, 0))
        speed = jnp.where(lane < 96, moved[:, 128:], physical[2])
        forcing.append(field - 0.4 * (profile[tile : tile + 1] + speed) * moved[:, :128])
    forcing = jnp.concatenate(forcing, axis=1)
    top, rest = halves(forcing)
    return product(analysis, jnp.concatenate([top, rest, top], axis=0), (1, 0))


def write_spectral(spectral, count_ref, mode_ref, out_ref):
    members, ignored, width, ignored = out_ref.shape
    kept = mode_ref[...] < count_ref[0]
    for tile in range(3):
        block = jnp.where(kept, spectral[:, tile * 128 : (tile + 1) * 128], 0.0)
        out_ref[:, tile] = block.reshape(members, width, 128)


def pack_halos(start_ref, last_ref, leading_ref, sems):
    planes = start_ref.shape[2]
    copies = [
        pltpu.make_async_copy(start_ref.at[:, :, planes - 1], last_ref, sems.at[0]),
        pltpu.make_async_copy(start_ref.at[:, :, 0], leading_ref, sems.at[1]),
    ]
    for copy in copies:
        copy.start()
    for copy in copies:
        copy.wait()


def synthesized(rows, synthesis):
    top, rest = halves(jnp.concatenate(rows, axis=0))
    return product(jnp.concatenate([top, rest, top], axis=1), synthesis, (1, 0))


def own_physical(own_ref, synthesis_ref, out_ref):
    groups, components, planes, radii, columns = own_ref.shape
    rows = own_ref[...].reshape(groups * components * planes * radii, columns)
    out_ref[...] = synthesized([rows], synthesis_ref[...]).reshape(out_ref.shape)


def first_phase_a(
    count_ref,
    before_ref,
    own_ref,
    after_ref,
    synthesis_ref,
    analysis_ref,
    mode_ref,
    profile_ref,
    out_ref,
    held_ref,
):
    groups, components, planes, radii, columns = own_ref.shape
    strips = columns // 128
    count = groups * components
    sides = [ref[...].reshape(count * radii, columns) for ref in (before_ref, after_ref)]
    sides = synthesized(sides, synthesis_ref[...]).reshape(2, groups, components, radii, columns)
    profile = jnp.concatenate([profile_ref[...]] * strips, axis=1)
    for segment in range(groups):
        for plane in range(planes):
            speed = 0.4 * (profile + own_ref[segment, 2, plane])
            for component in range(components):
                line = [own_ref[segment, component, i] for i in range(planes)]
                line = [sides[0, segment, component], *line, sides[1, segment, component]]
                forcing = line[plane + 1] - speed * (line[plane + 2] - line[plane])
                first = (component * groups + segment) * radii * planes
                at = pl.ds(first + plane, radii, stride=planes)
                for strip in range(strips):
                    held_ref[strip, at, :] = forcing[:, strip * 128 : (strip + 1) * 128]
    quad = 4 * planes
    lines = []
    for strip in range(strips):
        parts = []
        for tile in range(3):
            for four, members in ((tile, range(components)), (3, (tile,))):
                for component in members:
                    for at in range(four * quad, (four + 1) * quad, quad // 2):
                        for segment in range(groups):
                            row = (component * groups + segment) * radii * planes + at
                            parts.append(held_ref[strip, row : row + quad // 2, :])
        lines.append(jnp.concatenate(parts, axis=0))
    top, rest = halves(jnp.concatenate(lines, axis=1))
    spectral = product(analysis_ref[...], jnp.concatenate([top, rest, top], axis=1), (1, 1))
    write_spectral(spectral, count_ref, mode_ref, out_ref)


def later_phase_a(
    count_ref,
    wire_ref,
    synthesis_ref,
    analysis_ref,
    mode_ref,
    profile_ref,
    moves_ref,
    out_ref,
    held_ref,
    physical_ref,
):
    sources, tiles, ignored, ignored = wire_ref.shape
    halves_of_ax, pairs, ignored, ignored = held_ref.shape
    parts = out_ref.shape[2] // 8

    def unpack():
        @pl.loop(0, sources, unroll=UNROLL[5])
        def _(source):
            half = lax.rem(source, 4) // 2
            member = source // 4 * 2 + lax.rem(source, 2)
            blocks = gathered_list(pieces(wire_ref[source].reshape(tiles * 8, 128)), pairs * parts)
            for part in range(parts):
                at = pl.ds(pl.multiple_of((member * parts + part) * 8, 8), 8)
                for pair in range(pairs):
                    held_ref[half, pair, at, :] = blocks[part * pairs + pair]

    def begin(group):
        radii = []
        for pair in range(2):
            one, two = (held_ref[half, 2 * group + pair] for half in range(halves_of_ax))
            low = lane_index(one) & 8 == 0
            radii.append(jnp.where(low, one, pltpu.roll(two, 8, 1)))
            radii.append(jnp.where(low, pltpu.roll(one, 120, 1), two))
        top, rest = halves(jnp.concatenate(spread(radii[:3], radii[3]), axis=1))
        physical_ref[group % 2] = product(
            synthesis_ref[...], jnp.concatenate([top, rest, top], axis=0), (1, 0)
        )

    def finish(group):
        physical = [physical_ref[group % 2, :, tile * 128 : (tile + 1) * 128] for tile in range(3)]
        spectral = physical_to_spectral(
            physical, profile_ref[group], analysis_ref[...], moves_ref[...]
        )
        write_spectral(spectral, count_ref, mode_ref, out_ref)

    for step in range(pairs // 2 + 1):

        @pl.when(pl.program_id(0) == step)
        def _(step=step):
            if step == 0:
                unpack()
            if step < pairs // 2:
                begin(step)
            if step > 0:
                finish(step - 1)


def unpack_quads(wire_ref, held_ref, peers):
    members, tiles, width, ignored = wire_ref.shape
    seg_places, rad_places, ignored = peers
    lane = lax.broadcasted_iota(jnp.int32, (4 * width, 128), 1)
    sixteen, four = lane & 16 == 0, lane & 4 == 0

    def swapped(mask, step, left, right):
        return (
            jnp.where(mask, left, pltpu.roll(right, step, 1)),
            jnp.where(mask, pltpu.roll(left, 128 - step, 1), right),
        )

    groups = tiles // 3

    @pl.loop(0, rad_places * groups, unroll=UNROLL[1])
    def _(index):
        rad, group = index // groups, lax.rem(index, groups)
        sources = [(s * rad_places + rad) * 2 + l for s in range(seg_places) for l in range(2)]
        waves = [
            jnp.concatenate([wire_ref[source, 3 * group + tile] for source in sources], axis=0)
            for tile in range(3)
        ]
        quads = gathered(waves)
        one, two, three, last = (
            jnp.concatenate([quad[at : at + width] for quad in quads], axis=0)
            for at in range(0, 4 * width, width)
        )
        one, three = swapped(sixteen, 16, one, three)
        two, last = swapped(sixteen, 16, two, last)
        radii = swapped(four, 4, one, two) + swapped(four, 4, three, last)
        for place, block in enumerate(radii):
            for quad in range(4):
                at = pl.multiple_of((index * 16 + 4 * quad + place) * width, 8)
                held_ref[pl.ds(at, width), :] = block[quad * width : (quad + 1) * width]


def first_radius(member, own):
    rad = lax.rem(member // 2, 4)
    return ((rad * 2 + member // 8) * 2 + lax.rem(member, 2)) * own


def unpack_radii(wire_ref, held_ref):
    members, tiles, width, ignored = wire_ref.shape
    own = tiles * 4 // 3

    @pl.loop(0, members, unroll=UNROLL[2])
    def _(member):
        first = first_radius(member, own)
        waves = [
            jnp.concatenate([wire_ref[member, at] for at in range(tile, tiles, 3)], axis=0)
            for tile in range(3)
        ]
        for index, block in enumerate(gathered(waves)):
            for group in range(tiles // 3):
                at = pl.multiple_of((first + 4 * group + index) * width, 8)
                held_ref[pl.ds(at, width), :] = block[group * width : (group + 1) * width]


def pack_sent(
    place_ref, offset_ref, inverse_ref, start_ref, out_ref, first_ref, held_ref, start_held_ref, sems
):
    each, radii, ignored = held_ref.shape
    copy = pltpu.make_async_copy(
        inverse_ref.at[pl.ds(place_ref[0] * each, each)], held_ref, sems.at[0]
    )
    copy.start()
    first = pltpu.make_async_copy(start_ref.at[0], start_held_ref, sems.at[1])
    first.start()
    rows = first_ref.shape[0] - 8
    for index in range(8):
        offset = offset_ref[index % offset_ref.shape[0]].astype(jnp.float32)
        first_ref[rows + index : rows + index + 1, :] = jnp.full((1, first_ref.shape[1]), offset)
    copy.wait()
    for index in range(each):
        out_ref[index] = held_ref[index, :, :128]
    for index in range(each // 2):
        out_ref[each + index, :, :64] = held_ref[index, :, 128:]
        out_ref[each + index, :, 64:] = held_ref[each // 2 + index, :, 128:]
    first.wait()
    first_ref[0:rows, :] = start_held_ref[...].reshape(rows, first_ref.shape[1])


def ordered_inverse(place_ref, own_ref, other_ref, top_ref, rest_ref):
    each = top_ref.shape[0] // 2
    first_half = place_ref[1] == 0

    def matrix(ref, index):
        side = index // (each // 2) * 64
        tail = ref[each + index % (each // 2), :, side : side + 64]
        return jnp.concatenate([ref[index], tail], axis=1)

    for index in range(each):
        here, there = matrix(own_ref, index), matrix(other_ref, index)
        top_ref[index], rest_ref[index] = halves(jnp.where(first_half, here, there))
        top_ref[each + index], rest_ref[each + index] = halves(jnp.where(first_half, there, here))


def inverse_copies(top_hbm, rest_hbm, top_ref, rest_ref, sems):
    copies = [
        pltpu.make_async_copy(source, target, sems.at[index])
        for index, (source, target) in enumerate(((top_hbm, top_ref), (rest_hbm, rest_ref)))
    ]
    for copy in copies:
        copy.start()
    return copies


def solved_modes(top_ref, rest_ref, held_ref, transposed, store):
    modes, radii, ignored = top_ref.shape
    width = 2 * modes

    @pl.loop(0, modes, unroll=UNROLL[0])
    def _(mode):
        matrix_top, matrix_rest = top_ref[mode], rest_ref[mode]
        state = jnp.concatenate(
            [held_ref[pl.ds(2 * mode + part, radii, stride=width), :] for part in range(2)], axis=1
        )
        if transposed:
            matrix_top, matrix_rest = (
                jnp.concatenate([m[:96], m[:32], m[96:], m[:32]], axis=0)
                for m in (matrix_top, matrix_rest)
            )
            top, rest = halves(state.T)
            solved = product(top, matrix_top, (1, 1))
            solved += product(rest, matrix_top, (1, 1)) + product(top, matrix_rest, (1, 1))
        else:
            top, rest = halves(state)
            solved = product(matrix_top, top, (1, 0))
            solved += product(matrix_top, rest, (1, 0)) + product(matrix_rest, top, (1, 0))
        store(mode, solved)


def phase_b(
    peers, top_hbm, rest_hbm, wire_ref, out_ref, held_ref, solved_ref, top_ref, rest_ref, sems
):
    members, tiles, width, ignored = wire_ref.shape
    radii = top_ref.shape[1]
    ax_places = peers[2]
    copies = inverse_copies(top_hbm, rest_hbm, top_ref, rest_ref, sems)
    unpack_quads(wire_ref, held_ref, peers)
    for copy in copies:
        copy.wait()

    def store(mode, solved):
        for part in range(2):
            solved_ref[pl.ds(2 * mode + part, radii, stride=width), :] = solved[
                :, part * 128 : (part + 1) * 128
            ]

    solved_modes(top_ref, rest_ref, held_ref, False, store)
    own = radii // members
    low = lax.broadcasted_iota(jnp.int32, (own * width // 2, 128), 1) & 8 == 0

    @pl.loop(0, members, unroll=UNROLL[3])
    def _(member):
        place = first_radius(member, own) * width
        for half in range(2):
            one, two = (
                jnp.concatenate(
                    [
                        solved_ref[pl.ds(pl.multiple_of(place + index * width, 8), width), :]
                        for index in range(first, own, 2)
                    ],
                    axis=0,
                )
                for first in range(2)
            )
            if half == 0:
                blocks = pieces(jnp.where(low, one, pltpu.roll(two, 8, 1)))
            else:
                blocks = pieces(jnp.where(low, pltpu.roll(one, 120, 1), two))
            parts = width // 8
            split = [block for part in range(parts) for block in blocks[part::parts]]
            target = member // 2 * ax_places + 2 * half + lax.rem(member, 2)
            for index, block in enumerate(spread_list(split)):
                out_ref[target, index] = block


def last_phase_b(
    peers,
    place_ref,
    own_offset_ref,
    other_offset_ref,
    top_hbm,
    rest_hbm,
    wire_ref,
    out_ref,
    held_ref,
    solved_ref,
    top_ref,
    rest_ref,
    sems,
):
    members, tiles, width, ignored = wire_ref.shape
    radii = top_ref.shape[1]
    seg_places, rad_places, ax_places = peers
    planes = 16 // ax_places
    each = radii // rad_places
    half = place_ref[1]
    rows = other_offset_ref.shape[0] - 8
    others = [jnp.max(other_offset_ref[rows + i : rows + i + 1, :128]) for i in range(2)]
    other_offset = jnp.where(half == 0, *others).astype(jnp.int32)
    copies = inverse_copies(top_hbm, rest_hbm, top_ref, rest_ref, sems)
    unpack_radii(wire_ref, held_ref)
    for copy in copies:
        copy.wait()

    def store(mode, solved):
        for part in range(2):
            rows = pl.ds(2 * mode + part, 96, stride=width)
            block = solved[part * 128 : part * 128 + 96]
            for strip in range(2):
                solved_ref[strip, rows, :] = block[:, strip * 128 : (strip + 1) * 128]

    solved_modes(top_ref, rest_ref, held_ref, True, store)
    lane = lax.broadcasted_iota(jnp.int32, (planes // 2 * width, 128), 1)


    @pl.loop(0, seg_places * ax_places, unroll=UNROLL[4])
    def _(index):
        seg, ax = index // ax_places, lax.rem(index, ax_places)
        offset = jnp.where(place_ref[2] == seg, own_offset_ref[half], other_offset)
        blocks = {}
        for component in range(3):
            for plane in range(planes):
                source = lax.rem(ax * planes + plane - offset + 16, 16)
                row = (component * 32 + seg * 16 + source) * width
                row = pl.multiple_of(row, 8)
                blocks[component, plane] = row
        for rad in range(rad_places):
            parts = width // 8
            slots = []
            for component in range(3):
                sides = []
                for side in range(2):
                    rows = [
                        pl.ds(blocks[component, plane], width) for plane in range(side, planes, 2)
                    ]
                    lines = [solved_ref[rad // 2, at, :] for at in rows]
                    sides.append(jnp.concatenate(lines, axis=0))
                if rad % 2 == 0:
                    sides[1] = pltpu.roll(sides[1], each, 1)
                else:
                    sides[0] = pltpu.roll(sides[0], 128 - each, 1)
                slots += pieces(jnp.where(lane < each, *sides))
            split = [block for part in range(parts) for block in slots[part::parts]]
            target = (seg * rad_places + rad) * ax_places + ax
            for at, block in enumerate(spread_list(split)):
                out_ref[target, at] = block


def residual_end(peers, wire_ref, start_ref, following_ref, out_ref, held_ref):
    seg_places, rad_places, ax_places = peers
    ignored, components, planes, each, columns = out_ref.shape
    shares = seg_places * rad_places
    width = columns // (2 * shares)
    chunk = width // 2
    count = (width // 8) * components * (planes // 2)
    slots = components * (planes // 2)
    half = pl.program_id(0)

    @pl.loop(0, 2 * shares, unroll=UNROLL[6])
    def _(member):
        share, low = member // 2, lax.rem(member, 2)
        source = share * ax_places + 2 * half + low
        split = gathered_list(pieces(wire_ref[source].reshape(-1, 128)), count)
        for slot in range(slots):
            parts = [split[part * slots + slot] for part in range(width // 8)]
            rows = jnp.concatenate(parts, axis=0)
            for high in range(2):
                at = (2 * high + low) * (columns // 4) + share * chunk
                held_ref[slot, pl.ds(at, chunk), :] = rows[high * chunk : (high + 1) * chunk]

    @pl.loop(0, slots, unroll=UNROLL[7])
    def _(slot):
        component, pair = slot // (planes // 2), lax.rem(slot, planes // 2)
        ending = held_ref[slot].T
        for side in range(2):
            plane = 2 * pair + side
            row = pl.multiple_of((component * planes + plane) * each, 8)
            upcoming = jnp.where(
                half + 1 < pl.num_programs(0),
                start_ref[0, component, plane],
                following_ref[pl.ds(row, each), :],
            )
            out_ref[0, component, plane] = ending[side * each : (side + 1) * each] - upcoming


def in_place(value):
    return pltpu.with_memory_space_constraint(value, pltpu.HBM)


def whole_blocks(count):
    return [pl.BlockSpec(memory_space=pltpu.VMEM)] * count


def fits(shape, peers):
    groups, components, axial_rows, radial_rows, columns = shape
    seg_places, rad_places, ax_places = peers
    members = seg_places * rad_places * 2
    return (
        (groups, components, seg_places, ax_places) == (2, 3, 2, 4)
        and axial_rows * ax_places == 16
        and radial_rows == 48
        and rad_places * radial_rows == 192
        and columns == 384
        and members == 16
    )


def half_body(peers, start_states, radial_inverse, offsets, mode_count):
    groups, components, axial_rows, radial_rows, columns = start_states.shape
    seg_places, rad_places, ax_places = peers
    axial = axial_rows * ax_places
    radii = radial_rows * rad_places
    shares = seg_places * rad_places
    members = 2 * shares
    own_radii = radii // members
    own_modes = radial_inverse.shape[0] // shares
    width = columns // members
    tiles = own_radii * 3 // 4
    order = column_order(columns, radial_inverse.shape[0], shares)
    synthesis_natural, synthesis, analysis, mode_of_row = tables(columns, order)

    seg, rad, ax = (lax.axis_index(name) for name in MESH_AXES)
    half, low = ax // 2, ax % 2

    def device(s, r, a):
        return (s * rad_places + r) * ax_places + a

    half_groups = [
        [
            device(s, r, 2 * h + l)
            for s in range(seg_places)
            for r in range(rad_places)
            for l in range(2)
        ]
        for h in range(2)
    ]
    mirror = [(a, (a + 2) % 4) for a in range(4)]
    params = pltpu.CompilerParams(vmem_limit_bytes=VMEM_LIMIT)
    up = [(i, (i + 1) % ax_places) for i in range(ax_places)]
    down = [(j, i) for i, j in up]
    halo = jax.ShapeDtypeStruct((groups, components, radial_rows, columns), jnp.float32)
    with jax.named_scope("pack_halos"):
        last, leading = pl.pallas_call(
            pack_halos,
            in_specs=[pl.BlockSpec(memory_space=pltpu.HBM)],
            out_specs=whole_blocks(2),
            out_shape=[halo, halo],
            scratch_shapes=[pltpu.SemaphoreType.DMA((2,))],
            compiler_params=params,
        )(in_place(start_states))
    before = lax.ppermute(last, "ax", up)
    after = lax.ppermute(leading, "ax", down)

    share = seg * rad_places + rad
    place = jnp.stack([share, half, seg]).astype(jnp.int32)
    first_rows = components * axial_rows * radial_rows
    with jax.named_scope("pack_sent"):
        dense_inverse, first_start = pl.pallas_call(
            pack_sent,
            in_specs=[
                pl.BlockSpec(memory_space=pltpu.SMEM),
                pl.BlockSpec(memory_space=pltpu.SMEM),
                pl.BlockSpec(memory_space=pltpu.HBM),
                pl.BlockSpec(memory_space=pltpu.HBM),
            ],
            out_specs=whole_blocks(2),
            out_shape=[
                jax.ShapeDtypeStruct((own_modes * 3 // 2, radii, 128), jnp.float32),
                jax.ShapeDtypeStruct((first_rows + 8, columns), jnp.float32),
            ],
            scratch_shapes=[
                pltpu.VMEM((own_modes, radii, radii), jnp.float32),
                pltpu.VMEM(start_states.shape[1:], jnp.float32),
                pltpu.SemaphoreType.DMA((2,)),
            ],
            compiler_params=params,
        )(place, offsets, in_place(radial_inverse), in_place(start_states))
    first = rad * radial_rows + (seg * 2 + low) * own_radii
    tile_index = np.arange(tiles)[:, None]
    lane = np.arange(128)[None, :]
    local = 4 * (tile_index // 3) + np.where(lane < 96, tile_index % 3, 3)
    radius = ((first + jnp.asarray(local)).astype(jnp.float32) + 0.5) / radii
    profile = (1.0 - radius * radius).reshape(tiles // 3, 3, 128)

    own_radius = ((rad * radial_rows + jnp.arange(radial_rows)).astype(jnp.float32) + 0.5) / radii
    own_profile = jnp.broadcast_to((1.0 - own_radius * own_radius)[:, None], (radial_rows, 128))

    synthesis_natural, synthesis, analysis = (
        jnp.asarray(table) for table in (synthesis_natural, synthesis, analysis)
    )
    mode_rows = jnp.asarray(np.repeat(mode_of_row[:, None], 128, axis=1))
    wire = jax.ShapeDtypeStruct((members, tiles, width, 128), jnp.float32)
    wire_spec = pl.BlockSpec((members, 3, width, 128), lambda g: (0, g, 0, 0))
    held = pltpu.VMEM((radii * width, 128), jnp.float32)
    count = (width // 8) * components * (axial_rows // 2)
    end_tiles = (count // 4) * 3 + count % 4
    everyone = seg_places * rad_places * ax_places
    spread_wire = jax.ShapeDtypeStruct((everyone, end_tiles, 8, 128), jnp.float32)

    def exchanged(value):
        return lax.all_to_all(
            value, MESH_AXES, 0, 0, axis_index_groups=half_groups, tiled=True
        )

    step = radial_rows // 3
    halo_spec = pl.BlockSpec((groups, components, step, columns), lambda g: (0, 0, g, 0))
    own_spec = pl.BlockSpec(
        (groups, components, axial_rows, step, columns), lambda g: (0, 0, 0, g, 0)
    )
    with jax.named_scope("own_physical"):
        physical = pl.pallas_call(
            own_physical,
            grid=(3,),
            in_specs=[own_spec] + whole_blocks(1),
            out_specs=own_spec,
            out_shape=jax.ShapeDtypeStruct(start_states.shape, jnp.float32),
            compiler_params=params,
        )(start_states, synthesis_natural)
    before, after, dense_inverse, physical, profile, own_profile = lax.optimization_barrier(
        (before, after, dense_inverse, physical, profile, own_profile)
    )
    other_inverse = lax.ppermute(dense_inverse, "ax", mirror)
    with jax.named_scope("phase_a_first"):
        spectral = pl.pallas_call(
            first_phase_a,
            grid=(3,),
            in_specs=[
                pl.BlockSpec(memory_space=pltpu.SMEM),
                halo_spec,
                own_spec,
                halo_spec,
                *whole_blocks(3),
                pl.BlockSpec((step, 128), lambda g: (g, 0)),
            ],
            out_specs=wire_spec,
            out_shape=pltpu.HBM(wire.shape, wire.dtype),
            scratch_shapes=[
                pltpu.VMEM(
                    (columns // 128, groups * components * axial_rows * step, 128), jnp.float32
                )
            ],
            compiler_params=params,
        )(
            mode_count,
            before,
            physical,
            after,
            synthesis_natural,
            analysis,
            mode_rows,
            own_profile,
        )
    matrices = jax.ShapeDtypeStruct((2 * own_modes, radii, radii), jnp.bfloat16)
    in_hbm = [pl.BlockSpec(memory_space=pltpu.HBM)] * 2
    inverse_scratch = [pltpu.VMEM(matrices.shape, matrices.dtype)] * 2
    inverse_scratch += [pltpu.SemaphoreType.DMA((2,))]
    with jax.named_scope("ordered_inverse"):
        inverse = pl.pallas_call(
            ordered_inverse,
            in_specs=[pl.BlockSpec(memory_space=pltpu.SMEM)] + whole_blocks(2),
            out_specs=[pl.BlockSpec(matrices.shape, lambda: (0, 0, 0))] * 2,
            out_shape=[pltpu.HBM(matrices.shape, matrices.dtype)] * 2,
            compiler_params=params,
            cost_estimate=pl.CostEstimate(
                flops=FLOPS, bytes_accessed=16 * own_modes * radii * radii, transcendentals=0
            ),
        )(place, dense_inverse, other_inverse)
    spectral, first_start = lax.optimization_barrier((spectral, first_start))
    following = passed_along(first_start, "seg", -1)
    lines = exchanged(spectral)
    with jax.named_scope("phase_b_first"):
        solved = pl.pallas_call(
            functools.partial(phase_b, peers),
            in_specs=in_hbm + whole_blocks(1),
            out_specs=pl.BlockSpec(memory_space=pltpu.VMEM),
            out_shape=spread_wire,
            scratch_shapes=[held, held] + inverse_scratch,
            compiler_params=params,
        )(*map(in_place, inverse), lines)
    solved, following = lax.optimization_barrier((solved, following))
    state = lax.all_to_all(solved, MESH_AXES, 0, 0, tiled=True)
    with jax.named_scope("phase_a_later"):
        spectral = pl.pallas_call(
            later_phase_a,
            grid=(tiles // 3 + 1,),
            in_specs=[
                pl.BlockSpec(memory_space=pltpu.SMEM),
                *whole_blocks(6),
            ],
            out_specs=pl.BlockSpec(
                wire_spec.block_shape, lambda g: (0, jnp.maximum(g - 1, 0), 0, 0)
            ),
            out_shape=wire,
            scratch_shapes=[
                pltpu.VMEM((2, own_radii // 2, columns, 128), jnp.float32),
                pltpu.VMEM((2, columns, 3 * 128), jnp.float32),
            ],
            compiler_params=params,
        )(mode_count, state, synthesis, analysis, mode_rows, profile, jnp.asarray(lane_moves()))
    lines = exchanged(spectral)
    with jax.named_scope("phase_b_last"):
        ending = pl.pallas_call(
            functools.partial(last_phase_b, peers),
            in_specs=[pl.BlockSpec(memory_space=pltpu.SMEM)] * 2
            + whole_blocks(1)
            + in_hbm
            + whole_blocks(1),
            out_specs=pl.BlockSpec(memory_space=pltpu.VMEM),
            out_shape=spread_wire,
            scratch_shapes=[held, pltpu.VMEM((2, 96 * width, 128), jnp.float32)]
            + inverse_scratch,
            compiler_params=params,
        )(place, offsets, following, *map(in_place, inverse), lines)
    ending = lax.all_to_all(ending, MESH_AXES, 0, 0, tiled=True)
    with jax.named_scope("residual_end"):
        return pl.pallas_call(
            functools.partial(residual_end, peers),
            grid=(groups,),
            in_specs=[
                *whole_blocks(1),
                pl.BlockSpec((1,) + start_states.shape[1:], lambda b: (groups - 1, 0, 0, 0, 0)),
                *whole_blocks(1),
            ],
            out_specs=pl.BlockSpec((1,) + start_states.shape[1:], lambda b: (b, 0, 0, 0, 0)),
            out_shape=jax.ShapeDtypeStruct(start_states.shape, jnp.float32),
            scratch_shapes=[pltpu.VMEM((components * (axial_rows // 2), columns, 128), jnp.float32)],
            compiler_params=params,
        )(ending, start_states, following)


def solution(mesh):
    peers = tuple(mesh.shape[name] for name in MESH_AXES)

    def body(start_states, radial_inverse, offsets, mode_count):
        if fits(start_states.shape, peers):
            return half_body(peers, start_states, radial_inverse, offsets, mode_count)
        return general_body(start_states, radial_inverse, offsets, mode_count)

    placed = (P("seg", None, "ax", "rad", None), P("ax", None, None), P("seg"), P())
    return jax.shard_map(
        body,
        mesh=mesh,
        in_specs=placed,
        out_specs=P("seg", None, "ax", "rad", None),
        check_vma=False,
    )
```

```python
import functools
import math

import jax
import jax.numpy as jnp
import ml_dtypes
import numpy as np
from jax import lax
from jax.experimental import pallas as pl
from jax.experimental.pallas import tpu as pltpu
from jax.sharding import PartitionSpec as P

STEPS = 2
MESH_AXES = ("seg", "rad", "ax")
UNROLL = [12, 12, 16, 16, 8, 32, 16, 6]
VMEM_LIMIT = 24 * 1024 * 1024
FLOPS = 40_000_000_000

highest = lax.Precision.HIGHEST


def passed_along(value, axis, steps):
    count = lax.axis_size(axis)
    pairs = [(source, (source + steps) % count) for source in range(count)]
    return lax.ppermute(value, axis, pairs)


def padded_2(array, sides, width):
    for axis, dim in sides:
        peers, length = (lax.axis_size(axis), array.shape[dim])
        up = [(i, (i + 1) % peers) for i in range(peers)]
        down = [(j, i) for i, j in up]
        last = lax.slice_in_dim(array, length - width, length, axis=dim)
        leading = lax.slice_in_dim(array, 0, width, axis=dim)
        before = lax.ppermute(last, axis, up)
        after = lax.ppermute(leading, axis, down)
        array = jnp.concatenate([before, array, after], axis=dim)
    return array


def fourier_tables(columns, kept_modes):
    modes_total = columns // 2
    row_index = lax.broadcasted_iota(jnp.int32, (columns, columns), 0)
    point_index = lax.broadcasted_iota(jnp.int32, (columns, columns), 1)
    mode_index = row_index // 2
    phase = (mode_index * point_index % columns).astype(jnp.float32) * (2.0 * math.pi / columns)
    even_rows = row_index % 2 == 0
    cosine = jnp.cos(phase)
    sine = jnp.sin(phase)
    root = math.sqrt(modes_total)
    synthesis = jnp.where(even_rows, cosine, sine) / root
    weights = jnp.where(mode_index == 0, 1.0, 2.0)
    analysis = jnp.where(even_rows, weights * cosine, 2.0 * sine) * (root / columns)
    analysis = jnp.where(mode_index < kept_modes, analysis, 0.0)
    return (synthesis, analysis)


def radial_solve(pencils, radial_inverse, radial_rows):
    local_modes = radial_inverse.shape[0]
    local_columns, members, axial_cells, ignored = pencils.shape
    own_rows = lax.dynamic_slice_in_dim(
        radial_inverse, lax.axis_index("rad") * radial_rows, radial_rows, 1
    )
    piece = lax.all_gather(pencils, "rad", axis=3, tiled=True)
    piece_rows = piece.shape[3]
    grouped = piece.reshape(local_modes, 2, members, axial_cells, piece_rows)
    product = jnp.einsum("mrs,mkqzs->mkqzr", own_rows, grouped, precision=highest)
    return product.reshape(local_columns, members, axial_cells, radial_rows)


def general_body(start_states, radial_inverse, offsets, mode_count):
    groups, components, axial_rows, radial_rows, columns = start_states.shape
    synthesis, analysis = fourier_tables(columns, mode_count[0])
    radius = (
        (lax.axis_index("rad") * radial_rows + jnp.arange(radial_rows)).astype(jnp.float32) + 0.5
    ) / (radial_rows * lax.axis_size("rad"))
    profile = (1.0 - radius * radius).reshape(1, 1, 1, radial_rows, 1)
    following = passed_along(start_states[0], "seg", -1)
    current = start_states
    for step_index in range(STEPS):
        if step_index == 0:
            physical = jnp.einsum("gczrj,jp->gczrp", current, synthesis, precision=highest)
        else:
            physical = jnp.einsum("jgczr,jp->gczrp", current, synthesis, precision=highest)
        padded = padded_2(physical, (("ax", 2),), 1)
        gradient = (padded[:, :, 2:] - padded[:, :, :-2]) * 20.0
        advecting = profile + padded[:, 2:3, 1:-1]
        forcing = physical - 0.02 * advecting * gradient
        spectral = jnp.einsum("gczrp,jp->jgczr", forcing, analysis, precision=highest)
        pencils = lax.all_to_all(spectral, "ax", split_axis=0, concat_axis=3, tiled=True)
        local_columns = pencils.shape[0]
        axial_cells = pencils.shape[3]
        pencils = pencils.reshape(local_columns, groups * components, axial_cells, radial_rows)
        solved = radial_solve(pencils, radial_inverse, radial_rows)
        if step_index == STEPS - 1:
            blocks = solved.reshape(local_columns, groups, components, axial_cells, radial_rows)
            shifted = [
                jnp.roll(blocks[:, member], offsets[member], axis=2) for member in range(groups)
            ]
            solved = jnp.stack(shifted, axis=1).reshape(
                local_columns, groups * components, axial_cells, radial_rows
            )
        returned = lax.all_to_all(solved, "ax", split_axis=2, concat_axis=0, tiled=True)
        current = returned.reshape(columns, groups, components, axial_rows, radial_rows)
    ending = jnp.transpose(current, (1, 2, 3, 4, 0))
    upcoming = jnp.concatenate([start_states[1:], following[None]], axis=0)
    return ending - upcoming


def halves(high):
    top = high.astype(jnp.bfloat16)
    return top, (high - top.astype(jnp.float32)).astype(jnp.bfloat16)


def product(left, right, contract):
    return lax.dot_general(
        left, right, ((contract[:1], contract[1:]), ((), ())), preferred_element_type=jnp.float32
    )


def stacked_table(table):
    top = table.astype(ml_dtypes.bfloat16)
    rest = (table - top.astype(np.float64)).astype(ml_dtypes.bfloat16)
    return np.concatenate([top, top, rest], axis=1)


def column_order(columns, quarter_modes, shares):
    each = quarter_modes // shares
    order = []
    for share in range(shares):
        for low in range(2):
            for high in range(2):
                first = (2 * high + low) * quarter_modes + share * each
                order.extend(range(2 * first, 2 * (first + each)))
    assert sorted(order) == list(range(columns))
    return np.array(order)


def tables(columns, order):
    modes_total = columns // 2
    rows = np.arange(columns)
    mode = rows // 2
    phase = (mode[:, None] * np.arange(columns)[None, :]) % columns * (2.0 * np.pi / columns)
    even = (rows % 2 == 0)[:, None]
    root = math.sqrt(modes_total)
    synthesis = np.where(even, np.cos(phase), np.sin(phase)) / root
    weights = np.where(mode == 0, 1.0, 2.0)[:, None]
    analysis = np.where(even, weights * np.cos(phase), 2.0 * np.sin(phase)) * (root / columns)
    return (
        np.ascontiguousarray(stacked_table(synthesis.T).T),
        stacked_table(np.ascontiguousarray(synthesis.T[:, order])),
        stacked_table(analysis[order]),
        mode[order].astype(np.int32),
    )


def lane_index(block):
    return lax.broadcasted_iota(jnp.int32, block.shape, 1)


def spread(tiles, fourth):
    lane = lane_index(fourth)
    return [
        jnp.where(lane < 96, block, pltpu.roll(fourth, 96 - 32 * index, 1))
        for index, block in enumerate(tiles)
    ]


def gathered(waves):
    lane = lane_index(waves[0])
    fourth = jnp.where(lane < 32, pltpu.roll(waves[0], 32, 1), pltpu.roll(waves[1], 64, 1))
    return waves + [jnp.where(lane < 64, fourth, pltpu.roll(waves[2], 96, 1))]


def every(blocks, first, step):
    return jnp.concatenate(blocks[first::step], axis=0)


def pieces(block):
    return [block[at : at + 8] for at in range(0, block.shape[0], 8)]


def spread_list(blocks):
    whole = len(blocks) // 4 * 4
    quarters = [every(blocks[:whole], first, 4) for first in range(4)]
    full = [pieces(block) for block in spread(quarters[:3], quarters[3])]
    return [block for group in zip(*full) for block in group] + blocks[whole:]


def gathered_list(full, count):
    whole = count // 4 * 3
    blocks = [pieces(block) for block in gathered([every(full[:whole], i, 3) for i in range(3)])]
    return [block for group in zip(*blocks) for block in group] + full[whole:]


def lane_moves():
    lane = np.arange(128)
    moves = np.zeros((128, 256), np.float32)
    above = lane // 16 * 16 + (lane + 1) % 16
    below = lane // 16 * 16 + (lane + 15) % 16
    np.add.at(moves, (above, lane), 1.0)
    np.add.at(moves, (below, lane), -1.0)
    whole = lane[:96]
    moves[64 + whole % 32, 128 + whole] = 1.0
    return np.concatenate([moves, moves], axis=0).astype(ml_dtypes.bfloat16)


def physical_to_spectral(physical, profile, analysis, moves):
    lane = lane_index(physical[0])
    forcing = []
    for tile in range(3):
        field = physical[tile]
        moved = product(jnp.concatenate(halves(field), axis=1), moves, (1, 0))
        speed = jnp.where(lane < 96, moved[:, 128:], physical[2])
        forcing.append(field - 0.4 * (profile[tile : tile + 1] + speed) * moved[:, :128])
    forcing = jnp.concatenate(forcing, axis=1)
    top, rest = halves(forcing)
    return product(analysis, jnp.concatenate([top, rest, top], axis=0), (1, 0))


def write_spectral(spectral, count_ref, mode_ref, out_ref):
    members, ignored, width, ignored = out_ref.shape
    kept = mode_ref[...] < count_ref[0]
    for tile in range(3):
        block = jnp.where(kept, spectral[:, tile * 128 : (tile + 1) * 128], 0.0)
        out_ref[:, tile] = block.reshape(members, width, 128)


def pack_halos(start_ref, last_ref, leading_ref, sems):
    planes = start_ref.shape[2]
    copies = [
        pltpu.make_async_copy(start_ref.at[:, :, planes - 1], last_ref, sems.at[0]),
        pltpu.make_async_copy(start_ref.at[:, :, 0], leading_ref, sems.at[1]),
    ]
    for copy in copies:
        copy.start()
    for copy in copies:
        copy.wait()


def synthesized(rows, synthesis):
    top, rest = halves(jnp.concatenate(rows, axis=0))
    return product(jnp.concatenate([top, rest, top], axis=1), synthesis, (1, 0))


def own_physical(own_ref, synthesis_ref, out_ref):
    groups, components, planes, radii, columns = own_ref.shape
    rows = own_ref[...].reshape(groups * components * planes * radii, columns)
    out_ref[...] = synthesized([rows], synthesis_ref[...]).reshape(out_ref.shape)


def first_phase_a(
    count_ref,
    before_ref,
    own_ref,
    after_ref,
    synthesis_ref,
    analysis_ref,
    mode_ref,
    profile_ref,
    out_ref,
    held_ref,
):
    groups, components, planes, radii, columns = own_ref.shape
    strips = columns // 128
    count = groups * components
    sides = [ref[...].reshape(count * radii, columns) for ref in (before_ref, after_ref)]
    sides = synthesized(sides, synthesis_ref[...]).reshape(2, groups, components, radii, columns)
    profile = jnp.concatenate([profile_ref[...]] * strips, axis=1)
    for segment in range(groups):
        for plane in range(planes):
            speed = 0.4 * (profile + own_ref[segment, 2, plane])
            for component in range(components):
                line = [own_ref[segment, component, i] for i in range(planes)]
                line = [sides[0, segment, component], *line, sides[1, segment, component]]
                forcing = line[plane + 1] - speed * (line[plane + 2] - line[plane])
                first = (component * groups + segment) * radii * planes
                at = pl.ds(first + plane, radii, stride=planes)
                for strip in range(strips):
                    held_ref[strip, at, :] = forcing[:, strip * 128 : (strip + 1) * 128]
    quad = 4 * planes
    lines = []
    for strip in range(strips):
        parts = []
        for tile in range(3):
            for four, members in ((tile, range(components)), (3, (tile,))):
                for component in members:
                    for at in range(four * quad, (four + 1) * quad, quad // 2):
                        for segment in range(groups):
                            row = (component * groups + segment) * radii * planes + at
                            parts.append(held_ref[strip, row : row + quad // 2, :])
        lines.append(jnp.concatenate(parts, axis=0))
    top, rest = halves(jnp.concatenate(lines, axis=1))
    spectral = product(analysis_ref[...], jnp.concatenate([top, rest, top], axis=1), (1, 1))
    write_spectral(spectral, count_ref, mode_ref, out_ref)


def later_phase_a(
    count_ref,
    wire_ref,
    synthesis_ref,
    analysis_ref,
    mode_ref,
    profile_ref,
    moves_ref,
    out_ref,
    held_ref,
    physical_ref,
):
    sources, tiles, ignored, ignored = wire_ref.shape
    halves_of_ax, pairs, ignored, ignored = held_ref.shape
    parts = out_ref.shape[2] // 8

    def unpack():
        @pl.loop(0, sources, unroll=UNROLL[5])
        def _(source):
            half = lax.rem(source, 4) // 2
            member = source // 4 * 2 + lax.rem(source, 2)
            blocks = gathered_list(pieces(wire_ref[source].reshape(tiles * 8, 128)), pairs * parts)
            for part in range(parts):
                at = pl.ds(pl.multiple_of((member * parts + part) * 8, 8), 8)
                for pair in range(pairs):
                    held_ref[half, pair, at, :] = blocks[part * pairs + pair]

    def begin(group):
        radii = []
        for pair in range(2):
            one, two = (held_ref[half, 2 * group + pair] for half in range(halves_of_ax))
            low = lane_index(one) & 8 == 0
            radii.append(jnp.where(low, one, pltpu.roll(two, 8, 1)))
            radii.append(jnp.where(low, pltpu.roll(one, 120, 1), two))
        top, rest = halves(jnp.concatenate(spread(radii[:3], radii[3]), axis=1))
        physical_ref[group % 2] = product(
            synthesis_ref[...], jnp.concatenate([top, rest, top], axis=0), (1, 0)
        )

    def finish(group):
        physical = [physical_ref[group % 2, :, tile * 128 : (tile + 1) * 128] for tile in range(3)]
        spectral = physical_to_spectral(
            physical, profile_ref[group], analysis_ref[...], moves_ref[...]
        )
        write_spectral(spectral, count_ref, mode_ref, out_ref)

    for step in range(pairs // 2 + 1):

        @pl.when(pl.program_id(0) == step)
        def _(step=step):
            if step == 0:
                unpack()
            if step < pairs // 2:
                begin(step)
            if step > 0:
                finish(step - 1)


def quad_moves():
    moves = np.zeros((4, 128, 4, 128), np.float32)
    for source in range(4):
        for lane in range(96):
            block, two, segment, one, z = (
                lane // 32,
                lane // 16 % 2,
                lane // 8 % 2,
                lane // 4 % 2,
                lane % 4,
            )
            target = block * 32 + source // 2 * 16 + segment * 8 + source % 2 * 4 + z
            moves[source, lane, 2 * two + one, target] = 1.0
    return moves.reshape(512, 512).astype(ml_dtypes.bfloat16)


def unpack_quads(wire_ref, moves_ref, held_ref, peers):
    members, tiles, width, ignored = wire_ref.shape
    seg_places, rad_places, ignored = peers
    groups = tiles // 3

    @pl.loop(0, rad_places * groups, unroll=UNROLL[1])
    def _(index):
        rad, group = index // groups, lax.rem(index, groups)
        sources = [(s * rad_places + rad) * 2 + l for s in range(seg_places) for l in range(2)]
        waves = [
            jnp.concatenate([wire_ref[source, 3 * group + tile] for source in sources], axis=0)
            for tile in range(3)
        ]
        quads = gathered(waves)
        lines = [
            jnp.concatenate([quad[at : at + width] for quad in quads], axis=0)
            for at in range(0, 4 * width, width)
        ]
        top, rest = halves(jnp.concatenate(lines, axis=1))
        radii = product(top, moves_ref[...], (1, 0)) + product(rest, moves_ref[...], (1, 0))
        for place in range(4):
            for quad in range(4):
                at = pl.multiple_of((index * 16 + 4 * quad + place) * width, 8)
                held_ref[pl.ds(at, width), :] = radii[
                    quad * width : (quad + 1) * width, place * 128 : (place + 1) * 128
                ]


def first_radius(member, own):
    rad = lax.rem(member // 2, 4)
    return ((rad * 2 + member // 8) * 2 + lax.rem(member, 2)) * own


def unpack_radii(wire_ref, held_ref):
    members, tiles, width, ignored = wire_ref.shape
    own = tiles * 4 // 3

    @pl.loop(0, members, unroll=UNROLL[2])
    def _(member):
        first = first_radius(member, own)
        waves = [
            jnp.concatenate([wire_ref[member, at] for at in range(tile, tiles, 3)], axis=0)
            for tile in range(3)
        ]
        for index, block in enumerate(gathered(waves)):
            for group in range(tiles // 3):
                at = pl.multiple_of((first + 4 * group + index) * width, 8)
                held_ref[pl.ds(at, width), :] = block[group * width : (group + 1) * width]


def pack_sent(
    place_ref, offset_ref, inverse_ref, start_ref, out_ref, first_ref, held_ref, start_held_ref, sems
):
    each, radii, ignored = held_ref.shape
    copy = pltpu.make_async_copy(
        inverse_ref.at[pl.ds(place_ref[0] * each, each)], held_ref, sems.at[0]
    )
    copy.start()
    first = pltpu.make_async_copy(start_ref.at[0], start_held_ref, sems.at[1])
    first.start()
    rows = first_ref.shape[0] - 8
    for index in range(8):
        offset = offset_ref[index % offset_ref.shape[0]].astype(jnp.float32)
        first_ref[rows + index : rows + index + 1, :] = jnp.full((1, first_ref.shape[1]), offset)
    copy.wait()
    for index in range(each):
        out_ref[index] = held_ref[index, :, :128]
    for index in range(each // 2):
        out_ref[each + index, :, :64] = held_ref[index, :, 128:]
        out_ref[each + index, :, 64:] = held_ref[each // 2 + index, :, 128:]
    first.wait()
    first_ref[0:rows, :] = start_held_ref[...].reshape(rows, first_ref.shape[1])


def ordered_inverse(place_ref, own_ref, other_ref, top_ref, rest_ref):
    each = top_ref.shape[0] // 2
    first_half = place_ref[1] == 0

    def matrix(ref, index):
        side = index // (each // 2) * 64
        tail = ref[each + index % (each // 2), :, side : side + 64]
        return jnp.concatenate([ref[index], tail], axis=1)

    for index in range(each):
        here, there = matrix(own_ref, index), matrix(other_ref, index)
        top_ref[index], rest_ref[index] = halves(jnp.where(first_half, here, there))
        top_ref[each + index], rest_ref[each + index] = halves(jnp.where(first_half, there, here))


def inverse_copies(top_hbm, rest_hbm, top_ref, rest_ref, sems):
    copies = [
        pltpu.make_async_copy(source, target, sems.at[index])
        for index, (source, target) in enumerate(((top_hbm, top_ref), (rest_hbm, rest_ref)))
    ]
    for copy in copies:
        copy.start()
    return copies


def solved_modes(top_ref, rest_ref, held_ref, transposed, store):
    modes, radii, ignored = top_ref.shape
    width = 2 * modes

    @pl.loop(0, modes, unroll=UNROLL[0])
    def _(mode):
        matrix_top, matrix_rest = top_ref[mode], rest_ref[mode]
        state = jnp.concatenate(
            [held_ref[pl.ds(2 * mode + part, radii, stride=width), :] for part in range(2)], axis=1
        )
        if transposed:
            matrix_top, matrix_rest = (
                jnp.concatenate([m[:96], m[:32], m[96:], m[:32]], axis=0)
                for m in (matrix_top, matrix_rest)
            )
            top, rest = halves(state.T)
            solved = product(top, matrix_top, (1, 1))
            solved += product(rest, matrix_top, (1, 1)) + product(top, matrix_rest, (1, 1))
        else:
            top, rest = halves(state)
            solved = product(matrix_top, top, (1, 0))
            solved += product(matrix_top, rest, (1, 0)) + product(matrix_rest, top, (1, 0))
        store(mode, solved)


def phase_b(
    peers,
    top_hbm,
    rest_hbm,
    moves_hbm,
    wire_ref,
    out_ref,
    held_ref,
    solved_ref,
    moves_ref,
    top_ref,
    rest_ref,
    sems,
):
    members, tiles, width, ignored = wire_ref.shape
    radii = top_ref.shape[1]
    ax_places = peers[2]
    first = pltpu.make_async_copy(moves_hbm, moves_ref, sems.at[2])
    first.start()
    copies = inverse_copies(top_hbm, rest_hbm, top_ref, rest_ref, sems)
    first.wait()
    unpack_quads(wire_ref, moves_ref, held_ref, peers)
    for copy in copies:
        copy.wait()

    def store(mode, solved):
        for part in range(2):
            solved_ref[pl.ds(2 * mode + part, radii, stride=width), :] = solved[
                :, part * 128 : (part + 1) * 128
            ]

    solved_modes(top_ref, rest_ref, held_ref, False, store)
    own = radii // members
    low = lax.broadcasted_iota(jnp.int32, (own * width // 2, 128), 1) & 8 == 0

    @pl.loop(0, members, unroll=UNROLL[3])
    def _(member):
        place = first_radius(member, own) * width
        for half in range(2):
            one, two = (
                jnp.concatenate(
                    [
                        solved_ref[pl.ds(pl.multiple_of(place + index * width, 8), width), :]
                        for index in range(first, own, 2)
                    ],
                    axis=0,
                )
                for first in range(2)
            )
            if half == 0:
                blocks = pieces(jnp.where(low, one, pltpu.roll(two, 8, 1)))
            else:
                blocks = pieces(jnp.where(low, pltpu.roll(one, 120, 1), two))
            parts = width // 8
            split = [block for part in range(parts) for block in blocks[part::parts]]
            target = member // 2 * ax_places + 2 * half + lax.rem(member, 2)
            for index, block in enumerate(spread_list(split)):
                out_ref[target, index] = block


def last_phase_b(
    peers,
    place_ref,
    own_offset_ref,
    other_offset_ref,
    top_hbm,
    rest_hbm,
    wire_ref,
    out_ref,
    held_ref,
    solved_ref,
    top_ref,
    rest_ref,
    sems,
):
    members, tiles, width, ignored = wire_ref.shape
    radii = top_ref.shape[1]
    seg_places, rad_places, ax_places = peers
    planes = 16 // ax_places
    each = radii // rad_places
    half = place_ref[1]
    rows = other_offset_ref.shape[0] - 8
    others = [jnp.max(other_offset_ref[rows + i : rows + i + 1, :128]) for i in range(2)]
    other_offset = jnp.where(half == 0, *others).astype(jnp.int32)
    copies = inverse_copies(top_hbm, rest_hbm, top_ref, rest_ref, sems)
    unpack_radii(wire_ref, held_ref)
    for copy in copies:
        copy.wait()

    def store(mode, solved):
        for part in range(2):
            rows = pl.ds(2 * mode + part, 96, stride=width)
            block = solved[part * 128 : part * 128 + 96]
            for strip in range(2):
                solved_ref[strip, rows, :] = block[:, strip * 128 : (strip + 1) * 128]

    solved_modes(top_ref, rest_ref, held_ref, True, store)
    lane = lax.broadcasted_iota(jnp.int32, (planes // 2 * width, 128), 1)


    @pl.loop(0, seg_places * ax_places, unroll=UNROLL[4])
    def _(index):
        seg, ax = index // ax_places, lax.rem(index, ax_places)
        offset = jnp.where(place_ref[2] == seg, own_offset_ref[half], other_offset)
        blocks = {}
        for component in range(3):
            for plane in range(planes):
                source = lax.rem(ax * planes + plane - offset + 16, 16)
                row = (component * 32 + seg * 16 + source) * width
                row = pl.multiple_of(row, 8)
                blocks[component, plane] = row
        for rad in range(rad_places):
            parts = width // 8
            slots = []
            for component in range(3):
                sides = []
                for side in range(2):
                    rows = [
                        pl.ds(blocks[component, plane], width) for plane in range(side, planes, 2)
                    ]
                    lines = [solved_ref[rad // 2, at, :] for at in rows]
                    sides.append(jnp.concatenate(lines, axis=0))
                if rad % 2 == 0:
                    sides[1] = pltpu.roll(sides[1], each, 1)
                else:
                    sides[0] = pltpu.roll(sides[0], 128 - each, 1)
                slots += pieces(jnp.where(lane < each, *sides))
            split = [block for part in range(parts) for block in slots[part::parts]]
            target = (seg * rad_places + rad) * ax_places + ax
            for at, block in enumerate(spread_list(split)):
                out_ref[target, at] = block


def residual_end(peers, wire_ref, start_ref, following_ref, out_ref, held_ref):
    seg_places, rad_places, ax_places = peers
    ignored, components, planes, each, columns = out_ref.shape
    shares = seg_places * rad_places
    width = columns // (2 * shares)
    chunk = width // 2
    count = (width // 8) * components * (planes // 2)
    slots = components * (planes // 2)
    half = pl.program_id(0)

    @pl.loop(0, 2 * shares, unroll=UNROLL[6])
    def _(member):
        share, low = member // 2, lax.rem(member, 2)
        source = share * ax_places + 2 * half + low
        split = gathered_list(pieces(wire_ref[source].reshape(-1, 128)), count)
        for slot in range(slots):
            parts = [split[part * slots + slot] for part in range(width // 8)]
            rows = jnp.concatenate(parts, axis=0)
            for high in range(2):
                at = (2 * high + low) * (columns // 4) + share * chunk
                held_ref[slot, pl.ds(at, chunk), :] = rows[high * chunk : (high + 1) * chunk]

    @pl.loop(0, slots, unroll=UNROLL[7])
    def _(slot):
        component, pair = slot // (planes // 2), lax.rem(slot, planes // 2)
        ending = held_ref[slot].T
        for side in range(2):
            plane = 2 * pair + side
            row = pl.multiple_of((component * planes + plane) * each, 8)
            upcoming = jnp.where(
                half + 1 < pl.num_programs(0),
                start_ref[0, component, plane],
                following_ref[pl.ds(row, each), :],
            )
            out_ref[0, component, plane] = ending[side * each : (side + 1) * each] - upcoming


def in_place(value):
    return pltpu.with_memory_space_constraint(value, pltpu.HBM)


def whole_blocks(count):
    return [pl.BlockSpec(memory_space=pltpu.VMEM)] * count


def fits(shape, peers):
    groups, components, axial_rows, radial_rows, columns = shape
    seg_places, rad_places, ax_places = peers
    members = seg_places * rad_places * 2
    return (
        (groups, components, seg_places, ax_places) == (2, 3, 2, 4)
        and axial_rows * ax_places == 16
        and radial_rows == 48
        and rad_places * radial_rows == 192
        and columns == 384
        and members == 16
    )


def half_body(peers, start_states, radial_inverse, offsets, mode_count):
    groups, components, axial_rows, radial_rows, columns = start_states.shape
    seg_places, rad_places, ax_places = peers
    axial = axial_rows * ax_places
    radii = radial_rows * rad_places
    shares = seg_places * rad_places
    members = 2 * shares
    own_radii = radii // members
    own_modes = radial_inverse.shape[0] // shares
    width = columns // members
    tiles = own_radii * 3 // 4
    order = column_order(columns, radial_inverse.shape[0], shares)
    synthesis_natural, synthesis, analysis, mode_of_row = tables(columns, order)

    seg, rad, ax = (lax.axis_index(name) for name in MESH_AXES)
    half, low = ax // 2, ax % 2

    def device(s, r, a):
        return (s * rad_places + r) * ax_places + a

    half_groups = [
        [
            device(s, r, 2 * h + l)
            for s in range(seg_places)
            for r in range(rad_places)
            for l in range(2)
        ]
        for h in range(2)
    ]
    mirror = [(a, (a + 2) % 4) for a in range(4)]
    params = pltpu.CompilerParams(vmem_limit_bytes=VMEM_LIMIT)
    up = [(i, (i + 1) % ax_places) for i in range(ax_places)]
    down = [(j, i) for i, j in up]
    halo = jax.ShapeDtypeStruct((groups, components, radial_rows, columns), jnp.float32)
    with jax.named_scope("pack_halos"):
        last, leading = pl.pallas_call(
            pack_halos,
            in_specs=[pl.BlockSpec(memory_space=pltpu.HBM)],
            out_specs=whole_blocks(2),
            out_shape=[halo, halo],
            scratch_shapes=[pltpu.SemaphoreType.DMA((2,))],
            compiler_params=params,
        )(in_place(start_states))
    before = lax.ppermute(last, "ax", up)
    after = lax.ppermute(leading, "ax", down)

    share = seg * rad_places + rad
    place = jnp.stack([share, half, seg]).astype(jnp.int32)
    first_rows = components * axial_rows * radial_rows
    with jax.named_scope("pack_sent"):
        dense_inverse, first_start = pl.pallas_call(
            pack_sent,
            in_specs=[
                pl.BlockSpec(memory_space=pltpu.SMEM),
                pl.BlockSpec(memory_space=pltpu.SMEM),
                pl.BlockSpec(memory_space=pltpu.HBM),
                pl.BlockSpec(memory_space=pltpu.HBM),
            ],
            out_specs=whole_blocks(2),
            out_shape=[
                jax.ShapeDtypeStruct((own_modes * 3 // 2, radii, 128), jnp.float32),
                jax.ShapeDtypeStruct((first_rows + 8, columns), jnp.float32),
            ],
            scratch_shapes=[
                pltpu.VMEM((own_modes, radii, radii), jnp.float32),
                pltpu.VMEM(start_states.shape[1:], jnp.float32),
                pltpu.SemaphoreType.DMA((2,)),
            ],
            compiler_params=params,
        )(place, offsets, in_place(radial_inverse), in_place(start_states))
    first = rad * radial_rows + (seg * 2 + low) * own_radii
    tile_index = np.arange(tiles)[:, None]
    lane = np.arange(128)[None, :]
    local = 4 * (tile_index // 3) + np.where(lane < 96, tile_index % 3, 3)
    radius = ((first + jnp.asarray(local)).astype(jnp.float32) + 0.5) / radii
    profile = (1.0 - radius * radius).reshape(tiles // 3, 3, 128)

    own_radius = ((rad * radial_rows + jnp.arange(radial_rows)).astype(jnp.float32) + 0.5) / radii
    own_profile = jnp.broadcast_to((1.0 - own_radius * own_radius)[:, None], (radial_rows, 128))

    synthesis_natural, synthesis, analysis = (
        jnp.asarray(table) for table in (synthesis_natural, synthesis, analysis)
    )
    mode_rows = jnp.asarray(np.repeat(mode_of_row[:, None], 128, axis=1))
    wire = jax.ShapeDtypeStruct((members, tiles, width, 128), jnp.float32)
    wire_spec = pl.BlockSpec((members, 3, width, 128), lambda g: (0, g, 0, 0))
    held = pltpu.VMEM((radii * width, 128), jnp.float32)
    count = (width // 8) * components * (axial_rows // 2)
    end_tiles = (count // 4) * 3 + count % 4
    everyone = seg_places * rad_places * ax_places
    spread_wire = jax.ShapeDtypeStruct((everyone, end_tiles, 8, 128), jnp.float32)

    def exchanged(value):
        return lax.all_to_all(
            value, MESH_AXES, 0, 0, axis_index_groups=half_groups, tiled=True
        )

    step = radial_rows // 3
    halo_spec = pl.BlockSpec((groups, components, step, columns), lambda g: (0, 0, g, 0))
    own_spec = pl.BlockSpec(
        (groups, components, axial_rows, step, columns), lambda g: (0, 0, 0, g, 0)
    )
    with jax.named_scope("own_physical"):
        physical = pl.pallas_call(
            own_physical,
            grid=(3,),
            in_specs=[own_spec] + whole_blocks(1),
            out_specs=own_spec,
            out_shape=jax.ShapeDtypeStruct(start_states.shape, jnp.float32),
            compiler_params=params,
        )(start_states, synthesis_natural)
    before, after, dense_inverse, physical, profile, own_profile = lax.optimization_barrier(
        (before, after, dense_inverse, physical, profile, own_profile)
    )
    other_inverse = lax.ppermute(dense_inverse, "ax", mirror)
    with jax.named_scope("phase_a_first"):
        spectral = pl.pallas_call(
            first_phase_a,
            grid=(3,),
            in_specs=[
                pl.BlockSpec(memory_space=pltpu.SMEM),
                halo_spec,
                own_spec,
                halo_spec,
                *whole_blocks(3),
                pl.BlockSpec((step, 128), lambda g: (g, 0)),
            ],
            out_specs=wire_spec,
            out_shape=pltpu.HBM(wire.shape, wire.dtype),
            scratch_shapes=[
                pltpu.VMEM(
                    (columns // 128, groups * components * axial_rows * step, 128), jnp.float32
                )
            ],
            compiler_params=params,
        )(
            mode_count,
            before,
            physical,
            after,
            synthesis_natural,
            analysis,
            mode_rows,
            own_profile,
        )
    matrices = jax.ShapeDtypeStruct((2 * own_modes, radii, radii), jnp.bfloat16)
    in_hbm = [pl.BlockSpec(memory_space=pltpu.HBM)] * 2
    inverse_scratch = [pltpu.VMEM(matrices.shape, matrices.dtype)] * 2
    inverse_scratch += [pltpu.SemaphoreType.DMA((3,))]
    with jax.named_scope("ordered_inverse"):
        inverse = pl.pallas_call(
            ordered_inverse,
            in_specs=[pl.BlockSpec(memory_space=pltpu.SMEM)] + whole_blocks(2),
            out_specs=[pl.BlockSpec(matrices.shape, lambda: (0, 0, 0))] * 2,
            out_shape=[pltpu.HBM(matrices.shape, matrices.dtype)] * 2,
            compiler_params=params,
            cost_estimate=pl.CostEstimate(
                flops=FLOPS, bytes_accessed=16 * own_modes * radii * radii, transcendentals=0
            ),
        )(place, dense_inverse, other_inverse)
    spectral, first_start = lax.optimization_barrier((spectral, first_start))
    following = passed_along(first_start, "seg", -1)
    lines = exchanged(spectral)
    moves = jnp.asarray(quad_moves())
    with jax.named_scope("phase_b_first"):
        solved = pl.pallas_call(
            functools.partial(phase_b, peers),
            in_specs=in_hbm + [pl.BlockSpec(memory_space=pltpu.HBM)] + whole_blocks(1),
            out_specs=pl.BlockSpec(memory_space=pltpu.VMEM),
            out_shape=spread_wire,
            scratch_shapes=[held, held, pltpu.VMEM(moves.shape, moves.dtype)] + inverse_scratch,
            compiler_params=params,
        )(*map(in_place, (*inverse, moves)), lines)
    solved, following = lax.optimization_barrier((solved, following))
    state = lax.all_to_all(solved, MESH_AXES, 0, 0, tiled=True)
    with jax.named_scope("phase_a_later"):
        spectral = pl.pallas_call(
            later_phase_a,
            grid=(tiles // 3 + 1,),
            in_specs=[
                pl.BlockSpec(memory_space=pltpu.SMEM),
                *whole_blocks(6),
            ],
            out_specs=pl.BlockSpec(
                wire_spec.block_shape, lambda g: (0, jnp.maximum(g - 1, 0), 0, 0)
            ),
            out_shape=wire,
            scratch_shapes=[
                pltpu.VMEM((2, own_radii // 2, columns, 128), jnp.float32),
                pltpu.VMEM((2, columns, 3 * 128), jnp.float32),
            ],
            compiler_params=params,
        )(mode_count, state, synthesis, analysis, mode_rows, profile, jnp.asarray(lane_moves()))
    lines = exchanged(spectral)
    with jax.named_scope("phase_b_last"):
        ending = pl.pallas_call(
            functools.partial(last_phase_b, peers),
            in_specs=[pl.BlockSpec(memory_space=pltpu.SMEM)] * 2
            + whole_blocks(1)
            + in_hbm
            + whole_blocks(1),
            out_specs=pl.BlockSpec(memory_space=pltpu.VMEM),
            out_shape=spread_wire,
            scratch_shapes=[held, pltpu.VMEM((2, 96 * width, 128), jnp.float32)]
            + inverse_scratch,
            compiler_params=params,
        )(place, offsets, following, *map(in_place, inverse), lines)
    ending = lax.all_to_all(ending, MESH_AXES, 0, 0, tiled=True)
    with jax.named_scope("residual_end"):
        return pl.pallas_call(
            functools.partial(residual_end, peers),
            grid=(groups,),
            in_specs=[
                *whole_blocks(1),
                pl.BlockSpec((1,) + start_states.shape[1:], lambda b: (groups - 1, 0, 0, 0, 0)),
                *whole_blocks(1),
            ],
            out_specs=pl.BlockSpec((1,) + start_states.shape[1:], lambda b: (b, 0, 0, 0, 0)),
            out_shape=jax.ShapeDtypeStruct(start_states.shape, jnp.float32),
            scratch_shapes=[pltpu.VMEM((components * (axial_rows // 2), columns, 128), jnp.float32)],
            compiler_params=params,
        )(ending, start_states, following)


def solution(mesh):
    peers = tuple(mesh.shape[name] for name in MESH_AXES)

    def body(start_states, radial_inverse, offsets, mode_count):
        if fits(start_states.shape, peers):
            return half_body(peers, start_states, radial_inverse, offsets, mode_count)
        return general_body(start_states, radial_inverse, offsets, mode_count)

    placed = (P("seg", None, "ax", "rad", None), P("ax", None, None), P("seg"), P())
    return jax.shard_map(
        body,
        mesh=mesh,
        in_specs=placed,
        out_specs=P("seg", None, "ax", "rad", None),
        check_vma=False,
    )
```

```python
import functools
import math

import jax
import jax.numpy as jnp
import ml_dtypes
import numpy as np
from jax import lax
from jax.experimental import pallas as pl
from jax.experimental.pallas import tpu as pltpu
from jax.sharding import PartitionSpec as P

STEPS = 2
MESH_AXES = ("seg", "rad", "ax")
UNROLL = [12, 12, 16, 16, 8, 32, 16, 6]
VMEM_LIMIT = 24 * 1024 * 1024
FLOPS = 40_000_000_000

highest = lax.Precision.HIGHEST


def passed_along(value, axis, steps):
    count = lax.axis_size(axis)
    pairs = [(source, (source + steps) % count) for source in range(count)]
    return lax.ppermute(value, axis, pairs)


def padded_2(array, sides, width):
    for axis, dim in sides:
        peers, length = (lax.axis_size(axis), array.shape[dim])
        up = [(i, (i + 1) % peers) for i in range(peers)]
        down = [(j, i) for i, j in up]
        last = lax.slice_in_dim(array, length - width, length, axis=dim)
        leading = lax.slice_in_dim(array, 0, width, axis=dim)
        before = lax.ppermute(last, axis, up)
        after = lax.ppermute(leading, axis, down)
        array = jnp.concatenate([before, array, after], axis=dim)
    return array


def fourier_tables(columns, kept_modes):
    modes_total = columns // 2
    row_index = lax.broadcasted_iota(jnp.int32, (columns, columns), 0)
    point_index = lax.broadcasted_iota(jnp.int32, (columns, columns), 1)
    mode_index = row_index // 2
    phase = (mode_index * point_index % columns).astype(jnp.float32) * (2.0 * math.pi / columns)
    even_rows = row_index % 2 == 0
    cosine = jnp.cos(phase)
    sine = jnp.sin(phase)
    root = math.sqrt(modes_total)
    synthesis = jnp.where(even_rows, cosine, sine) / root
    weights = jnp.where(mode_index == 0, 1.0, 2.0)
    analysis = jnp.where(even_rows, weights * cosine, 2.0 * sine) * (root / columns)
    analysis = jnp.where(mode_index < kept_modes, analysis, 0.0)
    return (synthesis, analysis)


def radial_solve(pencils, radial_inverse, radial_rows):
    local_modes = radial_inverse.shape[0]
    local_columns, members, axial_cells, ignored = pencils.shape
    own_rows = lax.dynamic_slice_in_dim(
        radial_inverse, lax.axis_index("rad") * radial_rows, radial_rows, 1
    )
    piece = lax.all_gather(pencils, "rad", axis=3, tiled=True)
    piece_rows = piece.shape[3]
    grouped = piece.reshape(local_modes, 2, members, axial_cells, piece_rows)
    product = jnp.einsum("mrs,mkqzs->mkqzr", own_rows, grouped, precision=highest)
    return product.reshape(local_columns, members, axial_cells, radial_rows)


def general_body(start_states, radial_inverse, offsets, mode_count):
    groups, components, axial_rows, radial_rows, columns = start_states.shape
    synthesis, analysis = fourier_tables(columns, mode_count[0])
    radius = (
        (lax.axis_index("rad") * radial_rows + jnp.arange(radial_rows)).astype(jnp.float32) + 0.5
    ) / (radial_rows * lax.axis_size("rad"))
    profile = (1.0 - radius * radius).reshape(1, 1, 1, radial_rows, 1)
    following = passed_along(start_states[0], "seg", -1)
    current = start_states
    for step_index in range(STEPS):
        if step_index == 0:
            physical = jnp.einsum("gczrj,jp->gczrp", current, synthesis, precision=highest)
        else:
            physical = jnp.einsum("jgczr,jp->gczrp", current, synthesis, precision=highest)
        padded = padded_2(physical, (("ax", 2),), 1)
        gradient = (padded[:, :, 2:] - padded[:, :, :-2]) * 20.0
        advecting = profile + padded[:, 2:3, 1:-1]
        forcing = physical - 0.02 * advecting * gradient
        spectral = jnp.einsum("gczrp,jp->jgczr", forcing, analysis, precision=highest)
        pencils = lax.all_to_all(spectral, "ax", split_axis=0, concat_axis=3, tiled=True)
        local_columns = pencils.shape[0]
        axial_cells = pencils.shape[3]
        pencils = pencils.reshape(local_columns, groups * components, axial_cells, radial_rows)
        solved = radial_solve(pencils, radial_inverse, radial_rows)
        if step_index == STEPS - 1:
            blocks = solved.reshape(local_columns, groups, components, axial_cells, radial_rows)
            shifted = [
                jnp.roll(blocks[:, member], offsets[member], axis=2) for member in range(groups)
            ]
            solved = jnp.stack(shifted, axis=1).reshape(
                local_columns, groups * components, axial_cells, radial_rows
            )
        returned = lax.all_to_all(solved, "ax", split_axis=2, concat_axis=0, tiled=True)
        current = returned.reshape(columns, groups, components, axial_rows, radial_rows)
    ending = jnp.transpose(current, (1, 2, 3, 4, 0))
    upcoming = jnp.concatenate([start_states[1:], following[None]], axis=0)
    return ending - upcoming


def halves(high):
    top = high.astype(jnp.bfloat16)
    return top, (high - top.astype(jnp.float32)).astype(jnp.bfloat16)


def product(left, right, contract):
    return lax.dot_general(
        left, right, ((contract[:1], contract[1:]), ((), ())), preferred_element_type=jnp.float32
    )


def stacked_table(table):
    top = table.astype(ml_dtypes.bfloat16)
    rest = (table - top.astype(np.float64)).astype(ml_dtypes.bfloat16)
    return np.concatenate([top, top, rest], axis=1)


def column_order(columns, quarter_modes, shares):
    each = quarter_modes // shares
    order = []
    for share in range(shares):
        for low in range(2):
            for high in range(2):
                first = (2 * high + low) * quarter_modes + share * each
                order.extend(range(2 * first, 2 * (first + each)))
    assert sorted(order) == list(range(columns))
    return np.array(order)


def tables(columns, order):
    modes_total = columns // 2
    rows = np.arange(columns)
    mode = rows // 2
    phase = (mode[:, None] * np.arange(columns)[None, :]) % columns * (2.0 * np.pi / columns)
    even = (rows % 2 == 0)[:, None]
    root = math.sqrt(modes_total)
    synthesis = np.where(even, np.cos(phase), np.sin(phase)) / root
    weights = np.where(mode == 0, 1.0, 2.0)[:, None]
    analysis = np.where(even, weights * np.cos(phase), 2.0 * np.sin(phase)) * (root / columns)
    return (
        np.ascontiguousarray(stacked_table(synthesis.T).T),
        stacked_table(np.ascontiguousarray(synthesis.T[:, order])),
        stacked_table(analysis[order]),
        mode[order].astype(np.int32),
    )


def lane_index(block):
    return lax.broadcasted_iota(jnp.int32, block.shape, 1)


def spread(tiles, fourth):
    lane = lane_index(fourth)
    return [
        jnp.where(lane < 96, block, pltpu.roll(fourth, 96 - 32 * index, 1))
        for index, block in enumerate(tiles)
    ]


def gathered(waves):
    lane = lane_index(waves[0])
    fourth = jnp.where(lane < 32, pltpu.roll(waves[0], 32, 1), pltpu.roll(waves[1], 64, 1))
    return waves + [jnp.where(lane < 64, fourth, pltpu.roll(waves[2], 96, 1))]


def every(blocks, first, step):
    return jnp.concatenate(blocks[first::step], axis=0)


def pieces(block):
    return [block[at : at + 8] for at in range(0, block.shape[0], 8)]


def spread_list(blocks):
    whole = len(blocks) // 4 * 4
    quarters = [every(blocks[:whole], first, 4) for first in range(4)]
    full = [pieces(block) for block in spread(quarters[:3], quarters[3])]
    return [block for group in zip(*full) for block in group] + blocks[whole:]


def gathered_list(full, count):
    whole = count // 4 * 3
    blocks = [pieces(block) for block in gathered([every(full[:whole], i, 3) for i in range(3)])]
    return [block for group in zip(*blocks) for block in group] + full[whole:]


def lane_moves():
    lane = np.arange(128)
    moves = np.zeros((128, 256), np.float32)
    above = lane // 16 * 16 + (lane + 1) % 16
    below = lane // 16 * 16 + (lane + 15) % 16
    np.add.at(moves, (above, lane), 1.0)
    np.add.at(moves, (below, lane), -1.0)
    whole = lane[:96]
    moves[64 + whole % 32, 128 + whole] = 1.0
    return np.concatenate([moves, moves], axis=0).astype(ml_dtypes.bfloat16)


def physical_to_spectral(physical, profile, analysis, moves):
    lane = lane_index(physical[0])
    forcing = []
    for tile in range(3):
        field = physical[tile]
        moved = product(jnp.concatenate(halves(field), axis=1), moves, (1, 0))
        speed = jnp.where(lane < 96, moved[:, 128:], physical[2])
        forcing.append(field - 0.4 * (profile[tile : tile + 1] + speed) * moved[:, :128])
    forcing = jnp.concatenate(forcing, axis=1)
    top, rest = halves(forcing)
    return product(analysis, jnp.concatenate([top, rest, top], axis=0), (1, 0))


def write_spectral(spectral, count_ref, mode_ref, out_ref):
    members, ignored, width, ignored = out_ref.shape
    kept = mode_ref[...] < count_ref[0]
    for tile in range(3):
        block = jnp.where(kept, spectral[:, tile * 128 : (tile + 1) * 128], 0.0)
        out_ref[:, tile] = block.reshape(members, width, 128)


def pack_halos(start_ref, last_ref, leading_ref, sems):
    planes = start_ref.shape[2]
    copies = [
        pltpu.make_async_copy(start_ref.at[:, :, planes - 1], last_ref, sems.at[0]),
        pltpu.make_async_copy(start_ref.at[:, :, 0], leading_ref, sems.at[1]),
    ]
    for copy in copies:
        copy.start()
    for copy in copies:
        copy.wait()


def synthesized(rows, synthesis):
    top, rest = halves(jnp.concatenate(rows, axis=0))
    return product(jnp.concatenate([top, rest, top], axis=1), synthesis, (1, 0))


def own_physical(own_ref, synthesis_ref, out_ref):
    groups, components, planes, radii, columns = own_ref.shape
    rows = own_ref[...].reshape(groups * components * planes * radii, columns)
    out_ref[...] = synthesized([rows], synthesis_ref[...]).reshape(out_ref.shape)


def first_phase_a(
    count_ref,
    before_ref,
    own_ref,
    after_ref,
    synthesis_ref,
    analysis_ref,
    mode_ref,
    profile_ref,
    out_ref,
    held_ref,
):
    groups, components, planes, radii, columns = own_ref.shape
    strips = columns // 128
    count = groups * components
    sides = [ref[...].reshape(count * radii, columns) for ref in (before_ref, after_ref)]
    sides = synthesized(sides, synthesis_ref[...]).reshape(2, groups, components, radii, columns)
    profile = jnp.concatenate([profile_ref[...]] * strips, axis=1)
    for segment in range(groups):
        for plane in range(planes):
            speed = 0.4 * (profile + own_ref[segment, 2, plane])
            for component in range(components):
                line = [own_ref[segment, component, i] for i in range(planes)]
                line = [sides[0, segment, component], *line, sides[1, segment, component]]
                forcing = line[plane + 1] - speed * (line[plane + 2] - line[plane])
                first = (component * groups + segment) * radii * planes
                at = pl.ds(first + plane, radii, stride=planes)
                for strip in range(strips):
                    held_ref[strip, at, :] = forcing[:, strip * 128 : (strip + 1) * 128]
    quad = 4 * planes
    lines = []
    for strip in range(strips):
        parts = []
        for tile in range(3):
            for four, members in ((tile, range(components)), (3, (tile,))):
                for component in members:
                    for at in range(four * quad, (four + 1) * quad, quad // 2):
                        for segment in range(groups):
                            row = (component * groups + segment) * radii * planes + at
                            parts.append(held_ref[strip, row : row + quad // 2, :])
        lines.append(jnp.concatenate(parts, axis=0))
    top, rest = halves(jnp.concatenate(lines, axis=1))
    spectral = product(analysis_ref[...], jnp.concatenate([top, rest, top], axis=1), (1, 1))
    write_spectral(spectral, count_ref, mode_ref, out_ref)


def later_phase_a(
    count_ref,
    wire_ref,
    synthesis_ref,
    analysis_ref,
    mode_ref,
    profile_ref,
    moves_ref,
    out_ref,
    held_ref,
    physical_ref,
):
    sources, tiles, ignored, ignored = wire_ref.shape
    halves_of_ax, pairs, ignored, ignored = held_ref.shape
    parts = out_ref.shape[2] // 8

    def unpack():
        @pl.loop(0, sources, unroll=UNROLL[5])
        def _(source):
            half = lax.rem(source, 4) // 2
            member = source // 4 * 2 + lax.rem(source, 2)
            blocks = gathered_list(pieces(wire_ref[source].reshape(tiles * 8, 128)), pairs * parts)
            for part in range(parts):
                at = pl.ds(pl.multiple_of((member * parts + part) * 8, 8), 8)
                for pair in range(pairs):
                    held_ref[half, pair, at, :] = blocks[part * pairs + pair]

    def begin(group):
        radii = []
        for pair in range(2):
            one, two = (held_ref[half, 2 * group + pair] for half in range(halves_of_ax))
            low = lane_index(one) & 8 == 0
            radii.append(jnp.where(low, one, pltpu.roll(two, 8, 1)))
            radii.append(jnp.where(low, pltpu.roll(one, 120, 1), two))
        top, rest = halves(jnp.concatenate(spread(radii[:3], radii[3]), axis=1))
        physical_ref[group % 2] = product(
            synthesis_ref[...], jnp.concatenate([top, rest, top], axis=0), (1, 0)
        )

    def finish(group):
        physical = [physical_ref[group % 2, :, tile * 128 : (tile + 1) * 128] for tile in range(3)]
        spectral = physical_to_spectral(
            physical, profile_ref[group], analysis_ref[...], moves_ref[...]
        )
        write_spectral(spectral, count_ref, mode_ref, out_ref)

    for step in range(pairs // 2 + 1):

        @pl.when(pl.program_id(0) == step)
        def _(step=step):
            if step == 0:
                unpack()
            if step < pairs // 2:
                begin(step)
            if step > 0:
                finish(step - 1)


def quad_moves():
    moves = np.zeros((4, 128, 4, 128), np.float32)
    for source in range(4):
        for lane in range(96):
            block, two, segment, one, z = (
                lane // 32,
                lane // 16 % 2,
                lane // 8 % 2,
                lane // 4 % 2,
                lane % 4,
            )
            target = block * 32 + source // 2 * 16 + segment * 8 + source % 2 * 4 + z
            moves[source, lane, 2 * two + one, target] = 1.0
    return moves.reshape(512, 512).astype(ml_dtypes.bfloat16)


def unpack_quads(wire_ref, moves_ref, held_ref, peers):
    members, tiles, width, ignored = wire_ref.shape
    seg_places, rad_places, ignored = peers
    groups = tiles // 3

    @pl.loop(0, rad_places * groups, unroll=UNROLL[1])
    def _(index):
        rad, group = index // groups, lax.rem(index, groups)
        sources = [(s * rad_places + rad) * 2 + l for s in range(seg_places) for l in range(2)]
        waves = [
            jnp.concatenate([wire_ref[source, 3 * group + tile] for source in sources], axis=0)
            for tile in range(3)
        ]
        quads = gathered(waves)
        lines = [
            jnp.concatenate([quad[at : at + width] for quad in quads], axis=0)
            for at in range(0, 4 * width, width)
        ]
        top, rest = halves(jnp.concatenate(lines, axis=1))
        radii = product(top, moves_ref[...], (1, 0)) + product(rest, moves_ref[...], (1, 0))
        for place in range(4):
            for quad in range(4):
                at = pl.multiple_of((index * 16 + 4 * quad + place) * width, 8)
                held_ref[pl.ds(at, width), :] = radii[
                    quad * width : (quad + 1) * width, place * 128 : (place + 1) * 128
                ]


def first_radius(member, own):
    rad = lax.rem(member // 2, 4)
    return ((rad * 2 + member // 8) * 2 + lax.rem(member, 2)) * own


def unpack_radii(wire_ref, held_ref):
    members, tiles, width, ignored = wire_ref.shape
    own = tiles * 4 // 3

    @pl.loop(0, members, unroll=UNROLL[2])
    def _(member):
        first = first_radius(member, own)
        waves = [
            jnp.concatenate([wire_ref[member, at] for at in range(tile, tiles, 3)], axis=0)
            for tile in range(3)
        ]
        for index, block in enumerate(gathered(waves)):
            for group in range(tiles // 3):
                at = pl.multiple_of((first + 4 * group + index) * width, 8)
                held_ref[pl.ds(at, width), :] = block[group * width : (group + 1) * width]


def pack_sent(
    place_ref, offset_ref, inverse_ref, start_ref, out_ref, first_ref, held_ref, start_held_ref, sems
):
    each, radii, ignored = held_ref.shape
    copy = pltpu.make_async_copy(
        inverse_ref.at[pl.ds(place_ref[0] * each, each)], held_ref, sems.at[0]
    )
    copy.start()
    first = pltpu.make_async_copy(start_ref.at[0], start_held_ref, sems.at[1])
    first.start()
    rows = first_ref.shape[0] - 16
    for index in range(offset_ref.shape[0]):
        offset = offset_ref[index].astype(jnp.float32)
        first_ref[rows + index : rows + index + 1, :] = jnp.full((1, first_ref.shape[1]), offset)
    copy.wait()
    for index in range(each):
        out_ref[index] = held_ref[index, :, :128]
    for index in range(each // 2):
        out_ref[each + index, :, :64] = held_ref[index, :, 128:]
        out_ref[each + index, :, 64:] = held_ref[each // 2 + index, :, 128:]
    first.wait()
    first_ref[0:rows, :] = start_held_ref[...].reshape(rows, first_ref.shape[1])


def ordered_inverse(place_ref, own_ref, other_ref, top_ref, rest_ref):
    each = top_ref.shape[0] // 2
    first_half = place_ref[1] == 0

    def matrix(ref, index):
        side = index // (each // 2) * 64
        tail = ref[each + index % (each // 2), :, side : side + 64]
        return jnp.concatenate([ref[index], tail], axis=1)

    for index in range(each):
        here, there = matrix(own_ref, index), matrix(other_ref, index)
        top_ref[index], rest_ref[index] = halves(jnp.where(first_half, here, there))
        top_ref[each + index], rest_ref[each + index] = halves(jnp.where(first_half, there, here))


def inverse_copies(top_hbm, rest_hbm, top_ref, rest_ref, sems):
    copies = [
        pltpu.make_async_copy(source, target, sems.at[index])
        for index, (source, target) in enumerate(((top_hbm, top_ref), (rest_hbm, rest_ref)))
    ]
    for copy in copies:
        copy.start()
    return copies


def solved_modes(top_ref, rest_ref, held_ref, transposed, store):
    modes, radii, ignored = top_ref.shape
    width = 2 * modes

    @pl.loop(0, modes, unroll=UNROLL[0])
    def _(mode):
        matrix_top, matrix_rest = top_ref[mode], rest_ref[mode]
        state = jnp.concatenate(
            [held_ref[pl.ds(2 * mode + part, radii, stride=width), :] for part in range(2)], axis=1
        )
        if transposed:
            matrix_top, matrix_rest = (
                jnp.concatenate([m[:96], m[:32], m[96:], m[:32]], axis=0)
                for m in (matrix_top, matrix_rest)
            )
            top, rest = halves(state.T)
            solved = product(top, matrix_top, (1, 1))
            solved += product(rest, matrix_top, (1, 1)) + product(top, matrix_rest, (1, 1))
        else:
            top, rest = halves(state)
            solved = product(matrix_top, top, (1, 0))
            solved += product(matrix_top, rest, (1, 0)) + product(matrix_rest, top, (1, 0))
        store(mode, solved)


def phase_b(
    peers,
    top_hbm,
    rest_hbm,
    moves_hbm,
    wire_ref,
    out_ref,
    held_ref,
    solved_ref,
    moves_ref,
    top_ref,
    rest_ref,
    sems,
):
    members, tiles, width, ignored = wire_ref.shape
    radii = top_ref.shape[1]
    ax_places = peers[2]
    first = pltpu.make_async_copy(moves_hbm, moves_ref, sems.at[2])
    first.start()
    copies = inverse_copies(top_hbm, rest_hbm, top_ref, rest_ref, sems)
    first.wait()
    unpack_quads(wire_ref, moves_ref, held_ref, peers)
    for copy in copies:
        copy.wait()

    def store(mode, solved):
        for part in range(2):
            solved_ref[pl.ds(2 * mode + part, radii, stride=width), :] = solved[
                :, part * 128 : (part + 1) * 128
            ]

    solved_modes(top_ref, rest_ref, held_ref, False, store)
    own = radii // members
    low = lax.broadcasted_iota(jnp.int32, (own * width // 2, 128), 1) & 8 == 0

    @pl.loop(0, members, unroll=UNROLL[3])
    def _(member):
        place = first_radius(member, own) * width
        for half in range(2):
            one, two = (
                jnp.concatenate(
                    [
                        solved_ref[pl.ds(pl.multiple_of(place + index * width, 8), width), :]
                        for index in range(first, own, 2)
                    ],
                    axis=0,
                )
                for first in range(2)
            )
            if half == 0:
                blocks = pieces(jnp.where(low, one, pltpu.roll(two, 8, 1)))
            else:
                blocks = pieces(jnp.where(low, pltpu.roll(one, 120, 1), two))
            parts = width // 8
            split = [block for part in range(parts) for block in blocks[part::parts]]
            target = member // 2 * ax_places + 2 * half + lax.rem(member, 2)
            for index, block in enumerate(spread_list(split)):
                out_ref[target, index] = block


def last_phase_b(
    peers,
    place_ref,
    own_offset_ref,
    other_offset_ref,
    top_hbm,
    rest_hbm,
    wire_ref,
    out_ref,
    held_ref,
    solved_ref,
    top_ref,
    rest_ref,
    sems,
):
    members, tiles, width, ignored = wire_ref.shape
    radii = top_ref.shape[1]
    seg_places, rad_places, ax_places = peers
    planes = 16 // ax_places
    each = radii // rad_places
    half = place_ref[1]
    rows = other_offset_ref.shape[0] - 16
    others = [jnp.max(other_offset_ref[rows + i : rows + i + 1, :128]) for i in range(2)]
    other_offset = jnp.where(half == 0, *others).astype(jnp.int32)
    copies = inverse_copies(top_hbm, rest_hbm, top_ref, rest_ref, sems)
    unpack_radii(wire_ref, held_ref)
    for copy in copies:
        copy.wait()

    def store(mode, solved):
        for part in range(2):
            rows = pl.ds(2 * mode + part, 96, stride=width)
            block = solved[part * 128 : part * 128 + 96]
            for strip in range(2):
                solved_ref[strip, rows, :] = block[:, strip * 128 : (strip + 1) * 128]

    solved_modes(top_ref, rest_ref, held_ref, True, store)
    lane = lax.broadcasted_iota(jnp.int32, (planes // 2 * width, 128), 1)


    @pl.loop(0, seg_places * ax_places, unroll=UNROLL[4])
    def _(index):
        seg, ax = index // ax_places, lax.rem(index, ax_places)
        offset = jnp.where(place_ref[2] == seg, own_offset_ref[half], other_offset)
        blocks = {}
        for component in range(3):
            for plane in range(planes):
                source = lax.rem(ax * planes + plane - offset + 16, 16)
                row = (component * 32 + seg * 16 + source) * width
                row = pl.multiple_of(row, 8)
                blocks[component, plane] = row
        for rad in range(rad_places):
            parts = width // 8
            slots = []
            for component in range(3):
                sides = []
                for side in range(2):
                    rows = [
                        pl.ds(blocks[component, plane], width) for plane in range(side, planes, 2)
                    ]
                    lines = [solved_ref[rad // 2, at, :] for at in rows]
                    sides.append(jnp.concatenate(lines, axis=0))
                if rad % 2 == 0:
                    sides[1] = pltpu.roll(sides[1], each, 1)
                else:
                    sides[0] = pltpu.roll(sides[0], 128 - each, 1)
                slots += pieces(jnp.where(lane < each, *sides))
            split = [block for part in range(parts) for block in slots[part::parts]]
            target = (seg * rad_places + rad) * ax_places + ax
            for at, block in enumerate(spread_list(split)):
                out_ref[target, at] = block


def residual_end(peers, wire_ref, start_ref, following_ref, out_ref, held_ref):
    seg_places, rad_places, ax_places = peers
    ignored, components, planes, each, columns = out_ref.shape
    shares = seg_places * rad_places
    width = columns // (2 * shares)
    chunk = width // 2
    count = (width // 8) * components * (planes // 2)
    slots = components * (planes // 2)
    half = pl.program_id(0)

    @pl.loop(0, 2 * shares, unroll=UNROLL[6])
    def _(member):
        share, low = member // 2, lax.rem(member, 2)
        source = share * ax_places + 2 * half + low
        split = gathered_list(pieces(wire_ref[source].reshape(-1, 128)), count)
        for slot in range(slots):
            parts = [split[part * slots + slot] for part in range(width // 8)]
            rows = jnp.concatenate(parts, axis=0)
            for high in range(2):
                at = (2 * high + low) * (columns // 4) + share * chunk
                held_ref[slot, pl.ds(at, chunk), :] = rows[high * chunk : (high + 1) * chunk]

    @pl.loop(0, slots, unroll=UNROLL[7])
    def _(slot):
        component, pair = slot // (planes // 2), lax.rem(slot, planes // 2)
        ending = held_ref[slot, :columns].T
        for side in range(2):
            plane = 2 * pair + side
            row = pl.multiple_of((component * planes + plane) * each, 8)
            upcoming = jnp.where(
                half + 1 < pl.num_programs(0),
                start_ref[0, component, plane],
                following_ref[pl.ds(row, each), :],
            )
            out_ref[0, component, plane] = ending[side * each : (side + 1) * each] - upcoming


def in_place(value):
    return pltpu.with_memory_space_constraint(value, pltpu.HBM)


def whole_blocks(count):
    return [pl.BlockSpec(memory_space=pltpu.VMEM)] * count


def fits(shape, peers):
    groups, components, axial_rows, radial_rows, columns = shape
    seg_places, rad_places, ax_places = peers
    members = seg_places * rad_places * 2
    return (
        (groups, components, seg_places, ax_places) == (2, 3, 2, 4)
        and axial_rows * ax_places == 16
        and radial_rows == 48
        and rad_places * radial_rows == 192
        and columns == 384
        and members == 16
    )


def half_body(peers, start_states, radial_inverse, offsets, mode_count):
    groups, components, axial_rows, radial_rows, columns = start_states.shape
    seg_places, rad_places, ax_places = peers
    axial = axial_rows * ax_places
    radii = radial_rows * rad_places
    shares = seg_places * rad_places
    members = 2 * shares
    own_radii = radii // members
    own_modes = radial_inverse.shape[0] // shares
    width = columns // members
    tiles = own_radii * 3 // 4
    order = column_order(columns, radial_inverse.shape[0], shares)
    synthesis_natural, synthesis, analysis, mode_of_row = tables(columns, order)

    seg, rad, ax = (lax.axis_index(name) for name in MESH_AXES)
    half, low = ax // 2, ax % 2

    def device(s, r, a):
        return (s * rad_places + r) * ax_places + a

    half_groups = [
        [
            device(s, r, 2 * h + l)
            for s in range(seg_places)
            for r in range(rad_places)
            for l in range(2)
        ]
        for h in range(2)
    ]
    mirror = [(a, (a + 2) % 4) for a in range(4)]
    params = pltpu.CompilerParams(vmem_limit_bytes=VMEM_LIMIT)
    up = [(i, (i + 1) % ax_places) for i in range(ax_places)]
    down = [(j, i) for i, j in up]
    halo = jax.ShapeDtypeStruct((groups, components, radial_rows, columns), jnp.float32)
    with jax.named_scope("pack_halos"):
        last, leading = pl.pallas_call(
            pack_halos,
            in_specs=[pl.BlockSpec(memory_space=pltpu.HBM)],
            out_specs=whole_blocks(2),
            out_shape=[halo, halo],
            scratch_shapes=[pltpu.SemaphoreType.DMA((2,))],
            compiler_params=params,
        )(in_place(start_states))
    before = lax.ppermute(last, "ax", up)
    after = lax.ppermute(leading, "ax", down)

    share = seg * rad_places + rad
    place = jnp.stack([share, half, seg]).astype(jnp.int32)
    first_rows = components * axial_rows * radial_rows
    with jax.named_scope("pack_sent"):
        dense_inverse, first_start = pl.pallas_call(
            pack_sent,
            in_specs=[
                pl.BlockSpec(memory_space=pltpu.SMEM),
                pl.BlockSpec(memory_space=pltpu.SMEM),
                pl.BlockSpec(memory_space=pltpu.HBM),
                pl.BlockSpec(memory_space=pltpu.HBM),
            ],
            out_specs=whole_blocks(2),
            out_shape=[
                jax.ShapeDtypeStruct((own_modes * 3 // 2, radii, 128), jnp.float32),
                jax.ShapeDtypeStruct((first_rows + 16, columns), jnp.float32),
            ],
            scratch_shapes=[
                pltpu.VMEM((own_modes, radii, radii), jnp.float32),
                pltpu.VMEM(start_states.shape[1:], jnp.float32),
                pltpu.SemaphoreType.DMA((2,)),
            ],
            compiler_params=params,
        )(place, offsets, in_place(radial_inverse), in_place(start_states))
    first = rad * radial_rows + (seg * 2 + low) * own_radii
    tile_index = np.arange(tiles)[:, None]
    lane = np.arange(128)[None, :]
    local = 4 * (tile_index // 3) + np.where(lane < 96, tile_index % 3, 3)
    radius = ((first + jnp.asarray(local)).astype(jnp.float32) + 0.5) / radii
    profile = (1.0 - radius * radius).reshape(tiles // 3, 3, 128)

    own_radius = ((rad * radial_rows + jnp.arange(radial_rows)).astype(jnp.float32) + 0.5) / radii
    own_profile = jnp.broadcast_to((1.0 - own_radius * own_radius)[:, None], (radial_rows, 128))

    synthesis_natural, synthesis, analysis = (
        jnp.asarray(table) for table in (synthesis_natural, synthesis, analysis)
    )
    mode_rows = jnp.asarray(np.repeat(mode_of_row[:, None], 128, axis=1))
    wire = jax.ShapeDtypeStruct((members, tiles, width, 128), jnp.float32)
    wire_spec = pl.BlockSpec((members, 3, width, 128), lambda g: (0, g, 0, 0))
    held = pltpu.VMEM((radii * width, 128), jnp.float32)
    count = (width // 8) * components * (axial_rows // 2)
    end_tiles = (count // 4) * 3 + count % 4
    everyone = seg_places * rad_places * ax_places
    spread_wire = jax.ShapeDtypeStruct((everyone, end_tiles, 8, 128), jnp.float32)

    def exchanged(value):
        return lax.all_to_all(
            value, MESH_AXES, 0, 0, axis_index_groups=half_groups, tiled=True
        )

    step = radial_rows // 3
    halo_spec = pl.BlockSpec((groups, components, step, columns), lambda g: (0, 0, g, 0))
    own_spec = pl.BlockSpec(
        (groups, components, axial_rows, step, columns), lambda g: (0, 0, 0, g, 0)
    )
    with jax.named_scope("own_physical"):
        physical = pl.pallas_call(
            own_physical,
            grid=(3,),
            in_specs=[own_spec] + whole_blocks(1),
            out_specs=own_spec,
            out_shape=jax.ShapeDtypeStruct(start_states.shape, jnp.float32),
            compiler_params=params,
        )(start_states, synthesis_natural)
    before, after, dense_inverse, physical, profile, own_profile = lax.optimization_barrier(
        (before, after, dense_inverse, physical, profile, own_profile)
    )
    other_inverse = lax.ppermute(dense_inverse, "ax", mirror)
    with jax.named_scope("phase_a_first"):
        spectral = pl.pallas_call(
            first_phase_a,
            grid=(3,),
            in_specs=[
                pl.BlockSpec(memory_space=pltpu.SMEM),
                halo_spec,
                own_spec,
                halo_spec,
                *whole_blocks(3),
                pl.BlockSpec((step, 128), lambda g: (g, 0)),
            ],
            out_specs=wire_spec,
            out_shape=pltpu.HBM(wire.shape, wire.dtype),
            scratch_shapes=[
                pltpu.VMEM(
                    (columns // 128, groups * components * axial_rows * step, 128), jnp.float32
                )
            ],
            compiler_params=params,
        )(
            mode_count,
            before,
            physical,
            after,
            synthesis_natural,
            analysis,
            mode_rows,
            own_profile,
        )
    matrices = jax.ShapeDtypeStruct((2 * own_modes, radii, radii), jnp.bfloat16)
    in_hbm = [pl.BlockSpec(memory_space=pltpu.HBM)] * 2
    inverse_scratch = [pltpu.VMEM(matrices.shape, matrices.dtype)] * 2
    inverse_scratch += [pltpu.SemaphoreType.DMA((3,))]
    with jax.named_scope("ordered_inverse"):
        inverse = pl.pallas_call(
            ordered_inverse,
            in_specs=[pl.BlockSpec(memory_space=pltpu.SMEM)] + whole_blocks(2),
            out_specs=[pl.BlockSpec(matrices.shape, lambda: (0, 0, 0))] * 2,
            out_shape=[pltpu.HBM(matrices.shape, matrices.dtype)] * 2,
            compiler_params=params,
            cost_estimate=pl.CostEstimate(
                flops=FLOPS, bytes_accessed=16 * own_modes * radii * radii, transcendentals=0
            ),
        )(place, dense_inverse, other_inverse)
    spectral, first_start = lax.optimization_barrier((spectral, first_start))
    following = passed_along(first_start, "seg", -1)
    lines = exchanged(spectral)
    moves = jnp.asarray(quad_moves())
    with jax.named_scope("phase_b_first"):
        solved = pl.pallas_call(
            functools.partial(phase_b, peers),
            in_specs=in_hbm + [pl.BlockSpec(memory_space=pltpu.HBM)] + whole_blocks(1),
            out_specs=pl.BlockSpec(memory_space=pltpu.VMEM),
            out_shape=spread_wire,
            scratch_shapes=[held, held, pltpu.VMEM(moves.shape, moves.dtype)] + inverse_scratch,
            compiler_params=params,
        )(*map(in_place, (*inverse, moves)), lines)
    solved, following = lax.optimization_barrier((solved, following))
    state = lax.all_to_all(solved, MESH_AXES, 0, 0, tiled=True)
    with jax.named_scope("phase_a_later"):
        spectral = pl.pallas_call(
            later_phase_a,
            grid=(tiles // 3 + 1,),
            in_specs=[
                pl.BlockSpec(memory_space=pltpu.SMEM),
                *whole_blocks(6),
            ],
            out_specs=pl.BlockSpec(
                wire_spec.block_shape, lambda g: (0, jnp.maximum(g - 1, 0), 0, 0)
            ),
            out_shape=wire,
            scratch_shapes=[
                pltpu.VMEM((2, own_radii // 2, columns, 128), jnp.float32),
                pltpu.VMEM((2, columns, 3 * 128), jnp.float32),
            ],
            compiler_params=params,
        )(mode_count, state, synthesis, analysis, mode_rows, profile, jnp.asarray(lane_moves()))
    lines = exchanged(spectral)
    with jax.named_scope("phase_b_last"):
        ending = pl.pallas_call(
            functools.partial(last_phase_b, peers),
            in_specs=[pl.BlockSpec(memory_space=pltpu.SMEM)] * 2
            + whole_blocks(1)
            + in_hbm
            + whole_blocks(1),
            out_specs=pl.BlockSpec(memory_space=pltpu.VMEM),
            out_shape=spread_wire,
            scratch_shapes=[held, pltpu.VMEM((2, 96 * width, 128), jnp.float32)]
            + inverse_scratch,
            compiler_params=params,
        )(place, offsets, following, *map(in_place, inverse), lines)
    ending = lax.all_to_all(ending, MESH_AXES, 0, 0, tiled=True)
    with jax.named_scope("residual_end"):
        return pl.pallas_call(
            functools.partial(residual_end, peers),
            grid=(groups,),
            in_specs=[
                *whole_blocks(1),
                pl.BlockSpec((1,) + start_states.shape[1:], lambda b: (groups - 1, 0, 0, 0, 0)),
                *whole_blocks(1),
            ],
            out_specs=pl.BlockSpec((1,) + start_states.shape[1:], lambda b: (b, 0, 0, 0, 0)),
            out_shape=jax.ShapeDtypeStruct(start_states.shape, jnp.float32),
            scratch_shapes=[
                pltpu.VMEM((components * (axial_rows // 2), columns + 8, 128), jnp.float32)
            ],
            compiler_params=params,
        )(ending, start_states, following)


def solution(mesh):
    peers = tuple(mesh.shape[name] for name in MESH_AXES)

    def body(start_states, radial_inverse, offsets, mode_count):
        if fits(start_states.shape, peers):
            return half_body(peers, start_states, radial_inverse, offsets, mode_count)
        return general_body(start_states, radial_inverse, offsets, mode_count)

    placed = (P("seg", None, "ax", "rad", None), P("ax", None, None), P("seg"), P())
    return jax.shard_map(
        body,
        mesh=mesh,
        in_specs=placed,
        out_specs=P("seg", None, "ax", "rad", None),
        check_vma=False,
    )
```

```python
import functools
import math

import jax
import jax.numpy as jnp
import ml_dtypes
import numpy as np
from jax import lax
from jax.experimental import pallas as pl
from jax.experimental.pallas import tpu as pltpu
from jax.sharding import PartitionSpec as P

STEPS = 2
MESH_AXES = ("seg", "rad", "ax")
UNROLL = [12, 12, 16, 16, 8, 32, 16, 6]
VMEM_LIMIT = 24 * 1024 * 1024
FLOPS = 40_000_000_000

highest = lax.Precision.HIGHEST


def passed_along(value, axis, steps):
    count = lax.axis_size(axis)
    pairs = [(source, (source + steps) % count) for source in range(count)]
    return lax.ppermute(value, axis, pairs)


def padded_2(array, sides, width):
    for axis, dim in sides:
        peers, length = (lax.axis_size(axis), array.shape[dim])
        up = [(i, (i + 1) % peers) for i in range(peers)]
        down = [(j, i) for i, j in up]
        last = lax.slice_in_dim(array, length - width, length, axis=dim)
        leading = lax.slice_in_dim(array, 0, width, axis=dim)
        before = lax.ppermute(last, axis, up)
        after = lax.ppermute(leading, axis, down)
        array = jnp.concatenate([before, array, after], axis=dim)
    return array


def fourier_tables(columns, kept_modes):
    modes_total = columns // 2
    row_index = lax.broadcasted_iota(jnp.int32, (columns, columns), 0)
    point_index = lax.broadcasted_iota(jnp.int32, (columns, columns), 1)
    mode_index = row_index // 2
    phase = (mode_index * point_index % columns).astype(jnp.float32) * (2.0 * math.pi / columns)
    even_rows = row_index % 2 == 0
    cosine = jnp.cos(phase)
    sine = jnp.sin(phase)
    root = math.sqrt(modes_total)
    synthesis = jnp.where(even_rows, cosine, sine) / root
    weights = jnp.where(mode_index == 0, 1.0, 2.0)
    analysis = jnp.where(even_rows, weights * cosine, 2.0 * sine) * (root / columns)
    analysis = jnp.where(mode_index < kept_modes, analysis, 0.0)
    return (synthesis, analysis)


def radial_solve(pencils, radial_inverse, radial_rows):
    local_modes = radial_inverse.shape[0]
    local_columns, members, axial_cells, ignored = pencils.shape
    own_rows = lax.dynamic_slice_in_dim(
        radial_inverse, lax.axis_index("rad") * radial_rows, radial_rows, 1
    )
    piece = lax.all_gather(pencils, "rad", axis=3, tiled=True)
    piece_rows = piece.shape[3]
    grouped = piece.reshape(local_modes, 2, members, axial_cells, piece_rows)
    product = jnp.einsum("mrs,mkqzs->mkqzr", own_rows, grouped, precision=highest)
    return product.reshape(local_columns, members, axial_cells, radial_rows)


def general_body(start_states, radial_inverse, offsets, mode_count):
    groups, components, axial_rows, radial_rows, columns = start_states.shape
    synthesis, analysis = fourier_tables(columns, mode_count[0])
    radius = (
        (lax.axis_index("rad") * radial_rows + jnp.arange(radial_rows)).astype(jnp.float32) + 0.5
    ) / (radial_rows * lax.axis_size("rad"))
    profile = (1.0 - radius * radius).reshape(1, 1, 1, radial_rows, 1)
    following = passed_along(start_states[0], "seg", -1)
    current = start_states
    for step_index in range(STEPS):
        if step_index == 0:
            physical = jnp.einsum("gczrj,jp->gczrp", current, synthesis, precision=highest)
        else:
            physical = jnp.einsum("jgczr,jp->gczrp", current, synthesis, precision=highest)
        padded = padded_2(physical, (("ax", 2),), 1)
        gradient = (padded[:, :, 2:] - padded[:, :, :-2]) * 20.0
        advecting = profile + padded[:, 2:3, 1:-1]
        forcing = physical - 0.02 * advecting * gradient
        spectral = jnp.einsum("gczrp,jp->jgczr", forcing, analysis, precision=highest)
        pencils = lax.all_to_all(spectral, "ax", split_axis=0, concat_axis=3, tiled=True)
        local_columns = pencils.shape[0]
        axial_cells = pencils.shape[3]
        pencils = pencils.reshape(local_columns, groups * components, axial_cells, radial_rows)
        solved = radial_solve(pencils, radial_inverse, radial_rows)
        if step_index == STEPS - 1:
            blocks = solved.reshape(local_columns, groups, components, axial_cells, radial_rows)
            shifted = [
                jnp.roll(blocks[:, member], offsets[member], axis=2) for member in range(groups)
            ]
            solved = jnp.stack(shifted, axis=1).reshape(
                local_columns, groups * components, axial_cells, radial_rows
            )
        returned = lax.all_to_all(solved, "ax", split_axis=2, concat_axis=0, tiled=True)
        current = returned.reshape(columns, groups, components, axial_rows, radial_rows)
    ending = jnp.transpose(current, (1, 2, 3, 4, 0))
    upcoming = jnp.concatenate([start_states[1:], following[None]], axis=0)
    return ending - upcoming


def halves(high):
    top = high.astype(jnp.bfloat16)
    return top, (high - top.astype(jnp.float32)).astype(jnp.bfloat16)


def product(left, right, contract):
    return lax.dot_general(
        left, right, ((contract[:1], contract[1:]), ((), ())), preferred_element_type=jnp.float32
    )


def stacked_table(table):
    top = table.astype(ml_dtypes.bfloat16)
    rest = (table - top.astype(np.float64)).astype(ml_dtypes.bfloat16)
    return np.concatenate([top, top, rest], axis=1)


def column_order(columns, quarter_modes, shares):
    each = quarter_modes // shares
    order = []
    for share in range(shares):
        for low in range(2):
            for high in range(2):
                first = (2 * high + low) * quarter_modes + share * each
                order.extend(range(2 * first, 2 * (first + each)))
    assert sorted(order) == list(range(columns))
    return np.array(order)


def tables(columns, order):
    modes_total = columns // 2
    rows = np.arange(columns)
    mode = rows // 2
    phase = (mode[:, None] * np.arange(columns)[None, :]) % columns * (2.0 * np.pi / columns)
    even = (rows % 2 == 0)[:, None]
    root = math.sqrt(modes_total)
    synthesis = np.where(even, np.cos(phase), np.sin(phase)) / root
    weights = np.where(mode == 0, 1.0, 2.0)[:, None]
    analysis = np.where(even, weights * np.cos(phase), 2.0 * np.sin(phase)) * (root / columns)
    return (
        np.ascontiguousarray(stacked_table(synthesis.T).T),
        stacked_table(np.ascontiguousarray(synthesis.T[:, order])),
        stacked_table(analysis[order]),
        mode[order].astype(np.int32),
    )


def lane_index(block):
    return lax.broadcasted_iota(jnp.int32, block.shape, 1)


def spread(tiles, fourth):
    lane = lane_index(fourth)
    return [
        jnp.where(lane < 96, block, pltpu.roll(fourth, 96 - 32 * index, 1))
        for index, block in enumerate(tiles)
    ]


def gathered(waves):
    lane = lane_index(waves[0])
    fourth = jnp.where(lane < 32, pltpu.roll(waves[0], 32, 1), pltpu.roll(waves[1], 64, 1))
    return waves + [jnp.where(lane < 64, fourth, pltpu.roll(waves[2], 96, 1))]


def every(blocks, first, step):
    return jnp.concatenate(blocks[first::step], axis=0)


def pieces(block):
    return [block[at : at + 8] for at in range(0, block.shape[0], 8)]


def spread_list(blocks):
    whole = len(blocks) // 4 * 4
    quarters = [every(blocks[:whole], first, 4) for first in range(4)]
    full = [pieces(block) for block in spread(quarters[:3], quarters[3])]
    return [block for group in zip(*full) for block in group] + blocks[whole:]


def gathered_list(full, count):
    whole = count // 4 * 3
    blocks = [pieces(block) for block in gathered([every(full[:whole], i, 3) for i in range(3)])]
    return [block for group in zip(*blocks) for block in group] + full[whole:]


def lane_moves():
    lane = np.arange(128)
    moves = np.zeros((128, 256), np.float32)
    above = lane // 16 * 16 + (lane + 1) % 16
    below = lane // 16 * 16 + (lane + 15) % 16
    np.add.at(moves, (above, lane), 1.0)
    np.add.at(moves, (below, lane), -1.0)
    whole = lane[:96]
    moves[64 + whole % 32, 128 + whole] = 1.0
    return np.concatenate([moves, moves], axis=0).astype(ml_dtypes.bfloat16)


def physical_to_spectral(physical, profile, analysis, moves):
    lane = lane_index(physical[0])
    forcing = []
    for tile in range(3):
        field = physical[tile]
        moved = product(jnp.concatenate(halves(field), axis=1), moves, (1, 0))
        speed = jnp.where(lane < 96, moved[:, 128:], physical[2])
        forcing.append(field - 0.4 * (profile[tile : tile + 1] + speed) * moved[:, :128])
    forcing = jnp.concatenate(forcing, axis=1)
    top, rest = halves(forcing)
    return product(analysis, jnp.concatenate([top, rest, top], axis=0), (1, 0))


def write_spectral(spectral, count_ref, mode_ref, out_ref):
    members, ignored, width, ignored = out_ref.shape
    kept = mode_ref[...] < count_ref[0]
    for tile in range(3):
        block = jnp.where(kept, spectral[:, tile * 128 : (tile + 1) * 128], 0.0)
        out_ref[:, tile] = block.reshape(members, width, 128)


def pack_halos(start_ref, last_ref, leading_ref, sems):
    planes = start_ref.shape[2]
    copies = [
        pltpu.make_async_copy(start_ref.at[:, :, planes - 1], last_ref, sems.at[0]),
        pltpu.make_async_copy(start_ref.at[:, :, 0], leading_ref, sems.at[1]),
    ]
    for copy in copies:
        copy.start()
    for copy in copies:
        copy.wait()


def synthesized(rows, synthesis):
    top, rest = halves(jnp.concatenate(rows, axis=0))
    return product(jnp.concatenate([top, rest, top], axis=1), synthesis, (1, 0))


def own_physical(own_ref, synthesis_ref, out_ref):
    groups, components, planes, radii, columns = own_ref.shape
    rows = own_ref[...].reshape(groups * components * planes * radii, columns)
    out_ref[...] = synthesized([rows], synthesis_ref[...]).reshape(out_ref.shape)


def first_phase_a(
    count_ref,
    before_ref,
    own_ref,
    after_ref,
    synthesis_ref,
    analysis_ref,
    mode_ref,
    profile_ref,
    out_ref,
    held_ref,
):
    groups, components, planes, radii, columns = own_ref.shape
    strips = columns // 128
    count = groups * components
    quad = 4 * planes

    def begin(step):
        sides = [ref[...].reshape(count * radii, columns) for ref in (before_ref, after_ref)]
        sides = synthesized(sides, synthesis_ref[...])
        sides = sides.reshape(2, groups, components, radii, columns)
        profile = jnp.concatenate([profile_ref[...]] * strips, axis=1)
        for segment in range(groups):
            for plane in range(planes):
                speed = 0.4 * (profile + own_ref[segment, 2, plane])
                for component in range(components):
                    line = [own_ref[segment, component, i] for i in range(planes)]
                    line = [sides[0, segment, component], *line, sides[1, segment, component]]
                    forcing = line[plane + 1] - speed * (line[plane + 2] - line[plane])
                    first = (component * groups + segment) * radii * planes
                    at = pl.ds(first + plane, radii, stride=planes)
                    for strip in range(strips):
                        held_ref[step % 2, strip, at, :] = forcing[
                            :, strip * 128 : (strip + 1) * 128
                        ]

    def finish(step):
        lines = []
        for strip in range(strips):
            parts = []
            for tile in range(3):
                for four, members in ((tile, range(components)), (3, (tile,))):
                    for component in members:
                        for at in range(four * quad, (four + 1) * quad, quad // 2):
                            for segment in range(groups):
                                row = (component * groups + segment) * radii * planes + at
                                parts.append(
                                    held_ref[step % 2, strip, row : row + quad // 2, :]
                                )
            lines.append(jnp.concatenate(parts, axis=0))
        top, rest = halves(jnp.concatenate(lines, axis=1))
        spectral = product(analysis_ref[...], jnp.concatenate([top, rest, top], axis=1), (1, 1))
        write_spectral(spectral, count_ref, mode_ref, out_ref)

    steps = out_ref.shape[2] // 8
    for step in range(steps + 1):

        @pl.when(pl.program_id(0) == step)
        def _(step=step):
            if step < steps:
                begin(step)
            if step > 0:
                finish(step - 1)


def later_phase_a(
    count_ref,
    wire_ref,
    synthesis_ref,
    analysis_ref,
    mode_ref,
    profile_ref,
    moves_ref,
    out_ref,
    held_ref,
    physical_ref,
):
    sources, tiles, ignored, ignored = wire_ref.shape
    halves_of_ax, pairs, ignored, ignored = held_ref.shape
    parts = out_ref.shape[2] // 8

    def unpack():
        @pl.loop(0, sources, unroll=UNROLL[5])
        def _(source):
            half = lax.rem(source, 4) // 2
            member = source // 4 * 2 + lax.rem(source, 2)
            blocks = gathered_list(pieces(wire_ref[source].reshape(tiles * 8, 128)), pairs * parts)
            for part in range(parts):
                at = pl.ds(pl.multiple_of((member * parts + part) * 8, 8), 8)
                for pair in range(pairs):
                    held_ref[half, pair, at, :] = blocks[part * pairs + pair]

    def begin(group):
        radii = []
        for pair in range(2):
            one, two = (held_ref[half, 2 * group + pair] for half in range(halves_of_ax))
            low = lane_index(one) & 8 == 0
            radii.append(jnp.where(low, one, pltpu.roll(two, 8, 1)))
            radii.append(jnp.where(low, pltpu.roll(one, 120, 1), two))
        top, rest = halves(jnp.concatenate(spread(radii[:3], radii[3]), axis=1))
        physical_ref[group % 2] = product(
            synthesis_ref[...], jnp.concatenate([top, rest, top], axis=0), (1, 0)
        )

    def finish(group):
        physical = [physical_ref[group % 2, :, tile * 128 : (tile + 1) * 128] for tile in range(3)]
        spectral = physical_to_spectral(
            physical, profile_ref[group], analysis_ref[...], moves_ref[...]
        )
        write_spectral(spectral, count_ref, mode_ref, out_ref)

    for step in range(pairs // 2 + 1):

        @pl.when(pl.program_id(0) == step)
        def _(step=step):
            if step == 0:
                unpack()
            if step < pairs // 2:
                begin(step)
            if step > 0:
                finish(step - 1)


def quad_moves():
    moves = np.zeros((4, 128, 4, 128), np.float32)
    for source in range(4):
        for lane in range(96):
            block, two, segment, one, z = (
                lane // 32,
                lane // 16 % 2,
                lane // 8 % 2,
                lane // 4 % 2,
                lane % 4,
            )
            target = block * 32 + source // 2 * 16 + segment * 8 + source % 2 * 4 + z
            moves[source, lane, 2 * two + one, target] = 1.0
    return moves.reshape(512, 512).astype(ml_dtypes.bfloat16)


def unpack_quads(wire_ref, moves_ref, held_ref, peers):
    members, tiles, width, ignored = wire_ref.shape
    seg_places, rad_places, ignored = peers
    groups = tiles // 3

    @pl.loop(0, rad_places * groups, unroll=UNROLL[1])
    def _(index):
        rad, group = index // groups, lax.rem(index, groups)
        sources = [(s * rad_places + rad) * 2 + l for s in range(seg_places) for l in range(2)]
        waves = [
            jnp.concatenate([wire_ref[source, 3 * group + tile] for source in sources], axis=0)
            for tile in range(3)
        ]
        quads = gathered(waves)
        lines = [
            jnp.concatenate([quad[at : at + width] for quad in quads], axis=0)
            for at in range(0, 4 * width, width)
        ]
        top, rest = halves(jnp.concatenate(lines, axis=1))
        radii = product(top, moves_ref[...], (1, 0)) + product(rest, moves_ref[...], (1, 0))
        for place in range(4):
            for quad in range(4):
                at = pl.multiple_of((index * 16 + 4 * quad + place) * width, 8)
                held_ref[pl.ds(at, width), :] = radii[
                    quad * width : (quad + 1) * width, place * 128 : (place + 1) * 128
                ]


def first_radius(member, own):
    rad = lax.rem(member // 2, 4)
    return ((rad * 2 + member // 8) * 2 + lax.rem(member, 2)) * own


def unpack_radii(wire_ref, held_ref):
    members, tiles, width, ignored = wire_ref.shape
    own = tiles * 4 // 3

    @pl.loop(0, members, unroll=UNROLL[2])
    def _(member):
        first = first_radius(member, own)
        waves = [
            jnp.concatenate([wire_ref[member, at] for at in range(tile, tiles, 3)], axis=0)
            for tile in range(3)
        ]
        for index, block in enumerate(gathered(waves)):
            for group in range(tiles // 3):
                at = pl.multiple_of((first + 4 * group + index) * width, 8)
                held_ref[pl.ds(at, width), :] = block[group * width : (group + 1) * width]


def pack_sent(
    place_ref, offset_ref, inverse_ref, start_ref, out_ref, first_ref, held_ref, start_held_ref, sems
):
    each, radii, ignored = held_ref.shape
    copy = pltpu.make_async_copy(
        inverse_ref.at[pl.ds(place_ref[0] * each, each)], held_ref, sems.at[0]
    )
    copy.start()
    first = pltpu.make_async_copy(start_ref.at[0], start_held_ref, sems.at[1])
    first.start()
    rows = first_ref.shape[0] - 16
    for index in range(offset_ref.shape[0]):
        offset = offset_ref[index].astype(jnp.float32)
        first_ref[rows + index : rows + index + 1, :] = jnp.full((1, first_ref.shape[1]), offset)
    copy.wait()
    for index in range(each):
        out_ref[index] = held_ref[index, :, :128]
    for index in range(each // 2):
        out_ref[each + index, :, :64] = held_ref[index, :, 128:]
        out_ref[each + index, :, 64:] = held_ref[each // 2 + index, :, 128:]
    first.wait()
    first_ref[0:rows, :] = start_held_ref[...].reshape(rows, first_ref.shape[1])


def ordered_inverse(place_ref, own_ref, other_ref, top_ref, rest_ref):
    each = top_ref.shape[0] // 2
    first_half = place_ref[1] == 0

    def matrix(ref, index):
        side = index // (each // 2) * 64
        tail = ref[each + index % (each // 2), :, side : side + 64]
        return jnp.concatenate([ref[index], tail], axis=1)

    for index in range(each):
        here, there = matrix(own_ref, index), matrix(other_ref, index)
        top_ref[index], rest_ref[index] = halves(jnp.where(first_half, here, there))
        top_ref[each + index], rest_ref[each + index] = halves(jnp.where(first_half, there, here))


def inverse_copies(top_hbm, rest_hbm, top_ref, rest_ref, sems):
    copies = [
        pltpu.make_async_copy(source, target, sems.at[index])
        for index, (source, target) in enumerate(((top_hbm, top_ref), (rest_hbm, rest_ref)))
    ]
    for copy in copies:
        copy.start()
    return copies


def solved_modes(top_ref, rest_ref, held_ref, transposed, store):
    modes, radii, ignored = top_ref.shape
    width = 2 * modes

    @pl.loop(0, modes, unroll=UNROLL[0])
    def _(mode):
        matrix_top, matrix_rest = top_ref[mode], rest_ref[mode]
        state = jnp.concatenate(
            [held_ref[pl.ds(2 * mode + part, radii, stride=width), :] for part in range(2)], axis=1
        )
        if transposed:
            matrix_top, matrix_rest = (
                jnp.concatenate([m[:96], m[:32], m[96:], m[:32]], axis=0)
                for m in (matrix_top, matrix_rest)
            )
            top, rest = (part.T for part in halves(state))
            solved = product(top, matrix_top, (1, 1))
            solved += product(rest, matrix_top, (1, 1)) + product(top, matrix_rest, (1, 1))
        else:
            top, rest = halves(state)
            solved = product(matrix_top, top, (1, 0))
            solved += product(matrix_top, rest, (1, 0)) + product(matrix_rest, top, (1, 0))
        store(mode, solved)


def phase_b(
    peers,
    top_hbm,
    rest_hbm,
    moves_hbm,
    wire_ref,
    out_ref,
    held_ref,
    solved_ref,
    moves_ref,
    top_ref,
    rest_ref,
    sems,
):
    members, tiles, width, ignored = wire_ref.shape
    radii = top_ref.shape[1]
    ax_places = peers[2]
    first = pltpu.make_async_copy(moves_hbm, moves_ref, sems.at[2])
    first.start()
    copies = inverse_copies(top_hbm, rest_hbm, top_ref, rest_ref, sems)
    first.wait()
    unpack_quads(wire_ref, moves_ref, held_ref, peers)
    for copy in copies:
        copy.wait()

    def store(mode, solved):
        for part in range(2):
            solved_ref[pl.ds(2 * mode + part, radii, stride=width), :] = solved[
                :, part * 128 : (part + 1) * 128
            ]

    solved_modes(top_ref, rest_ref, held_ref, False, store)
    own = radii // members
    low = lax.broadcasted_iota(jnp.int32, (own * width // 2, 128), 1) & 8 == 0

    @pl.loop(0, members, unroll=UNROLL[3])
    def _(member):
        place = first_radius(member, own) * width
        for half in range(2):
            one, two = (
                jnp.concatenate(
                    [
                        solved_ref[pl.ds(pl.multiple_of(place + index * width, 8), width), :]
                        for index in range(first, own, 2)
                    ],
                    axis=0,
                )
                for first in range(2)
            )
            if half == 0:
                blocks = pieces(jnp.where(low, one, pltpu.roll(two, 8, 1)))
            else:
                blocks = pieces(jnp.where(low, pltpu.roll(one, 120, 1), two))
            parts = width // 8
            split = [block for part in range(parts) for block in blocks[part::parts]]
            target = member // 2 * ax_places + 2 * half + lax.rem(member, 2)
            for index, block in enumerate(spread_list(split)):
                out_ref[target, index] = block


def last_phase_b(
    peers,
    place_ref,
    own_offset_ref,
    other_offset_ref,
    top_hbm,
    rest_hbm,
    wire_ref,
    out_ref,
    held_ref,
    solved_ref,
    top_ref,
    rest_ref,
    sems,
):
    members, tiles, width, ignored = wire_ref.shape
    radii = top_ref.shape[1]
    seg_places, rad_places, ax_places = peers
    planes = 16 // ax_places
    each = radii // rad_places
    half = place_ref[1]
    rows = other_offset_ref.shape[0] - 16
    others = [jnp.max(other_offset_ref[rows + i : rows + i + 1, :128]) for i in range(2)]
    other_offset = jnp.where(half == 0, *others).astype(jnp.int32)
    copies = inverse_copies(top_hbm, rest_hbm, top_ref, rest_ref, sems)
    unpack_radii(wire_ref, held_ref)
    for copy in copies:
        copy.wait()

    def store(mode, solved):
        for part in range(2):
            rows = pl.ds(2 * mode + part, 96, stride=width)
            block = solved[part * 128 : part * 128 + 96]
            for strip in range(2):
                solved_ref[strip, rows, :] = block[:, strip * 128 : (strip + 1) * 128]

    solved_modes(top_ref, rest_ref, held_ref, True, store)
    lane = lax.broadcasted_iota(jnp.int32, (planes // 2 * width, 128), 1)


    @pl.loop(0, seg_places * ax_places, unroll=UNROLL[4])
    def _(index):
        seg, ax = index // ax_places, lax.rem(index, ax_places)
        offset = jnp.where(place_ref[2] == seg, own_offset_ref[half], other_offset)
        blocks = {}
        for component in range(3):
            for plane in range(planes):
                source = lax.rem(ax * planes + plane - offset + 16, 16)
                row = (component * 32 + seg * 16 + source) * width
                row = pl.multiple_of(row, 8)
                blocks[component, plane] = row
        for rad in range(rad_places):
            parts = width // 8
            slots = []
            for component in range(3):
                sides = []
                for side in range(2):
                    rows = [
                        pl.ds(blocks[component, plane], width) for plane in range(side, planes, 2)
                    ]
                    lines = [solved_ref[rad // 2, at, :] for at in rows]
                    sides.append(jnp.concatenate(lines, axis=0))
                if rad % 2 == 0:
                    sides[1] = pltpu.roll(sides[1], each, 1)
                else:
                    sides[0] = pltpu.roll(sides[0], 128 - each, 1)
                slots += pieces(jnp.where(lane < each, *sides))
            split = [block for part in range(parts) for block in slots[part::parts]]
            target = (seg * rad_places + rad) * ax_places + ax
            for at, block in enumerate(spread_list(split)):
                out_ref[target, at] = block


def residual_end(peers, wire_ref, start_ref, following_ref, out_ref, held_ref):
    seg_places, rad_places, ax_places = peers
    ignored, components, planes, each, columns = out_ref.shape
    shares = seg_places * rad_places
    width = columns // (2 * shares)
    chunk = width // 2
    count = (width // 8) * components * (planes // 2)
    slots = components * (planes // 2)
    half = pl.program_id(0)

    @pl.loop(0, 2 * shares, unroll=UNROLL[6])
    def _(member):
        share, low = member // 2, lax.rem(member, 2)
        source = share * ax_places + 2 * half + low
        split = gathered_list(pieces(wire_ref[source].reshape(-1, 128)), count)
        for slot in range(slots):
            parts = [split[part * slots + slot] for part in range(width // 8)]
            rows = jnp.concatenate(parts, axis=0)
            for high in range(2):
                at = (2 * high + low) * (columns // 4) + share * chunk
                held_ref[slot, pl.ds(at, chunk), :] = rows[high * chunk : (high + 1) * chunk]

    @pl.loop(0, slots, unroll=UNROLL[7])
    def _(slot):
        component, pair = slot // (planes // 2), lax.rem(slot, planes // 2)
        ending = held_ref[slot, :columns].T
        for side in range(2):
            plane = 2 * pair + side
            row = pl.multiple_of((component * planes + plane) * each, 8)
            upcoming = jnp.where(
                half + 1 < pl.num_programs(0),
                start_ref[0, component, plane],
                following_ref[pl.ds(row, each), :],
            )
            out_ref[0, component, plane] = ending[side * each : (side + 1) * each] - upcoming


def in_place(value):
    return pltpu.with_memory_space_constraint(value, pltpu.HBM)


def whole_blocks(count):
    return [pl.BlockSpec(memory_space=pltpu.VMEM)] * count


def fits(shape, peers):
    groups, components, axial_rows, radial_rows, columns = shape
    seg_places, rad_places, ax_places = peers
    members = seg_places * rad_places * 2
    return (
        (groups, components, seg_places, ax_places) == (2, 3, 2, 4)
        and axial_rows * ax_places == 16
        and radial_rows == 48
        and rad_places * radial_rows == 192
        and columns == 384
        and members == 16
    )


def half_body(peers, start_states, radial_inverse, offsets, mode_count):
    groups, components, axial_rows, radial_rows, columns = start_states.shape
    seg_places, rad_places, ax_places = peers
    axial = axial_rows * ax_places
    radii = radial_rows * rad_places
    shares = seg_places * rad_places
    members = 2 * shares
    own_radii = radii // members
    own_modes = radial_inverse.shape[0] // shares
    width = columns // members
    tiles = own_radii * 3 // 4
    order = column_order(columns, radial_inverse.shape[0], shares)
    synthesis_natural, synthesis, analysis, mode_of_row = tables(columns, order)

    seg, rad, ax = (lax.axis_index(name) for name in MESH_AXES)
    half, low = ax // 2, ax % 2

    def device(s, r, a):
        return (s * rad_places + r) * ax_places + a

    half_groups = [
        [
            device(s, r, 2 * h + l)
            for s in range(seg_places)
            for r in range(rad_places)
            for l in range(2)
        ]
        for h in range(2)
    ]
    mirror = [(a, (a + 2) % 4) for a in range(4)]
    params = pltpu.CompilerParams(vmem_limit_bytes=VMEM_LIMIT)
    up = [(i, (i + 1) % ax_places) for i in range(ax_places)]
    down = [(j, i) for i, j in up]
    halo = jax.ShapeDtypeStruct((groups, components, radial_rows, columns), jnp.float32)
    with jax.named_scope("pack_halos"):
        last, leading = pl.pallas_call(
            pack_halos,
            in_specs=[pl.BlockSpec(memory_space=pltpu.HBM)],
            out_specs=whole_blocks(2),
            out_shape=[halo, halo],
            scratch_shapes=[pltpu.SemaphoreType.DMA((2,))],
            compiler_params=params,
        )(in_place(start_states))
    before = lax.ppermute(last, "ax", up)
    after = lax.ppermute(leading, "ax", down)

    share = seg * rad_places + rad
    place = jnp.stack([share, half, seg]).astype(jnp.int32)
    first_rows = components * axial_rows * radial_rows
    with jax.named_scope("pack_sent"):
        dense_inverse, first_start = pl.pallas_call(
            pack_sent,
            in_specs=[
                pl.BlockSpec(memory_space=pltpu.SMEM),
                pl.BlockSpec(memory_space=pltpu.SMEM),
                pl.BlockSpec(memory_space=pltpu.HBM),
                pl.BlockSpec(memory_space=pltpu.HBM),
            ],
            out_specs=whole_blocks(2),
            out_shape=[
                jax.ShapeDtypeStruct((own_modes * 3 // 2, radii, 128), jnp.float32),
                jax.ShapeDtypeStruct((first_rows + 16, columns), jnp.float32),
            ],
            scratch_shapes=[
                pltpu.VMEM((own_modes, radii, radii), jnp.float32),
                pltpu.VMEM(start_states.shape[1:], jnp.float32),
                pltpu.SemaphoreType.DMA((2,)),
            ],
            compiler_params=params,
        )(place, offsets, in_place(radial_inverse), in_place(start_states))
    first = rad * radial_rows + (seg * 2 + low) * own_radii
    tile_index = np.arange(tiles)[:, None]
    lane = np.arange(128)[None, :]
    local = 4 * (tile_index // 3) + np.where(lane < 96, tile_index % 3, 3)
    radius = ((first + jnp.asarray(local)).astype(jnp.float32) + 0.5) / radii
    profile = (1.0 - radius * radius).reshape(tiles // 3, 3, 128)

    own_radius = ((rad * radial_rows + jnp.arange(radial_rows)).astype(jnp.float32) + 0.5) / radii
    own_profile = jnp.broadcast_to((1.0 - own_radius * own_radius)[:, None], (radial_rows, 128))

    synthesis_natural, synthesis, analysis = (
        jnp.asarray(table) for table in (synthesis_natural, synthesis, analysis)
    )
    mode_rows = jnp.asarray(np.repeat(mode_of_row[:, None], 128, axis=1))
    wire = jax.ShapeDtypeStruct((members, tiles, width, 128), jnp.float32)
    wire_spec = pl.BlockSpec((members, 3, width, 128), lambda g: (0, g, 0, 0))
    held = pltpu.VMEM((radii * width, 128), jnp.float32)
    count = (width // 8) * components * (axial_rows // 2)
    end_tiles = (count // 4) * 3 + count % 4
    everyone = seg_places * rad_places * ax_places
    spread_wire = jax.ShapeDtypeStruct((everyone, end_tiles, 8, 128), jnp.float32)

    def exchanged(value):
        return lax.all_to_all(
            value, MESH_AXES, 0, 0, axis_index_groups=half_groups, tiled=True
        )

    step = radial_rows // 3
    late_halo_spec = pl.BlockSpec(
        (groups, components, step, columns), lambda g: (0, 0, jnp.minimum(g, 2), 0)
    )
    own_spec = pl.BlockSpec(
        (groups, components, axial_rows, step, columns), lambda g: (0, 0, 0, g, 0)
    )
    with jax.named_scope("own_physical"):
        physical = pl.pallas_call(
            own_physical,
            grid=(3,),
            in_specs=[own_spec] + whole_blocks(1),
            out_specs=own_spec,
            out_shape=jax.ShapeDtypeStruct(start_states.shape, jnp.float32),
            compiler_params=params,
        )(start_states, synthesis_natural)
    before, after, dense_inverse, physical, profile, own_profile = lax.optimization_barrier(
        (before, after, dense_inverse, physical, profile, own_profile)
    )
    other_inverse = lax.ppermute(dense_inverse, "ax", mirror)
    with jax.named_scope("phase_a_first"):
        spectral = pl.pallas_call(
            first_phase_a,
            grid=(4,),
            in_specs=[
                pl.BlockSpec(memory_space=pltpu.SMEM),
                late_halo_spec,
                pl.BlockSpec(
                    own_spec.block_shape, lambda g: (0, 0, 0, jnp.minimum(g, 2), 0)
                ),
                late_halo_spec,
                *whole_blocks(3),
                pl.BlockSpec((step, 128), lambda g: (jnp.minimum(g, 2), 0)),
            ],
            out_specs=pl.BlockSpec(
                wire_spec.block_shape, lambda g: (0, jnp.maximum(g - 1, 0), 0, 0)
            ),
            out_shape=pltpu.HBM(wire.shape, wire.dtype),
            scratch_shapes=[
                pltpu.VMEM(
                    (2, columns // 128, groups * components * axial_rows * step, 128), jnp.float32
                )
            ],
            compiler_params=params,
        )(
            mode_count,
            before,
            physical,
            after,
            synthesis_natural,
            analysis,
            mode_rows,
            own_profile,
        )
    matrices = jax.ShapeDtypeStruct((2 * own_modes, radii, radii), jnp.bfloat16)
    in_hbm = [pl.BlockSpec(memory_space=pltpu.HBM)] * 2
    inverse_scratch = [pltpu.VMEM(matrices.shape, matrices.dtype)] * 2
    inverse_scratch += [pltpu.SemaphoreType.DMA((3,))]
    with jax.named_scope("ordered_inverse"):
        inverse = pl.pallas_call(
            ordered_inverse,
            in_specs=[pl.BlockSpec(memory_space=pltpu.SMEM)] + whole_blocks(2),
            out_specs=[pl.BlockSpec(matrices.shape, lambda: (0, 0, 0))] * 2,
            out_shape=[pltpu.HBM(matrices.shape, matrices.dtype)] * 2,
            compiler_params=params,
            cost_estimate=pl.CostEstimate(
                flops=FLOPS, bytes_accessed=16 * own_modes * radii * radii, transcendentals=0
            ),
        )(place, dense_inverse, other_inverse)
    spectral, first_start = lax.optimization_barrier((spectral, first_start))
    following = passed_along(first_start, "seg", -1)
    lines = exchanged(spectral)
    moves = jnp.asarray(quad_moves())
    with jax.named_scope("phase_b_first"):
        solved = pl.pallas_call(
            functools.partial(phase_b, peers),
            in_specs=in_hbm + [pl.BlockSpec(memory_space=pltpu.HBM)] + whole_blocks(1),
            out_specs=pl.BlockSpec(memory_space=pltpu.VMEM),
            out_shape=spread_wire,
            scratch_shapes=[held, held, pltpu.VMEM(moves.shape, moves.dtype)] + inverse_scratch,
            compiler_params=params,
        )(*map(in_place, (*inverse, moves)), lines)
    solved, following = lax.optimization_barrier((solved, following))
    state = lax.all_to_all(solved, MESH_AXES, 0, 0, tiled=True)
    with jax.named_scope("phase_a_later"):
        spectral = pl.pallas_call(
            later_phase_a,
            grid=(tiles // 3 + 1,),
            in_specs=[
                pl.BlockSpec(memory_space=pltpu.SMEM),
                *whole_blocks(6),
            ],
            out_specs=pl.BlockSpec(
                wire_spec.block_shape, lambda g: (0, jnp.maximum(g - 1, 0), 0, 0)
            ),
            out_shape=wire,
            scratch_shapes=[
                pltpu.VMEM((2, own_radii // 2, columns, 128), jnp.float32),
                pltpu.VMEM((2, columns, 3 * 128), jnp.float32),
            ],
            compiler_params=params,
        )(mode_count, state, synthesis, analysis, mode_rows, profile, jnp.asarray(lane_moves()))
    lines = exchanged(spectral)
    with jax.named_scope("phase_b_last"):
        ending = pl.pallas_call(
            functools.partial(last_phase_b, peers),
            in_specs=[pl.BlockSpec(memory_space=pltpu.SMEM)] * 2
            + whole_blocks(1)
            + in_hbm
            + whole_blocks(1),
            out_specs=pl.BlockSpec(memory_space=pltpu.VMEM),
            out_shape=spread_wire,
            scratch_shapes=[held, pltpu.VMEM((2, 96 * width, 128), jnp.float32)]
            + inverse_scratch,
            compiler_params=params,
        )(place, offsets, following, *map(in_place, inverse), lines)
    ending = lax.all_to_all(ending, MESH_AXES, 0, 0, tiled=True)
    with jax.named_scope("residual_end"):
        return pl.pallas_call(
            functools.partial(residual_end, peers),
            grid=(groups,),
            in_specs=[
                *whole_blocks(1),
                pl.BlockSpec((1,) + start_states.shape[1:], lambda b: (groups - 1, 0, 0, 0, 0)),
                *whole_blocks(1),
            ],
            out_specs=pl.BlockSpec((1,) + start_states.shape[1:], lambda b: (b, 0, 0, 0, 0)),
            out_shape=jax.ShapeDtypeStruct(start_states.shape, jnp.float32),
            scratch_shapes=[
                pltpu.VMEM((components * (axial_rows // 2), columns + 8, 128), jnp.float32)
            ],
            compiler_params=params,
        )(ending, start_states, following)


def solution(mesh):
    peers = tuple(mesh.shape[name] for name in MESH_AXES)

    def body(start_states, radial_inverse, offsets, mode_count):
        if fits(start_states.shape, peers):
            return half_body(peers, start_states, radial_inverse, offsets, mode_count)
        return general_body(start_states, radial_inverse, offsets, mode_count)

    placed = (P("seg", None, "ax", "rad", None), P("ax", None, None), P("seg"), P())
    return jax.shard_map(
        body,
        mesh=mesh,
        in_specs=placed,
        out_specs=P("seg", None, "ax", "rad", None),
        check_vma=False,
    )
```

```python
import functools
import math

import jax
import jax.numpy as jnp
import ml_dtypes
import numpy as np
from jax import lax
from jax.experimental import pallas as pl
from jax.experimental.pallas import tpu as pltpu
from jax.sharding import PartitionSpec as P

STEPS = 2
MESH_AXES = ("seg", "rad", "ax")
UNROLL = [12, 12, 16, 16, 8, 32, 16, 6]
VMEM_LIMIT = 24 * 1024 * 1024
FLOPS = 40_000_000_000

highest = lax.Precision.HIGHEST


def passed_along(value, axis, steps):
    count = lax.axis_size(axis)
    pairs = [(source, (source + steps) % count) for source in range(count)]
    return lax.ppermute(value, axis, pairs)


def padded_2(array, sides, width):
    for axis, dim in sides:
        peers, length = (lax.axis_size(axis), array.shape[dim])
        up = [(i, (i + 1) % peers) for i in range(peers)]
        down = [(j, i) for i, j in up]
        last = lax.slice_in_dim(array, length - width, length, axis=dim)
        leading = lax.slice_in_dim(array, 0, width, axis=dim)
        before = lax.ppermute(last, axis, up)
        after = lax.ppermute(leading, axis, down)
        array = jnp.concatenate([before, array, after], axis=dim)
    return array


def fourier_tables(columns, kept_modes):
    modes_total = columns // 2
    row_index = lax.broadcasted_iota(jnp.int32, (columns, columns), 0)
    point_index = lax.broadcasted_iota(jnp.int32, (columns, columns), 1)
    mode_index = row_index // 2
    phase = (mode_index * point_index % columns).astype(jnp.float32) * (2.0 * math.pi / columns)
    even_rows = row_index % 2 == 0
    cosine = jnp.cos(phase)
    sine = jnp.sin(phase)
    root = math.sqrt(modes_total)
    synthesis = jnp.where(even_rows, cosine, sine) / root
    weights = jnp.where(mode_index == 0, 1.0, 2.0)
    analysis = jnp.where(even_rows, weights * cosine, 2.0 * sine) * (root / columns)
    analysis = jnp.where(mode_index < kept_modes, analysis, 0.0)
    return (synthesis, analysis)


def radial_solve(pencils, radial_inverse, radial_rows):
    local_modes = radial_inverse.shape[0]
    local_columns, members, axial_cells, ignored = pencils.shape
    own_rows = lax.dynamic_slice_in_dim(
        radial_inverse, lax.axis_index("rad") * radial_rows, radial_rows, 1
    )
    piece = lax.all_gather(pencils, "rad", axis=3, tiled=True)
    piece_rows = piece.shape[3]
    grouped = piece.reshape(local_modes, 2, members, axial_cells, piece_rows)
    product = jnp.einsum("mrs,mkqzs->mkqzr", own_rows, grouped, precision=highest)
    return product.reshape(local_columns, members, axial_cells, radial_rows)


def general_body(start_states, radial_inverse, offsets, mode_count):
    groups, components, axial_rows, radial_rows, columns = start_states.shape
    synthesis, analysis = fourier_tables(columns, mode_count[0])
    radius = (
        (lax.axis_index("rad") * radial_rows + jnp.arange(radial_rows)).astype(jnp.float32) + 0.5
    ) / (radial_rows * lax.axis_size("rad"))
    profile = (1.0 - radius * radius).reshape(1, 1, 1, radial_rows, 1)
    following = passed_along(start_states[0], "seg", -1)
    current = start_states
    for step_index in range(STEPS):
        if step_index == 0:
            physical = jnp.einsum("gczrj,jp->gczrp", current, synthesis, precision=highest)
        else:
            physical = jnp.einsum("jgczr,jp->gczrp", current, synthesis, precision=highest)
        padded = padded_2(physical, (("ax", 2),), 1)
        gradient = (padded[:, :, 2:] - padded[:, :, :-2]) * 20.0
        advecting = profile + padded[:, 2:3, 1:-1]
        forcing = physical - 0.02 * advecting * gradient
        spectral = jnp.einsum("gczrp,jp->jgczr", forcing, analysis, precision=highest)
        pencils = lax.all_to_all(spectral, "ax", split_axis=0, concat_axis=3, tiled=True)
        local_columns = pencils.shape[0]
        axial_cells = pencils.shape[3]
        pencils = pencils.reshape(local_columns, groups * components, axial_cells, radial_rows)
        solved = radial_solve(pencils, radial_inverse, radial_rows)
        if step_index == STEPS - 1:
            blocks = solved.reshape(local_columns, groups, components, axial_cells, radial_rows)
            shifted = [
                jnp.roll(blocks[:, member], offsets[member], axis=2) for member in range(groups)
            ]
            solved = jnp.stack(shifted, axis=1).reshape(
                local_columns, groups * components, axial_cells, radial_rows
            )
        returned = lax.all_to_all(solved, "ax", split_axis=2, concat_axis=0, tiled=True)
        current = returned.reshape(columns, groups, components, axial_rows, radial_rows)
    ending = jnp.transpose(current, (1, 2, 3, 4, 0))
    upcoming = jnp.concatenate([start_states[1:], following[None]], axis=0)
    return ending - upcoming


def halves(high):
    top = high.astype(jnp.bfloat16)
    return top, (high - top.astype(jnp.float32)).astype(jnp.bfloat16)


def product(left, right, contract):
    return lax.dot_general(
        left, right, ((contract[:1], contract[1:]), ((), ())), preferred_element_type=jnp.float32
    )


def stacked_table(table):
    top = table.astype(ml_dtypes.bfloat16)
    rest = (table - top.astype(np.float64)).astype(ml_dtypes.bfloat16)
    return np.concatenate([top, top, rest], axis=1)


def column_order(columns, quarter_modes, shares):
    each = quarter_modes // shares
    order = []
    for share in range(shares):
        for low in range(2):
            for high in range(2):
                first = (2 * high + low) * quarter_modes + share * each
                order.extend(range(2 * first, 2 * (first + each)))
    assert sorted(order) == list(range(columns))
    return np.array(order)


def tables(columns, order):
    modes_total = columns // 2
    rows = np.arange(columns)
    mode = rows // 2
    phase = (mode[:, None] * np.arange(columns)[None, :]) % columns * (2.0 * np.pi / columns)
    even = (rows % 2 == 0)[:, None]
    root = math.sqrt(modes_total)
    synthesis = np.where(even, np.cos(phase), np.sin(phase)) / root
    weights = np.where(mode == 0, 1.0, 2.0)[:, None]
    analysis = np.where(even, weights * np.cos(phase), 2.0 * np.sin(phase)) * (root / columns)
    return (
        np.ascontiguousarray(stacked_table(synthesis.T).T),
        stacked_table(np.ascontiguousarray(synthesis.T[:, order])),
        stacked_table(analysis[order]),
        mode[order].astype(np.int32),
    )


def lane_index(block):
    return lax.broadcasted_iota(jnp.int32, block.shape, 1)


def spread(tiles, fourth):
    lane = lane_index(fourth)
    return [
        jnp.where(lane < 96, block, pltpu.roll(fourth, 96 - 32 * index, 1))
        for index, block in enumerate(tiles)
    ]


def gathered(waves):
    lane = lane_index(waves[0])
    fourth = jnp.where(lane < 32, pltpu.roll(waves[0], 32, 1), pltpu.roll(waves[1], 64, 1))
    return waves + [jnp.where(lane < 64, fourth, pltpu.roll(waves[2], 96, 1))]


def every(blocks, first, step):
    return jnp.concatenate(blocks[first::step], axis=0)


def pieces(block):
    return [block[at : at + 8] for at in range(0, block.shape[0], 8)]


def spread_list(blocks):
    whole = len(blocks) // 4 * 4
    quarters = [every(blocks[:whole], first, 4) for first in range(4)]
    full = [pieces(block) for block in spread(quarters[:3], quarters[3])]
    return [block for group in zip(*full) for block in group] + blocks[whole:]


def gathered_list(full, count):
    whole = count // 4 * 3
    blocks = [pieces(block) for block in gathered([every(full[:whole], i, 3) for i in range(3)])]
    return [block for group in zip(*blocks) for block in group] + full[whole:]


def lane_moves():
    lane = np.arange(128)
    moves = np.zeros((128, 256), np.float32)
    above = lane // 16 * 16 + (lane + 1) % 16
    below = lane // 16 * 16 + (lane + 15) % 16
    np.add.at(moves, (above, lane), 1.0)
    np.add.at(moves, (below, lane), -1.0)
    whole = lane[:96]
    moves[64 + whole % 32, 128 + whole] = 1.0
    return np.concatenate([moves, moves], axis=0).astype(ml_dtypes.bfloat16)


def physical_to_spectral(physical, profile, analysis, moves):
    lane = lane_index(physical[0])
    forcing = []
    for tile in range(3):
        field = physical[tile]
        moved = product(jnp.concatenate(halves(field), axis=1), moves, (1, 0))
        speed = jnp.where(lane < 96, moved[:, 128:], physical[2])
        forcing.append(field - 0.4 * (profile[tile : tile + 1] + speed) * moved[:, :128])
    forcing = jnp.concatenate(forcing, axis=1)
    top, rest = halves(forcing)
    return product(analysis, jnp.concatenate([top, rest, top], axis=0), (1, 0))


def write_spectral(spectral, count_ref, mode_ref, out_ref):
    members, ignored, width, ignored = out_ref.shape
    kept = mode_ref[...] < count_ref[0]
    for tile in range(3):
        block = jnp.where(kept, spectral[:, tile * 128 : (tile + 1) * 128], 0.0)
        out_ref[:, tile] = block.reshape(members, width, 128)


def pack_halos(start_ref, last_ref, leading_ref, sems):
    planes = start_ref.shape[2]
    copies = [
        pltpu.make_async_copy(start_ref.at[:, :, planes - 1], last_ref, sems.at[0]),
        pltpu.make_async_copy(start_ref.at[:, :, 0], leading_ref, sems.at[1]),
    ]
    for copy in copies:
        copy.start()
    for copy in copies:
        copy.wait()


def synthesized(rows, synthesis):
    top, rest = halves(jnp.concatenate(rows, axis=0))
    return product(jnp.concatenate([top, rest, top], axis=1), synthesis, (1, 0))


def own_physical(own_ref, synthesis_ref, out_ref):
    groups, components, planes, radii, columns = own_ref.shape
    rows = own_ref[...].reshape(groups * components * planes * radii, columns)
    out_ref[...] = synthesized([rows], synthesis_ref[...]).reshape(out_ref.shape)


def first_phase_a(
    count_ref,
    before_ref,
    own_ref,
    after_ref,
    synthesis_ref,
    analysis_ref,
    mode_ref,
    profile_ref,
    out_ref,
    held_ref,
):
    groups, components, planes, radii, columns = own_ref.shape
    steps = 3
    radii //= steps
    strips = columns // 128
    count = groups * components
    quad = 4 * planes

    def begin(step):
        at = slice(step * radii, (step + 1) * radii)
        sides = [ref[:, :, at].reshape(count * radii, columns) for ref in (before_ref, after_ref)]
        sides = synthesized(sides, synthesis_ref[...])
        sides = sides.reshape(2, groups, components, radii, columns)
        profile = jnp.concatenate([profile_ref[at]] * strips, axis=1)
        for segment in range(groups):
            for plane in range(planes):
                speed = 0.4 * (profile + own_ref[segment, 2, plane, at])
                for component in range(components):
                    line = [own_ref[segment, component, i, at] for i in range(planes)]
                    line = [sides[0, segment, component], *line, sides[1, segment, component]]
                    forcing = line[plane + 1] - speed * (line[plane + 2] - line[plane])
                    first = (component * groups + segment) * radii * planes
                    spot = pl.ds(first + plane, radii, stride=planes)
                    for strip in range(strips):
                        held_ref[step % 2, strip, spot, :] = forcing[
                            :, strip * 128 : (strip + 1) * 128
                        ]

    def finish(step):
        lines = []
        for strip in range(strips):
            parts = []
            for tile in range(3):
                for four, members in ((tile, range(components)), (3, (tile,))):
                    for component in members:
                        for at in range(four * quad, (four + 1) * quad, quad // 2):
                            for segment in range(groups):
                                row = (component * groups + segment) * radii * planes + at
                                parts.append(
                                    held_ref[step % 2, strip, row : row + quad // 2, :]
                                )
            lines.append(jnp.concatenate(parts, axis=0))
        top, rest = halves(jnp.concatenate(lines, axis=1))
        spectral = product(analysis_ref[...], jnp.concatenate([top, rest, top], axis=1), (1, 1))
        write_spectral(spectral, count_ref, mode_ref, out_ref)

    for step in range(steps + 1):

        @pl.when(pl.program_id(0) == step)
        def _(step=step):
            if step < steps:
                begin(step)
            if step > 0:
                finish(step - 1)


def later_phase_a(
    count_ref,
    wire_ref,
    synthesis_ref,
    analysis_ref,
    mode_ref,
    profile_ref,
    moves_ref,
    out_ref,
    held_ref,
    physical_ref,
):
    sources, tiles, ignored, ignored = wire_ref.shape
    halves_of_ax, pairs, ignored, ignored = held_ref.shape
    parts = out_ref.shape[2] // 8

    def unpack():
        @pl.loop(0, sources, unroll=UNROLL[5])
        def _(source):
            half = lax.rem(source, 4) // 2
            member = source // 4 * 2 + lax.rem(source, 2)
            blocks = gathered_list(pieces(wire_ref[source].reshape(tiles * 8, 128)), pairs * parts)
            for part in range(parts):
                at = pl.ds(pl.multiple_of((member * parts + part) * 8, 8), 8)
                for pair in range(pairs):
                    held_ref[half, pair, at, :] = blocks[part * pairs + pair]

    def begin(group):
        radii = []
        for pair in range(2):
            one, two = (held_ref[half, 2 * group + pair] for half in range(halves_of_ax))
            low = lane_index(one) & 8 == 0
            radii.append(jnp.where(low, one, pltpu.roll(two, 8, 1)))
            radii.append(jnp.where(low, pltpu.roll(one, 120, 1), two))
        top, rest = halves(jnp.concatenate(spread(radii[:3], radii[3]), axis=1))
        physical_ref[group % 2] = product(
            synthesis_ref[...], jnp.concatenate([top, rest, top], axis=0), (1, 0)
        )

    def finish(group):
        physical = [physical_ref[group % 2, :, tile * 128 : (tile + 1) * 128] for tile in range(3)]
        spectral = physical_to_spectral(
            physical, profile_ref[group], analysis_ref[...], moves_ref[...]
        )
        write_spectral(spectral, count_ref, mode_ref, out_ref)

    for step in range(pairs // 2 + 1):

        @pl.when(pl.program_id(0) == step)
        def _(step=step):
            if step == 0:
                unpack()
            if step < pairs // 2:
                begin(step)
            if step > 0:
                finish(step - 1)


def quad_moves():
    moves = np.zeros((4, 128, 4, 128), np.float32)
    for source in range(4):
        for lane in range(96):
            block, two, segment, one, z = (
                lane // 32,
                lane // 16 % 2,
                lane // 8 % 2,
                lane // 4 % 2,
                lane % 4,
            )
            target = block * 32 + source // 2 * 16 + segment * 8 + source % 2 * 4 + z
            moves[source, lane, 2 * two + one, target] = 1.0
    return moves.reshape(512, 512).astype(ml_dtypes.bfloat16)


def unpack_quads(wire_ref, moves_ref, held_ref, peers):
    members, tiles, width, ignored = wire_ref.shape
    seg_places, rad_places, ignored = peers
    groups = tiles // 3

    @pl.loop(0, rad_places * groups, unroll=UNROLL[1])
    def _(index):
        rad, group = index // groups, lax.rem(index, groups)
        sources = [(s * rad_places + rad) * 2 + l for s in range(seg_places) for l in range(2)]
        waves = [
            jnp.concatenate([wire_ref[source, 3 * group + tile] for source in sources], axis=0)
            for tile in range(3)
        ]
        quads = gathered(waves)
        lines = [
            jnp.concatenate([quad[at : at + width] for quad in quads], axis=0)
            for at in range(0, 4 * width, width)
        ]
        top, rest = halves(jnp.concatenate(lines, axis=1))
        radii = product(top, moves_ref[...], (1, 0)) + product(rest, moves_ref[...], (1, 0))
        for place in range(4):
            for quad in range(4):
                at = pl.multiple_of((index * 16 + 4 * quad + place) * width, 8)
                held_ref[pl.ds(at, width), :] = radii[
                    quad * width : (quad + 1) * width, place * 128 : (place + 1) * 128
                ]


def first_radius(member, own):
    rad = lax.rem(member // 2, 4)
    return ((rad * 2 + member // 8) * 2 + lax.rem(member, 2)) * own


def unpack_radii(wire_ref, held_ref):
    members, tiles, width, ignored = wire_ref.shape
    own = tiles * 4 // 3

    @pl.loop(0, members, unroll=UNROLL[2])
    def _(member):
        first = first_radius(member, own)
        waves = [
            jnp.concatenate([wire_ref[member, at] for at in range(tile, tiles, 3)], axis=0)
            for tile in range(3)
        ]
        for index, block in enumerate(gathered(waves)):
            for group in range(tiles // 3):
                at = pl.multiple_of((first + 4 * group + index) * width, 8)
                held_ref[pl.ds(at, width), :] = block[group * width : (group + 1) * width]


def pack_sent(
    place_ref, offset_ref, inverse_ref, start_ref, out_ref, first_ref, held_ref, start_held_ref, sems
):
    each, radii, ignored = held_ref.shape
    copy = pltpu.make_async_copy(
        inverse_ref.at[pl.ds(place_ref[0] * each, each)], held_ref, sems.at[0]
    )
    copy.start()
    first = pltpu.make_async_copy(start_ref.at[0], start_held_ref, sems.at[1])
    first.start()
    rows = first_ref.shape[0] - 16
    for index in range(offset_ref.shape[0]):
        offset = offset_ref[index].astype(jnp.float32)
        first_ref[rows + index : rows + index + 1, :] = jnp.full((1, first_ref.shape[1]), offset)
    copy.wait()
    for index in range(each):
        out_ref[index] = held_ref[index, :, :128]
    for index in range(each // 2):
        out_ref[each + index, :, :64] = held_ref[index, :, 128:]
        out_ref[each + index, :, 64:] = held_ref[each // 2 + index, :, 128:]
    first.wait()
    first_ref[0:rows, :] = start_held_ref[...].reshape(rows, first_ref.shape[1])


def ordered_inverse(place_ref, own_ref, other_ref, top_ref, rest_ref):
    each = top_ref.shape[0] // 2
    first_half = place_ref[1] == 0

    def matrix(ref, index):
        side = index // (each // 2) * 64
        tail = ref[each + index % (each // 2), :, side : side + 64]
        return jnp.concatenate([ref[index], tail], axis=1)

    for index in range(each):
        here, there = matrix(own_ref, index), matrix(other_ref, index)
        top_ref[index], rest_ref[index] = halves(jnp.where(first_half, here, there))
        top_ref[each + index], rest_ref[each + index] = halves(jnp.where(first_half, there, here))


def inverse_copies(top_hbm, rest_hbm, top_ref, rest_ref, sems):
    copies = [
        pltpu.make_async_copy(source, target, sems.at[index])
        for index, (source, target) in enumerate(((top_hbm, top_ref), (rest_hbm, rest_ref)))
    ]
    for copy in copies:
        copy.start()
    return copies


def solved_modes(top_ref, rest_ref, held_ref, transposed, store):
    modes, radii, ignored = top_ref.shape
    width = 2 * modes

    @pl.loop(0, modes, unroll=UNROLL[0])
    def _(mode):
        matrix_top, matrix_rest = top_ref[mode], rest_ref[mode]
        state = jnp.concatenate(
            [held_ref[pl.ds(2 * mode + part, radii, stride=width), :] for part in range(2)], axis=1
        )
        if transposed:
            matrix_top, matrix_rest = (
                jnp.concatenate([m[:96], m[:32], m[96:], m[:32]], axis=0)
                for m in (matrix_top, matrix_rest)
            )
            top, rest = (part.T for part in halves(state))
            solved = product(top, matrix_top, (1, 1))
            solved += product(rest, matrix_top, (1, 1)) + product(top, matrix_rest, (1, 1))
        else:
            top, rest = halves(state)
            solved = product(matrix_top, top, (1, 0))
            solved += product(matrix_top, rest, (1, 0)) + product(matrix_rest, top, (1, 0))
        store(mode, solved)


def phase_b(
    peers,
    top_hbm,
    rest_hbm,
    moves_hbm,
    wire_ref,
    out_ref,
    held_ref,
    solved_ref,
    moves_ref,
    top_ref,
    rest_ref,
    sems,
):
    members, tiles, width, ignored = wire_ref.shape
    radii = top_ref.shape[1]
    ax_places = peers[2]
    first = pltpu.make_async_copy(moves_hbm, moves_ref, sems.at[2])
    first.start()
    copies = inverse_copies(top_hbm, rest_hbm, top_ref, rest_ref, sems)
    first.wait()
    unpack_quads(wire_ref, moves_ref, held_ref, peers)
    for copy in copies:
        copy.wait()

    def store(mode, solved):
        for part in range(2):
            solved_ref[pl.ds(2 * mode + part, radii, stride=width), :] = solved[
                :, part * 128 : (part + 1) * 128
            ]

    solved_modes(top_ref, rest_ref, held_ref, False, store)
    own = radii // members
    low = lax.broadcasted_iota(jnp.int32, (own * width // 2, 128), 1) & 8 == 0

    @pl.loop(0, members, unroll=UNROLL[3])
    def _(member):
        place = first_radius(member, own) * width
        for half in range(2):
            one, two = (
                jnp.concatenate(
                    [
                        solved_ref[pl.ds(pl.multiple_of(place + index * width, 8), width), :]
                        for index in range(first, own, 2)
                    ],
                    axis=0,
                )
                for first in range(2)
            )
            if half == 0:
                blocks = pieces(jnp.where(low, one, pltpu.roll(two, 8, 1)))
            else:
                blocks = pieces(jnp.where(low, pltpu.roll(one, 120, 1), two))
            parts = width // 8
            split = [block for part in range(parts) for block in blocks[part::parts]]
            target = member // 2 * ax_places + 2 * half + lax.rem(member, 2)
            for index, block in enumerate(spread_list(split)):
                out_ref[target, index] = block


def last_phase_b(
    peers,
    place_ref,
    own_offset_ref,
    other_offset_ref,
    top_hbm,
    rest_hbm,
    wire_ref,
    out_ref,
    held_ref,
    solved_ref,
    top_ref,
    rest_ref,
    sems,
):
    members, tiles, width, ignored = wire_ref.shape
    radii = top_ref.shape[1]
    seg_places, rad_places, ax_places = peers
    planes = 16 // ax_places
    each = radii // rad_places
    half = place_ref[1]
    rows = other_offset_ref.shape[0] - 16
    others = [jnp.max(other_offset_ref[rows + i : rows + i + 1, :128]) for i in range(2)]
    other_offset = jnp.where(half == 0, *others).astype(jnp.int32)
    copies = inverse_copies(top_hbm, rest_hbm, top_ref, rest_ref, sems)
    unpack_radii(wire_ref, held_ref)
    for copy in copies:
        copy.wait()

    def store(mode, solved):
        for part in range(2):
            rows = pl.ds(2 * mode + part, 96, stride=width)
            block = solved[part * 128 : part * 128 + 96]
            for strip in range(2):
                solved_ref[strip, rows, :] = block[:, strip * 128 : (strip + 1) * 128]

    solved_modes(top_ref, rest_ref, held_ref, True, store)
    lane = lax.broadcasted_iota(jnp.int32, (planes // 2 * width, 128), 1)


    @pl.loop(0, seg_places * ax_places, unroll=UNROLL[4])
    def _(index):
        seg, ax = index // ax_places, lax.rem(index, ax_places)
        offset = jnp.where(place_ref[2] == seg, own_offset_ref[half], other_offset)
        blocks = {}
        for component in range(3):
            for plane in range(planes):
                source = lax.rem(ax * planes + plane - offset + 16, 16)
                row = (component * 32 + seg * 16 + source) * width
                row = pl.multiple_of(row, 8)
                blocks[component, plane] = row
        for rad in range(rad_places):
            parts = width // 8
            slots = []
            for component in range(3):
                sides = []
                for side in range(2):
                    rows = [
                        pl.ds(blocks[component, plane], width) for plane in range(side, planes, 2)
                    ]
                    lines = [solved_ref[rad // 2, at, :] for at in rows]
                    sides.append(jnp.concatenate(lines, axis=0))
                if rad % 2 == 0:
                    sides[1] = pltpu.roll(sides[1], each, 1)
                else:
                    sides[0] = pltpu.roll(sides[0], 128 - each, 1)
                slots += pieces(jnp.where(lane < each, *sides))
            split = [block for part in range(parts) for block in slots[part::parts]]
            target = (seg * rad_places + rad) * ax_places + ax
            for at, block in enumerate(spread_list(split)):
                out_ref[target, at] = block


def residual_end(peers, wire_ref, start_ref, following_ref, out_ref, held_ref):
    seg_places, rad_places, ax_places = peers
    ignored, components, planes, each, columns = out_ref.shape
    shares = seg_places * rad_places
    width = columns // (2 * shares)
    chunk = width // 2
    count = (width // 8) * components * (planes // 2)
    slots = components * (planes // 2)
    half = pl.program_id(0)

    @pl.loop(0, 2 * shares, unroll=UNROLL[6])
    def _(member):
        share, low = member // 2, lax.rem(member, 2)
        source = share * ax_places + 2 * half + low
        split = gathered_list(pieces(wire_ref[source].reshape(-1, 128)), count)
        for slot in range(slots):
            parts = [split[part * slots + slot] for part in range(width // 8)]
            rows = jnp.concatenate(parts, axis=0)
            for high in range(2):
                at = (2 * high + low) * (columns // 4) + share * chunk
                held_ref[slot, pl.ds(at, chunk), :] = rows[high * chunk : (high + 1) * chunk]

    @pl.loop(0, slots, unroll=UNROLL[7])
    def _(slot):
        component, pair = slot // (planes // 2), lax.rem(slot, planes // 2)
        ending = held_ref[slot, :columns].T
        for side in range(2):
            plane = 2 * pair + side
            row = pl.multiple_of((component * planes + plane) * each, 8)
            upcoming = jnp.where(
                half + 1 < pl.num_programs(0),
                start_ref[0, component, plane],
                following_ref[pl.ds(row, each), :],
            )
            out_ref[0, component, plane] = ending[side * each : (side + 1) * each] - upcoming


def in_place(value):
    return pltpu.with_memory_space_constraint(value, pltpu.HBM)


def whole_blocks(count):
    return [pl.BlockSpec(memory_space=pltpu.VMEM)] * count


def fits(shape, peers):
    groups, components, axial_rows, radial_rows, columns = shape
    seg_places, rad_places, ax_places = peers
    members = seg_places * rad_places * 2
    return (
        (groups, components, seg_places, ax_places) == (2, 3, 2, 4)
        and axial_rows * ax_places == 16
        and radial_rows == 48
        and rad_places * radial_rows == 192
        and columns == 384
        and members == 16
    )


def half_body(peers, start_states, radial_inverse, offsets, mode_count):
    groups, components, axial_rows, radial_rows, columns = start_states.shape
    seg_places, rad_places, ax_places = peers
    axial = axial_rows * ax_places
    radii = radial_rows * rad_places
    shares = seg_places * rad_places
    members = 2 * shares
    own_radii = radii // members
    own_modes = radial_inverse.shape[0] // shares
    width = columns // members
    tiles = own_radii * 3 // 4
    order = column_order(columns, radial_inverse.shape[0], shares)
    synthesis_natural, synthesis, analysis, mode_of_row = tables(columns, order)

    seg, rad, ax = (lax.axis_index(name) for name in MESH_AXES)
    half, low = ax // 2, ax % 2

    def device(s, r, a):
        return (s * rad_places + r) * ax_places + a

    half_groups = [
        [
            device(s, r, 2 * h + l)
            for s in range(seg_places)
            for r in range(rad_places)
            for l in range(2)
        ]
        for h in range(2)
    ]
    mirror = [(a, (a + 2) % 4) for a in range(4)]
    params = pltpu.CompilerParams(vmem_limit_bytes=VMEM_LIMIT)
    up = [(i, (i + 1) % ax_places) for i in range(ax_places)]
    down = [(j, i) for i, j in up]
    halo = jax.ShapeDtypeStruct((groups, components, radial_rows, columns), jnp.float32)
    with jax.named_scope("pack_halos"):
        last, leading = pl.pallas_call(
            pack_halos,
            in_specs=[pl.BlockSpec(memory_space=pltpu.HBM)],
            out_specs=whole_blocks(2),
            out_shape=[halo, halo],
            scratch_shapes=[pltpu.SemaphoreType.DMA((2,))],
            compiler_params=params,
        )(in_place(start_states))
    before = lax.ppermute(last, "ax", up)
    after = lax.ppermute(leading, "ax", down)

    share = seg * rad_places + rad
    place = jnp.stack([share, half, seg]).astype(jnp.int32)
    first_rows = components * axial_rows * radial_rows
    with jax.named_scope("pack_sent"):
        dense_inverse, first_start = pl.pallas_call(
            pack_sent,
            in_specs=[
                pl.BlockSpec(memory_space=pltpu.SMEM),
                pl.BlockSpec(memory_space=pltpu.SMEM),
                pl.BlockSpec(memory_space=pltpu.HBM),
                pl.BlockSpec(memory_space=pltpu.HBM),
            ],
            out_specs=whole_blocks(2),
            out_shape=[
                jax.ShapeDtypeStruct((own_modes * 3 // 2, radii, 128), jnp.float32),
                jax.ShapeDtypeStruct((first_rows + 16, columns), jnp.float32),
            ],
            scratch_shapes=[
                pltpu.VMEM((own_modes, radii, radii), jnp.float32),
                pltpu.VMEM(start_states.shape[1:], jnp.float32),
                pltpu.SemaphoreType.DMA((2,)),
            ],
            compiler_params=params,
        )(place, offsets, in_place(radial_inverse), in_place(start_states))
    first = rad * radial_rows + (seg * 2 + low) * own_radii
    tile_index = np.arange(tiles)[:, None]
    lane = np.arange(128)[None, :]
    local = 4 * (tile_index // 3) + np.where(lane < 96, tile_index % 3, 3)
    radius = ((first + jnp.asarray(local)).astype(jnp.float32) + 0.5) / radii
    profile = (1.0 - radius * radius).reshape(tiles // 3, 3, 128)

    own_radius = ((rad * radial_rows + jnp.arange(radial_rows)).astype(jnp.float32) + 0.5) / radii
    own_profile = jnp.broadcast_to((1.0 - own_radius * own_radius)[:, None], (radial_rows, 128))

    synthesis_natural, synthesis, analysis = (
        jnp.asarray(table) for table in (synthesis_natural, synthesis, analysis)
    )
    mode_rows = jnp.asarray(np.repeat(mode_of_row[:, None], 128, axis=1))
    wire = jax.ShapeDtypeStruct((members, tiles, width, 128), jnp.float32)
    wire_spec = pl.BlockSpec((members, 3, width, 128), lambda g: (0, g, 0, 0))
    held = pltpu.VMEM((radii * width, 128), jnp.float32)
    count = (width // 8) * components * (axial_rows // 2)
    end_tiles = (count // 4) * 3 + count % 4
    everyone = seg_places * rad_places * ax_places
    spread_wire = jax.ShapeDtypeStruct((everyone, end_tiles, 8, 128), jnp.float32)

    def exchanged(value):
        return lax.all_to_all(
            value, MESH_AXES, 0, 0, axis_index_groups=half_groups, tiled=True
        )

    step = radial_rows // 3
    own_spec = pl.BlockSpec(
        (groups, components, axial_rows, step, columns), lambda g: (0, 0, 0, g, 0)
    )
    with jax.named_scope("own_physical"):
        physical = pl.pallas_call(
            own_physical,
            grid=(3,),
            in_specs=[own_spec] + whole_blocks(1),
            out_specs=own_spec,
            out_shape=jax.ShapeDtypeStruct(start_states.shape, jnp.float32),
            compiler_params=params,
        )(start_states, synthesis_natural)
    before, after, dense_inverse, physical, profile, own_profile = lax.optimization_barrier(
        (before, after, dense_inverse, physical, profile, own_profile)
    )
    other_inverse = lax.ppermute(dense_inverse, "ax", mirror)
    with jax.named_scope("phase_a_first"):
        spectral = pl.pallas_call(
            first_phase_a,
            grid=(4,),
            in_specs=[
                pl.BlockSpec(memory_space=pltpu.SMEM),
                *whole_blocks(7),
            ],
            out_specs=pl.BlockSpec(
                wire_spec.block_shape, lambda g: (0, jnp.maximum(g - 1, 0), 0, 0)
            ),
            out_shape=pltpu.HBM(wire.shape, wire.dtype),
            scratch_shapes=[
                pltpu.VMEM(
                    (2, columns // 128, groups * components * axial_rows * step, 128), jnp.float32
                )
            ],
            compiler_params=params,
        )(
            mode_count,
            before,
            physical,
            after,
            synthesis_natural,
            analysis,
            mode_rows,
            own_profile,
        )
    matrices = jax.ShapeDtypeStruct((2 * own_modes, radii, radii), jnp.bfloat16)
    in_hbm = [pl.BlockSpec(memory_space=pltpu.HBM)] * 2
    inverse_scratch = [pltpu.VMEM(matrices.shape, matrices.dtype)] * 2
    inverse_scratch += [pltpu.SemaphoreType.DMA((3,))]
    with jax.named_scope("ordered_inverse"):
        inverse = pl.pallas_call(
            ordered_inverse,
            in_specs=[pl.BlockSpec(memory_space=pltpu.SMEM)] + whole_blocks(2),
            out_specs=[pl.BlockSpec(matrices.shape, lambda: (0, 0, 0))] * 2,
            out_shape=[pltpu.HBM(matrices.shape, matrices.dtype)] * 2,
            compiler_params=params,
            cost_estimate=pl.CostEstimate(
                flops=FLOPS, bytes_accessed=16 * own_modes * radii * radii, transcendentals=0
            ),
        )(place, dense_inverse, other_inverse)
    spectral, first_start = lax.optimization_barrier((spectral, first_start))
    following = passed_along(first_start, "seg", -1)
    lines = exchanged(spectral)
    moves = jnp.asarray(quad_moves())
    with jax.named_scope("phase_b_first"):
        solved = pl.pallas_call(
            functools.partial(phase_b, peers),
            in_specs=in_hbm + [pl.BlockSpec(memory_space=pltpu.HBM)] + whole_blocks(1),
            out_specs=pl.BlockSpec(memory_space=pltpu.VMEM),
            out_shape=spread_wire,
            scratch_shapes=[held, held, pltpu.VMEM(moves.shape, moves.dtype)] + inverse_scratch,
            compiler_params=params,
        )(*map(in_place, (*inverse, moves)), lines)
    solved, following = lax.optimization_barrier((solved, following))
    state = lax.all_to_all(solved, MESH_AXES, 0, 0, tiled=True)
    with jax.named_scope("phase_a_later"):
        spectral = pl.pallas_call(
            later_phase_a,
            grid=(tiles // 3 + 1,),
            in_specs=[
                pl.BlockSpec(memory_space=pltpu.SMEM),
                *whole_blocks(6),
            ],
            out_specs=pl.BlockSpec(
                wire_spec.block_shape, lambda g: (0, jnp.maximum(g - 1, 0), 0, 0)
            ),
            out_shape=wire,
            scratch_shapes=[
                pltpu.VMEM((2, own_radii // 2, columns, 128), jnp.float32),
                pltpu.VMEM((2, columns, 3 * 128), jnp.float32),
            ],
            compiler_params=params,
        )(mode_count, state, synthesis, analysis, mode_rows, profile, jnp.asarray(lane_moves()))
    lines = exchanged(spectral)
    with jax.named_scope("phase_b_last"):
        ending = pl.pallas_call(
            functools.partial(last_phase_b, peers),
            in_specs=[pl.BlockSpec(memory_space=pltpu.SMEM)] * 2
            + whole_blocks(1)
            + in_hbm
            + whole_blocks(1),
            out_specs=pl.BlockSpec(memory_space=pltpu.VMEM),
            out_shape=spread_wire,
            scratch_shapes=[held, pltpu.VMEM((2, 96 * width, 128), jnp.float32)]
            + inverse_scratch,
            compiler_params=params,
        )(place, offsets, following, *map(in_place, inverse), lines)
    ending = lax.all_to_all(ending, MESH_AXES, 0, 0, tiled=True)
    with jax.named_scope("residual_end"):
        return pl.pallas_call(
            functools.partial(residual_end, peers),
            grid=(groups,),
            in_specs=[
                *whole_blocks(1),
                pl.BlockSpec((1,) + start_states.shape[1:], lambda b: (groups - 1, 0, 0, 0, 0)),
                *whole_blocks(1),
            ],
            out_specs=pl.BlockSpec((1,) + start_states.shape[1:], lambda b: (b, 0, 0, 0, 0)),
            out_shape=jax.ShapeDtypeStruct(start_states.shape, jnp.float32),
            scratch_shapes=[
                pltpu.VMEM((components * (axial_rows // 2), columns + 8, 128), jnp.float32)
            ],
            compiler_params=params,
        )(ending, start_states, following)


def solution(mesh):
    peers = tuple(mesh.shape[name] for name in MESH_AXES)

    def body(start_states, radial_inverse, offsets, mode_count):
        if fits(start_states.shape, peers):
            return half_body(peers, start_states, radial_inverse, offsets, mode_count)
        return general_body(start_states, radial_inverse, offsets, mode_count)

    placed = (P("seg", None, "ax", "rad", None), P("ax", None, None), P("seg"), P())
    return jax.shard_map(
        body,
        mesh=mesh,
        in_specs=placed,
        out_specs=P("seg", None, "ax", "rad", None),
        check_vma=False,
    )
```
